32 devices in a mesh: vir: 8 (over z, x), ph: 2 (over y), vec: 2 (over core).
Axes of the slice: x: 2, y: 2, z: 4, core: 2. Of those that a mesh axis runs over, the one named last changes fastest.
Arguments:
- vv_factor: bfloat16 [1024, 1024, 1024], P(('ph', 'vec'), 'vir'), may hold values from -0.1875 to 0.1875
- ladder_amp: bfloat16 [1024, 1024, 256], P(None, 'vir'), may hold values from -0.1875 to 0.1875
- cycle_amp: bfloat16 [1024, 32, 128], P(('vir', 'ph'), None, 'vec'), may hold values from -0.015625 to 0.015625
- ov_slots: bfloat16 [2048, 1024, 128], P(('vir', 'ph'), None, 'vec'), may hold values from -6 to 6
- owner_of: int32 [1024], P(('vir', 'ph')), may hold values from 0 to 1, as said below
- slot_of: int32 [1024], P(('vir', 'ph')), may hold values from 0 to 127, as said below
- ov_pairs: bfloat16 [1024, 8, 1024], P(('ph', 'vec'), None, 'vir'), may hold values from -0.1875 to 0.1875
- eps_vir: float32 [1024], replicated, may hold values from 0.5 to 3
- eps_occ: float32 [128], replicated, may hold values from -3 to -0.5
Outputs:
- residual: bfloat16 [1024, 256], P('vir', ('ph', 'vec'))
- update: float32 [1024, 256], P('vir', ('ph', 'vec'))
The draws below stay inside these ranges and needn't reach their ends.
Inputs may be any that keep to these rules, and one draw needn't show every extreme that they name: `owner_of`: within each run of 128 consecutive blocks (one vir index) one owner holds exactly 128 blocks and no owner more. `slot_of`: distinct among the blocks of one run with the same owner.
All inputs are finite; a program needn't handle non-finite values.
Results may differ from the reference program's by a relative error of at most 0.0055.
Values may be sent and summed in bfloat16 or wider, within the bound.
No kernel may reach another device: no remote copies, remote signals or barrier semaphores. Data moves between devices by JAX's collectives and lax.ppermute only.
A program may use at most 320 MiB of HBM per device.

```python
import jax
import jax.numpy as jnp
from jax import lax

V = 1024
NCHOL = 1024
NOCC = 128
BW = 128
I_OCC = 32
J_OCC = 8
NPAIR = 256
NBLK = 1024
NBD = 64
CAPB = 128
N_VIR = 8
N_PH = 2


def cycle_layout(key):
    group_size = N_PH * NBD

    def layout_group(group_index):
        subkey = jax.random.fold_in(key, group_index)
        first_key, second_key, third_key, fourth_key = jax.random.split(subkey, 4)
        shuffle = jax.random.permutation(first_key, group_size)
        busiest = jax.random.randint(second_key, (), 0, N_PH)
        offset = jax.random.randint(third_key, (), 0, N_PH - 1)
        position = jnp.arange(group_size)
        spread = (position - CAPB + offset) % (N_PH - 1)
        spread = spread + (spread >= busiest).astype(spread.dtype)
        by_position = jnp.where(position < CAPB, busiest, spread)
        owners = jnp.zeros((group_size,), by_position.dtype).at[shuffle].set(by_position)
        matches = (owners[:, None] == jnp.arange(N_PH)[None, :]).astype(owners.dtype)
        ranking = jnp.cumsum(matches, 0) - matches
        ranks = jnp.sum(ranking * matches, 1)
        owner_keys = jax.random.split(fourth_key, N_PH)
        orders = jax.vmap(lambda k: jax.random.permutation(k, CAPB))(owner_keys)
        slots = orders[owners, ranks]
        return (owners, slots)
    owners, slots = jax.vmap(layout_group)(jnp.arange(N_VIR))
    return (owners.reshape(-1).astype(jnp.int32), slots.reshape(-1).astype(jnp.int32))


def draw_owner_of(key, part):
    return cycle_layout(jax.random.fold_in(key, 11))[0]


def draw_slot_of(key, part):
    return cycle_layout(jax.random.fold_in(key, 11))[1]


def block_levels(rng, extent, cuts, low, largest):
    def one(dim, blocks):
        draws = jax.random.uniform(jax.random.fold_in(jax.random.fold_in(rng, 6), dim), (blocks,), jnp.float32, low / len(cuts), largest / len(cuts))
        return jnp.repeat(jnp.exp(draws), extent[dim] // blocks).reshape((-1,) + (1,) * (len(extent) - dim - 1))

    level = one(*cuts[0])
    for cut in cuts[1:]:
        level = level * one(*cut)
    return level


def scatter_about(key, dims, scale, bound, cuts=(), kind=jnp.bfloat16):
    values = scale * jax.random.normal(key, dims, jnp.float32)
    if cuts:
        values = values * block_levels(key, dims, cuts, -0.22, 0.18)
    return jnp.clip(values, -bound, bound).astype(kind)


def setup_inputs(seed: int = 0) -> dict:
    splits = jax.random.split(jax.random.key(seed), 10)
    return {
        "vv_factor": scatter_about(splits[0], (NCHOL, V, V), V ** -0.5, 0.1875, ((0, 4), (1, 8))),
        "ladder_amp": scatter_about(splits[1], (V, V, NPAIR), NCHOL ** -0.5, 0.1875, ((1, 8),)),
        "cycle_amp": scatter_about(splits[2], (NBLK, I_OCC, BW), (NOCC * V) ** -0.5, 0.015625, ((0, 16), (2, 2))),
        "ov_slots": scatter_about(splits[3], (N_VIR * N_PH * CAPB, NCHOL, BW), 1.0, 6.0, ((0, 16), (2, 2))),
        "owner_of": draw_owner_of(jax.random.fold_in(splits[9], 71), 0),
        "slot_of": draw_slot_of(jax.random.fold_in(splits[9], 71), 0),
        "ov_pairs": scatter_about(splits[6], (NCHOL, J_OCC, V), NCHOL ** -0.5, 0.1875, ((0, 4), (2, 8))),
        "eps_vir": jnp.clip(jax.random.uniform(splits[7], (V,), jnp.float32, 0.5, 3.0), 0.5, 3.0),
        "eps_occ": jnp.clip(jax.random.uniform(splits[8], (NOCC,), jnp.float32, -3.0, -0.5), -3.0, -0.5),
    }


def reference(vv_factor, ladder_amp, cycle_amp, ov_slots, owner_of, slot_of, ov_pairs, eps_vir, eps_occ):
    factor_row = vv_factor[:, :, 0]
    amp_matrix = ladder_amp.reshape(V, V * NPAIR)
    block_count = 8
    block_size = NCHOL // block_count

    def ladder_block(carry, block_index):
        start = (block_index * block_size).astype(jnp.int32)
        rows_part = lax.dynamic_slice_in_dim(factor_row, start, block_size, 0)
        half = jnp.dot(rows_part, amp_matrix, preferred_element_type=jnp.float32).astype(jnp.bfloat16)
        half = half.reshape(block_size * V, NPAIR)
        factor_block = lax.dynamic_slice_in_dim(vv_factor, start, block_size, 0).reshape(block_size * V, V)
        term = lax.dot_general(factor_block, half, (((0,), (0,)), ((), ())), preferred_element_type=jnp.float32)
        return carry + term, None

    ladder, unused = lax.scan(ladder_block, jnp.zeros((V, NPAIR), jnp.float32), jnp.arange(block_count, dtype=jnp.int32))

    group_size = N_PH * NBD
    group_of = jnp.arange(NBLK, dtype=jnp.int32) // group_size
    slot_rows = ((group_of * N_PH + owner_of) * CAPB + slot_of).astype(jnp.int32)

    def cycle_group(carry, inputs):
        amps, row_ids = inputs
        picked = jnp.take(ov_slots, row_ids, axis=0).astype(jnp.float32)
        return carry + jnp.einsum("giw,gpw->ip", amps.astype(jnp.float32), picked), None

    coupling, unused_too = lax.scan(
        cycle_group,
        jnp.zeros((I_OCC, NCHOL), jnp.float32),
        (cycle_amp.reshape(N_VIR, group_size, I_OCC, BW), slot_rows.reshape(N_VIR, group_size)),
    )
    coupling = coupling.astype(jnp.bfloat16)
    cycle = jnp.einsum("ip,pjb->bij", coupling.astype(jnp.float32), ov_pairs.astype(jnp.float32)).reshape(V, NPAIR)
    residual = (ladder + cycle).astype(jnp.bfloat16)
    pair_index = jnp.arange(NPAIR, dtype=jnp.int32)
    first_occ = eps_occ[pair_index // J_OCC]
    second_occ = eps_occ[pair_index % J_OCC]
    denominator = (eps_vir[0] + eps_vir)[:, None] - first_occ[None, :] - second_occ[None, :]
    update = residual.astype(jnp.float32) / denominator
    return residual, update
```

```python
import functools

import jax
import jax.numpy as jnp
from jax import lax
from jax.experimental import pallas as pl
from jax.experimental.pallas import tpu as pltpu
from jax.sharding import PartitionSpec as P

LANES = 128
bf16, f32 = jnp.bfloat16, jnp.float32


def plain(
    vv_factor, ladder_amp, cycle_amp, ov_slots, owner_of, slot_of, ov_pairs, eps_vir, eps_occ
):
    chol_local, slab_width, virtuals = vv_factor.shape
    pair_count = ladder_amp.shape[2]
    row_piece = vv_factor[:, :, 0]
    factor_row = lax.all_gather(row_piece, "vir", axis=1, tiled=True)
    half = jnp.dot(
        factor_row,
        ladder_amp.reshape(virtuals, slab_width * pair_count),
        preferred_element_type=jnp.float32,
    )
    half = half.astype(jnp.bfloat16).reshape(chol_local * slab_width, pair_count)
    flat_factor = vv_factor.reshape(chol_local * slab_width, virtuals)
    block_local, occ_rows, block_part = cycle_amp.shape
    owner_total = lax.axis_size("ph")
    targets = owner_of[None, :] == jnp.arange(owner_total, dtype=jnp.int32)[:, None]
    outgoing = jnp.where(targets[:, :, None, None], cycle_amp[None], jnp.zeros((), jnp.bfloat16))
    places = jnp.where(targets, slot_of[None, :], 0)
    arrived, arrived_slots = (
        lax.all_to_all(outgoing, "ph", split_axis=0, concat_axis=0, tiled=True),
        lax.all_to_all(places, "ph", split_axis=0, concat_axis=0, tiled=True),
    )
    capacity = ov_slots.shape[0]
    picks = (
        arrived_slots.reshape(-1)[:, None] == jnp.arange(capacity, dtype=jnp.int32)[None, :]
    ).astype(jnp.bfloat16)
    arranged = jnp.einsum(
        "ns,niw->siw",
        picks,
        arrived.reshape(-1, occ_rows, block_part),
        preferred_element_type=jnp.float32,
    )
    arranged = arranged.astype(jnp.bfloat16)
    cycle_part = jnp.einsum("siw,spw->ip", arranged, ov_slots, preferred_element_type=jnp.float32)
    near_groups = lax.axis_size("ph") * lax.axis_size("vec")
    summed = lax.psum(cycle_part, ("vir", "ph", "vec"))
    vector_share = summed.shape[1] // near_groups
    own_share = lax.dynamic_slice_in_dim(
        summed, lax.axis_index(("ph", "vec")) * vector_share, vector_share, 1
    )
    coupling = own_share.astype(jnp.bfloat16)
    second_count = ov_pairs.shape[1]
    cycle_term = jnp.einsum("ip,pjb->bij", coupling, ov_pairs, preferred_element_type=jnp.float32)
    cycle_term = cycle_term.reshape(slab_width, occ_rows * second_count)
    slab_start = lax.axis_index("vir") * slab_width
    slab = (
        lax.psum_scatter(
            lax.dot_general(
                flat_factor, half, (((0,), (0,)), ((), ())), preferred_element_type=jnp.float32
            ),
            "vir",
            scatter_dimension=0,
            tiled=True,
        )
        + cycle_term
    )
    result = lax.psum_scatter(slab, ("ph", "vec"), scatter_dimension=1, tiled=True)
    residual = result.astype(jnp.bfloat16)
    share_width = result.shape[1]
    pair_index = lax.axis_index(("ph", "vec")) * share_width + jnp.arange(
        share_width, dtype=jnp.int32
    )
    occ_count = eps_occ.shape[0]
    occ_ids = jnp.arange(occ_count, dtype=jnp.int32)[None, :]
    first_occ = jnp.sum(
        jnp.where((pair_index // second_count)[:, None] == occ_ids, eps_occ[None, :], 0.0), 1
    )
    second_occ = jnp.sum(
        jnp.where((pair_index % second_count)[:, None] == occ_ids, eps_occ[None, :], 0.0), 1
    )
    slab_energy = lax.dynamic_slice_in_dim(eps_vir, slab_start, slab_width, 0)
    denominator = (eps_vir[0] + slab_energy)[:, None] - first_occ[None, :] - second_occ[None, :]
    update = residual.astype(jnp.float32) / denominator
    return (residual, update)


def shifted(x, axes, k):
    n = lax.axis_size(axes)
    return lax.ppermute(x, axes, [(i, (i + k) % n) for i in range(n)])


def round_robin(x, axes):
    return [x] + [shifted(x, axes, k) for k in range(1, lax.axis_size(axes))]


def row_kernel(x_ref, out_ref, acc):
    step, rows = pl.program_id(1), x_ref.shape[0]
    lane = lax.broadcasted_iota(jnp.int32, acc.shape, 1)

    @pl.when(step == 0)
    def _():
        acc[...] = jnp.zeros_like(acc)

    part = jnp.zeros(acc.shape, f32)
    for p in range(rows):
        column = x_ref[p].astype(f32)
        part = jnp.where(lane == p, pltpu.roll(column, p, 1) if p else column, part)
    part = pltpu.roll(part, step * rows, 1)
    acc[...] = jnp.where(lane // rows == step, part, acc[...])

    @pl.when(step == pl.num_programs(1) - 1)
    def _():
        out_ref[...] = acc[...].T.astype(bf16)


def own_row(vv_factor):
    chol, slab, _ = vv_factor.shape
    rows = 32
    steps = LANES // rows
    return pl.pallas_call(
        row_kernel,
        grid=(chol // LANES, steps),
        in_specs=[pl.BlockSpec((rows, slab, LANES), lambda g, k: (g * steps + k, 0, 0))],
        out_specs=pl.BlockSpec((LANES, slab), lambda g, k: (g, 0)),
        out_shape=jax.ShapeDtypeStruct((chol, slab), bf16),
        scratch_shapes=[pltpu.VMEM((slab, LANES), f32)],
        compiler_params=pltpu.CompilerParams(vmem_limit_bytes=16 << 20),
        cost_estimate=pl.CostEstimate(
            flops=2 * chol * slab * LANES, bytes_accessed=2 * chol * slab * LANES, transcendentals=0
        ),
    )(vv_factor)


def cycle_kernel(shares, place_ref, code_ref, *refs):
    (*amp_refs, ov_ref, out_ref, amps, acc, block_of) = refs
    step = pl.program_id(0)
    blocks, slots = code_ref.shape[0], block_of.shape[0]
    own = amp_refs[0].shape[0]

    @pl.when(step == 0)
    def _():
        for k, ref in enumerate(amp_refs):
            amps[pl.ds(k * own, own)] = ref[...]
        amps[blocks] = jnp.zeros(amps.shape[1:], bf16)
        acc[...] = jnp.zeros_like(acc)
        first = place_ref[0] * slots

        @pl.loop(0, slots)
        def _(s):
            block_of[s] = blocks

        @pl.loop(0, blocks)
        def _(n):
            slot = code_ref[n] - first

            @pl.when((slot >= 0) & (slot < slots))
            def _():
                block_of[slot] = n

    here, width, chol = ov_ref.shape
    group = max(1, 256 // width)
    total = acc[...]
    for s in range(0, here, group):
        left = jnp.concatenate([amps[block_of[step * here + s + q]] for q in range(group)], axis=1)
        right = ov_ref[pl.ds(s, group)].reshape(group * width, chol)
        total += jnp.dot(left, right, preferred_element_type=f32)
    acc[...] = total

    @pl.when(step == pl.num_programs(0) - 1)
    def _():
        share = chol // shares
        for k in range(shares):
            start = lax.rem(place_ref[1] + k, shares) * share
            out_ref[k] = acc[:, pl.ds(pl.multiple_of(start, share), share)]


def cycle_partial(cycle_amp, ov_slots, owner_of, slot_of):
    slots, chol, width = ov_slots.shape
    occ = cycle_amp.shape[1]
    shares = lax.axis_size(("ph", "vec"))
    codes = jnp.concatenate(round_robin(owner_of * slots + slot_of, "ph"))
    amps = round_robin(cycle_amp, "ph")
    place = jnp.stack([lax.axis_index("ph"), lax.axis_index(("ph", "vec"))]).astype(jnp.int32)
    here = 16
    whole = pl.BlockSpec(memory_space=pltpu.VMEM)
    scalars = pl.BlockSpec(memory_space=pltpu.SMEM)
    return pl.pallas_call(
        functools.partial(cycle_kernel, shares),
        grid=(slots // here,),
        in_specs=[scalars, scalars]
        + [whole] * len(amps)
        + [pl.BlockSpec((here, width, chol), lambda i: (i, 0, 0))],
        out_specs=pl.BlockSpec((shares, occ, chol // shares), lambda i: (0, 0, 0)),
        out_shape=jax.ShapeDtypeStruct((shares, occ, chol // shares), f32),
        scratch_shapes=[
            pltpu.VMEM((codes.shape[0] + 1, occ, width), bf16),
            pltpu.VMEM((occ, chol), f32),
            pltpu.SMEM((slots,), jnp.int32),
        ],
        compiler_params=pltpu.CompilerParams(vmem_limit_bytes=24 << 20),
        cost_estimate=pl.CostEstimate(
            flops=2 * occ * slots * width * chol,
            bytes_accessed=2 * slots * width * chol,
            transcendentals=0,
        ),
    )(place, codes, *amps, jnp.swapaxes(ov_slots, 1, 2))


def ladder_kernel(place_ref, *refs):
    (*row_refs, amp_ref, factor_ref, out_ref, rows, turned, half, left, right) = refs
    virtuals, deep, pairs = amp_ref.shape
    chol, slab = row_refs[0].shape
    count = len(row_refs)

    @pl.when(pl.program_id(0) == 0)
    def _():
        out_ref[...] = jnp.zeros_like(out_ref)
        for k, ref in enumerate(row_refs):
            rows[lax.rem(place_ref[0] - k + count, count)] = ref[...]

    tall = left.shape[0] // deep

    @pl.loop(0, virtuals // tall)
    def _(k):
        for h, ref in enumerate((left, right)):
            x = amp_ref[pl.ds(k * tall, tall), :, pl.ds(h * LANES, LANES)]
            ref[...] = x.astype(f32).reshape(tall * deep, LANES)
        for d in range(deep):
            for h, ref in enumerate((left, right)):
                turned[d, pl.ds(k * tall, tall), pl.ds(h * LANES, LANES)] = ref[
                    pl.ds(d, tall, stride=deep), :
                ].astype(bf16)

    row = jnp.concatenate([rows[k] for k in range(count)], axis=1)
    for d in range(deep):
        product = jnp.dot(row, turned[d], preferred_element_type=f32)
        for h in range(2):
            half[h, pl.ds(d, chol, stride=deep), :] = product[:, h * LANES : (h + 1) * LANES]

    step = 512

    @pl.loop(0, chol * deep // step)
    def _(k):
        flat = jnp.concatenate([half[h, pl.ds(k * step, step), :] for h in range(2)], axis=1)
        block = factor_ref[pl.ds(k * (step // deep), step // deep)]
        out_ref[...] += lax.dot_general(
            flat.astype(bf16),
            block.reshape(step, block.shape[2]),
            (((0,), (0,)), ((), ())),
            preferred_element_type=f32,
        )


def ladder_partial(row_parts, ladder_amp, vv_factor):
    virtuals, slab, pairs = ladder_amp.shape
    chol = vv_factor.shape[0]
    deep, tall = 16, 128
    place = lax.axis_index("vir").astype(jnp.int32)[None]
    return pl.pallas_call(
        ladder_kernel,
        grid=(slab // deep,),
        in_specs=[pl.BlockSpec(memory_space=pltpu.SMEM)]
        + [pl.BlockSpec(memory_space=pltpu.VMEM)] * len(row_parts)
        + [
            pl.BlockSpec((virtuals, deep, pairs), lambda i: (0, i, 0)),
            pl.BlockSpec((chol, deep, virtuals), lambda i: (0, i, 0)),
        ],
        out_specs=pl.BlockSpec((pairs, virtuals), lambda i: (0, 0)),
        out_shape=jax.ShapeDtypeStruct((pairs, virtuals), f32),
        scratch_shapes=[
            pltpu.VMEM((len(row_parts), chol, slab), bf16),
            pltpu.VMEM((deep, virtuals, pairs), bf16),
            pltpu.VMEM((2, chol * deep, LANES), f32),
            pltpu.VMEM((tall * deep, LANES), f32),
            pltpu.VMEM((tall * deep, LANES), f32),
        ],
        compiler_params=pltpu.CompilerParams(vmem_limit_bytes=60 << 20),
        cost_estimate=pl.CostEstimate(
            flops=4 * chol * virtuals * slab * pairs,
            bytes_accessed=2 * virtuals * slab * (pairs + chol),
            transcendentals=0,
        ),
    )(place, *row_parts, ladder_amp, vv_factor)


def scatter_sum(x, axes):
    n = lax.axis_size(axes)
    me = lax.axis_index(axes)
    total = lax.dynamic_index_in_dim(x, me, 0, keepdims=False)
    sent = x.astype(bf16)
    for k in range(1, n):
        piece = lax.dynamic_index_in_dim(sent, (me + k) % n, 0, keepdims=False)
        total = total + shifted(piece, axes, k).astype(f32)
    return total


def local(
    vv_factor, ladder_amp, cycle_amp, ov_slots, owner_of, slot_of, ov_pairs, eps_vir, eps_occ
):
    chol, slab, virtuals = vv_factor.shape
    pairs = ladder_amp.shape[2]
    slots, _, width = ov_slots.shape
    n_vir, n_ph, n_vec = (lax.axis_size(a) for a in ("vir", "ph", "vec"))
    fits = slab == LANES and pairs == 2 * LANES and chol % LANES == 0 and slots % 16 == 0
    if not fits or 256 % width:
        return plain(
            vv_factor, ladder_amp, cycle_amp, ov_slots, owner_of, slot_of, ov_pairs, eps_vir, eps_occ
        )
    row_parts = round_robin(own_row(vv_factor), "vir")
    pieces = cycle_partial(cycle_amp, ov_slots, owner_of, slot_of)
    occ = pieces.shape[1]
    coupling = pieces[0]
    for k in range(1, n_ph * n_vec):
        coupling = coupling + shifted(pieces[k], ("ph", "vec"), k)
    coupling = sum(round_robin(coupling, "vir")).astype(bf16)
    second_count = ov_pairs.shape[1]
    cycle_term = jnp.einsum("ip,pjb->ijb", coupling, ov_pairs, preferred_element_type=f32)
    cycle_term = cycle_term.reshape(pairs, slab)

    ladder = ladder_partial(row_parts, ladder_amp, vv_factor)
    vir = lax.axis_index("vir")
    share = pairs // (n_ph * n_vec)
    own = jnp.arange(n_vir, dtype=jnp.int32)[None, :, None] == vir
    total = ladder.reshape(pairs, n_vir, slab) + jnp.where(own, cycle_term[:, None, :], 0.0)
    total = total.reshape(n_ph, n_vec, share, virtuals)
    total = scatter_sum(jnp.swapaxes(total, 0, 1), "vec")
    total = scatter_sum(total, "ph")
    total = scatter_sum(jnp.swapaxes(total.reshape(share, n_vir, slab), 0, 1), "vir")

    residual = total.T.astype(bf16)
    place = lax.axis_index(("ph", "vec"))
    pair_index = place * share + jnp.arange(share, dtype=jnp.int32)
    occ_ids = jnp.arange(eps_occ.shape[0], dtype=jnp.int32)[None, :]
    first_occ = jnp.sum(
        jnp.where((pair_index // second_count)[:, None] == occ_ids, eps_occ[None, :], 0.0), 1
    )
    second_occ = jnp.sum(
        jnp.where((pair_index % second_count)[:, None] == occ_ids, eps_occ[None, :], 0.0), 1
    )
    slab_energy = lax.dynamic_slice_in_dim(eps_vir, vir * slab, slab, 0)
    denominator = (eps_vir[0] + slab_energy)[:, None] - first_occ[None, :] - second_occ[None, :]
    update = residual.astype(f32) / denominator
    return residual, update


def solution(mesh):
    placed = (
        P(("ph", "vec"), "vir", None),
        P(None, "vir", None),
        P(("vir", "ph"), None, "vec"),
        P(("vir", "ph"), None, "vec"),
        P(("vir", "ph")),
        P(("vir", "ph")),
        P(("ph", "vec"), None, "vir"),
        P(),
        P(),
    )
    return jax.shard_map(
        local,
        mesh=mesh,
        in_specs=placed,
        out_specs=(P("vir", ("ph", "vec")), P("vir", ("ph", "vec"))),
        check_vma=False,
    )
```

```python
import functools

import jax
import jax.numpy as jnp
from jax import lax
from jax.experimental import pallas as pl
from jax.experimental.pallas import tpu as pltpu
from jax.sharding import PartitionSpec as P

LANES = 128
bf16, f32 = jnp.bfloat16, jnp.float32


def plain(
    vv_factor, ladder_amp, cycle_amp, ov_slots, owner_of, slot_of, ov_pairs, eps_vir, eps_occ
):
    chol_local, slab_width, virtuals = vv_factor.shape
    pair_count = ladder_amp.shape[2]
    row_piece = vv_factor[:, :, 0]
    factor_row = lax.all_gather(row_piece, "vir", axis=1, tiled=True)
    half = jnp.dot(
        factor_row,
        ladder_amp.reshape(virtuals, slab_width * pair_count),
        preferred_element_type=jnp.float32,
    )
    half = half.astype(jnp.bfloat16).reshape(chol_local * slab_width, pair_count)
    flat_factor = vv_factor.reshape(chol_local * slab_width, virtuals)
    block_local, occ_rows, block_part = cycle_amp.shape
    owner_total = lax.axis_size("ph")
    targets = owner_of[None, :] == jnp.arange(owner_total, dtype=jnp.int32)[:, None]
    outgoing = jnp.where(targets[:, :, None, None], cycle_amp[None], jnp.zeros((), jnp.bfloat16))
    places = jnp.where(targets, slot_of[None, :], 0)
    arrived, arrived_slots = (
        lax.all_to_all(outgoing, "ph", split_axis=0, concat_axis=0, tiled=True),
        lax.all_to_all(places, "ph", split_axis=0, concat_axis=0, tiled=True),
    )
    capacity = ov_slots.shape[0]
    picks = (
        arrived_slots.reshape(-1)[:, None] == jnp.arange(capacity, dtype=jnp.int32)[None, :]
    ).astype(jnp.bfloat16)
    arranged = jnp.einsum(
        "ns,niw->siw",
        picks,
        arrived.reshape(-1, occ_rows, block_part),
        preferred_element_type=jnp.float32,
    )
    arranged = arranged.astype(jnp.bfloat16)
    cycle_part = jnp.einsum("siw,spw->ip", arranged, ov_slots, preferred_element_type=jnp.float32)
    near_groups = lax.axis_size("ph") * lax.axis_size("vec")
    summed = lax.psum(cycle_part, ("vir", "ph", "vec"))
    vector_share = summed.shape[1] // near_groups
    own_share = lax.dynamic_slice_in_dim(
        summed, lax.axis_index(("ph", "vec")) * vector_share, vector_share, 1
    )
    coupling = own_share.astype(jnp.bfloat16)
    second_count = ov_pairs.shape[1]
    cycle_term = jnp.einsum("ip,pjb->bij", coupling, ov_pairs, preferred_element_type=jnp.float32)
    cycle_term = cycle_term.reshape(slab_width, occ_rows * second_count)
    slab_start = lax.axis_index("vir") * slab_width
    slab = (
        lax.psum_scatter(
            lax.dot_general(
                flat_factor, half, (((0,), (0,)), ((), ())), preferred_element_type=jnp.float32
            ),
            "vir",
            scatter_dimension=0,
            tiled=True,
        )
        + cycle_term
    )
    result = lax.psum_scatter(slab, ("ph", "vec"), scatter_dimension=1, tiled=True)
    residual = result.astype(jnp.bfloat16)
    share_width = result.shape[1]
    pair_index = lax.axis_index(("ph", "vec")) * share_width + jnp.arange(
        share_width, dtype=jnp.int32
    )
    occ_count = eps_occ.shape[0]
    occ_ids = jnp.arange(occ_count, dtype=jnp.int32)[None, :]
    first_occ = jnp.sum(
        jnp.where((pair_index // second_count)[:, None] == occ_ids, eps_occ[None, :], 0.0), 1
    )
    second_occ = jnp.sum(
        jnp.where((pair_index % second_count)[:, None] == occ_ids, eps_occ[None, :], 0.0), 1
    )
    slab_energy = lax.dynamic_slice_in_dim(eps_vir, slab_start, slab_width, 0)
    denominator = (eps_vir[0] + slab_energy)[:, None] - first_occ[None, :] - second_occ[None, :]
    update = residual.astype(jnp.float32) / denominator
    return (residual, update)


def shifted(x, axes, k):
    n = lax.axis_size(axes)
    return lax.ppermute(x, axes, [(i, (i + k) % n) for i in range(n)])


def round_robin(x, axes):
    return [x] + [shifted(x, axes, k) for k in range(1, lax.axis_size(axes))]


def row_kernel(x_ref, out_ref, acc):
    step, rows = pl.program_id(1), x_ref.shape[0]
    lane = lax.broadcasted_iota(jnp.int32, acc.shape, 1)

    @pl.when(step == 0)
    def _():
        acc[...] = jnp.zeros_like(acc)

    part = jnp.zeros(acc.shape, f32)
    for p in range(rows):
        column = x_ref[p].astype(f32)
        part = jnp.where(lane == p, pltpu.roll(column, p, 1) if p else column, part)
    part = pltpu.roll(part, step * rows, 1)
    acc[...] = jnp.where(lane // rows == step, part, acc[...])

    @pl.when(step == pl.num_programs(1) - 1)
    def _():
        out_ref[...] = acc[...].T.astype(bf16)


def own_row(vv_factor):
    chol, slab, _ = vv_factor.shape
    rows = 32
    steps = LANES // rows
    return pl.pallas_call(
        row_kernel,
        grid=(chol // LANES, steps),
        in_specs=[pl.BlockSpec((rows, slab, LANES), lambda g, k: (g * steps + k, 0, 0))],
        out_specs=pl.BlockSpec((LANES, slab), lambda g, k: (g, 0)),
        out_shape=jax.ShapeDtypeStruct((chol, slab), bf16),
        scratch_shapes=[pltpu.VMEM((slab, LANES), f32)],
        compiler_params=pltpu.CompilerParams(vmem_limit_bytes=16 << 20),
        cost_estimate=pl.CostEstimate(
            flops=2 * chol * slab * LANES, bytes_accessed=2 * chol * slab * LANES, transcendentals=0
        ),
    )(vv_factor)


def cycle_kernel(shares, place_ref, code_ref, *refs):
    (*amp_refs, ov_ref, out_ref, amps, acc, block_of) = refs
    step = pl.program_id(0)
    blocks, slots = code_ref.shape[0], block_of.shape[0]
    own, width = 2 * amp_refs[0].shape[0], amps.shape[2]

    @pl.when(step == 0)
    def _():
        for k, ref in enumerate(amp_refs):
            for h in range(2):
                amps[pl.ds(k * own + h * (own // 2), own // 2)] = ref[
                    :, :, h * width : (h + 1) * width
                ]
        amps[blocks] = jnp.zeros(amps.shape[1:], bf16)
        acc[...] = jnp.zeros_like(acc)
        first = place_ref[0] * slots

        @pl.loop(0, slots)
        def _(s):
            block_of[s] = blocks

        @pl.loop(0, blocks)
        def _(n):
            slot = code_ref[n] - first

            @pl.when((slot >= 0) & (slot < slots))
            def _():
                block_of[slot] = n

    here, _, chol = ov_ref.shape
    group = max(1, 256 // width)
    total = acc[...]
    for s in range(0, here, group):
        left = jnp.concatenate([amps[block_of[step * here + s + q]] for q in range(group)], axis=1)
        right = ov_ref[pl.ds(s, group)].reshape(group * width, chol)
        total += jnp.dot(left, right, preferred_element_type=f32)
    acc[...] = total

    @pl.when(step == pl.num_programs(0) - 1)
    def _():
        share = chol // shares
        for k in range(shares):
            out_ref[k] = acc[:, k * share : (k + 1) * share]


def cycle_partial(cycle_amp, ov_slots, owner_of, slot_of):
    slots, chol, width = ov_slots.shape
    occ = cycle_amp.shape[1]
    shares = lax.axis_size(("ph", "vec"))
    codes = jnp.concatenate(round_robin(owner_of * slots + slot_of, "ph"))
    near, far = jnp.split(cycle_amp, 2, 0)
    amps = round_robin(jnp.concatenate([near, far], 2), "ph")
    place = lax.axis_index("ph").astype(jnp.int32)[None]
    here = 16
    whole = pl.BlockSpec(memory_space=pltpu.VMEM)
    scalars = pl.BlockSpec(memory_space=pltpu.SMEM)
    return pl.pallas_call(
        functools.partial(cycle_kernel, shares),
        grid=(slots // here,),
        in_specs=[scalars, scalars]
        + [whole] * len(amps)
        + [pl.BlockSpec((here, width, chol), lambda i: (i, 0, 0))],
        out_specs=pl.BlockSpec((shares, occ, chol // shares), lambda i: (0, 0, 0)),
        out_shape=jax.ShapeDtypeStruct((shares, occ, chol // shares), f32),
        scratch_shapes=[
            pltpu.VMEM((codes.shape[0] + 1, occ, width), bf16),
            pltpu.VMEM((occ, chol), f32),
            pltpu.SMEM((slots,), jnp.int32),
        ],
        compiler_params=pltpu.CompilerParams(vmem_limit_bytes=60 << 20),
        cost_estimate=pl.CostEstimate(
            flops=2 * occ * slots * width * chol,
            bytes_accessed=2 * slots * width * chol,
            transcendentals=0,
        ),
    )(place, codes, *amps, jnp.swapaxes(ov_slots, 1, 2))


def swap_matrix(deep):
    n = deep * deep
    r = lax.broadcasted_iota(jnp.int32, (n, n), 0)
    s = lax.broadcasted_iota(jnp.int32, (n, n), 1)
    return (lax.rem(r, deep) * deep + lax.div(r, deep) == s).astype(bf16)


def ladder_kernel(row_ref, amp_ref, factor_ref, out_ref, swap, turned, half):
    virtuals, deep, pairs = amp_ref.shape
    count, chol, _ = row_ref.shape
    square = deep * deep

    @pl.when(pl.program_id(0) == 0)
    def _():
        out_ref[...] = jnp.zeros_like(out_ref)
        swap[...] = swap_matrix(deep)

    group = 8

    @pl.loop(0, virtuals // (deep * group))
    def _(k):
        for q in range(group):
            start = pl.multiple_of((k * group + q) * deep, deep)
            block = amp_ref[pl.ds(start, deep)].reshape(square, pairs)
            block = jnp.dot(swap[...], block, preferred_element_type=f32).astype(bf16)
            turned[:, pl.ds(start, deep), :] = block.reshape(deep, deep, pairs)

    row = jnp.concatenate([row_ref[k] for k in range(count)], axis=1)
    for d in range(deep):
        half[d] = jnp.dot(row, turned[d], preferred_element_type=f32).astype(bf16)

    join = 4

    @pl.loop(0, chol // (deep * join))
    def _(k):
        parts = []
        for q in range(join):
            start = pl.multiple_of((k * join + q) * deep, deep)
            block = half[:, pl.ds(start, deep), :].reshape(square, pairs)
            parts.append(jnp.dot(swap[...], block, preferred_element_type=f32).astype(bf16))
        flat = jnp.concatenate(parts, axis=0)
        start = pl.multiple_of(k * join * deep, deep)
        block = factor_ref[pl.ds(start, join * deep)]
        out_ref[...] += lax.dot_general(
            flat,
            block.reshape(join * square, block.shape[2]),
            (((0,), (0,)), ((), ())),
            preferred_element_type=f32,
        )


def ladder_partial(row, ladder_amp, vv_factor):
    virtuals, slab, pairs = ladder_amp.shape
    chol = vv_factor.shape[0]
    deep = 16
    return pl.pallas_call(
        ladder_kernel,
        grid=(slab // deep,),
        in_specs=[
            pl.BlockSpec(memory_space=pltpu.VMEM),
            pl.BlockSpec((virtuals, deep, pairs), lambda i: (0, i, 0)),
            pl.BlockSpec((chol, deep, virtuals), lambda i: (0, i, 0)),
        ],
        out_specs=pl.BlockSpec((pairs, virtuals), lambda i: (0, 0)),
        out_shape=jax.ShapeDtypeStruct((pairs, virtuals), f32),
        scratch_shapes=[
            pltpu.VMEM((deep * deep, deep * deep), bf16),
            pltpu.VMEM((deep, virtuals, pairs), bf16),
            pltpu.VMEM((deep, chol, pairs), bf16),
        ],
        compiler_params=pltpu.CompilerParams(vmem_limit_bytes=60 << 20),
        cost_estimate=pl.CostEstimate(
            flops=4 * chol * virtuals * slab * pairs,
            bytes_accessed=2 * virtuals * slab * (pairs + chol),
            transcendentals=0,
        ),
    )(row, ladder_amp, vv_factor)


def gather(x, axes):
    n = lax.axis_size(axes)
    return lax.all_to_all(jnp.broadcast_to(x[None], (n,) + x.shape), axes, 0, 0)


def scatter_sum(x, axes):
    n = lax.axis_size(axes)
    me = lax.axis_index(axes)
    total = lax.dynamic_index_in_dim(x, me, 0, keepdims=False)
    sent = x.astype(bf16)
    for k in range(1, n):
        piece = lax.dynamic_index_in_dim(sent, (me + k) % n, 0, keepdims=False)
        total = total + shifted(piece, axes, k).astype(f32)
    return total


def local(
    vv_factor, ladder_amp, cycle_amp, ov_slots, owner_of, slot_of, ov_pairs, eps_vir, eps_occ
):
    chol, slab, virtuals = vv_factor.shape
    pairs = ladder_amp.shape[2]
    slots, _, width = ov_slots.shape
    n_vir, n_ph, n_vec = (lax.axis_size(a) for a in ("vir", "ph", "vec"))
    fits = slab == LANES and pairs == 2 * LANES and chol % LANES == 0 and slots % 16 == 0
    if not fits or 256 % width or cycle_amp.shape[0] % 2:
        return plain(
            vv_factor, ladder_amp, cycle_amp, ov_slots, owner_of, slot_of, ov_pairs, eps_vir, eps_occ
        )
    row = gather(own_row(vv_factor), "vir")
    pieces = cycle_partial(cycle_amp, ov_slots, owner_of, slot_of)
    everyone = jnp.broadcast_to(pieces[None], (n_vir,) + pieces.shape)
    pieces = lax.all_to_all(everyone.reshape((-1,) + pieces.shape[1:]), ("vir", "ph", "vec"), 0, 0)
    coupling = jnp.sum(pieces, 0).astype(bf16)
    second_count = ov_pairs.shape[1]
    cycle_term = jnp.einsum("ip,pjb->ijb", coupling, ov_pairs, preferred_element_type=f32)
    cycle_term = cycle_term.reshape(pairs, slab)

    ladder = ladder_partial(row, ladder_amp, vv_factor)
    vir = lax.axis_index("vir")
    share = pairs // (n_ph * n_vec)
    own = jnp.arange(n_vir, dtype=jnp.int32)[None, :, None] == vir
    total = ladder.reshape(pairs, n_vir, slab) + jnp.where(own, cycle_term[:, None, :], 0.0)
    total = total.reshape(n_ph, n_vec, share, virtuals)
    total = scatter_sum(jnp.swapaxes(total, 0, 1), "vec")
    total = scatter_sum(total, "ph")
    total = jnp.swapaxes(total.reshape(share, n_vir, slab), 0, 1).astype(bf16)
    total = jnp.sum(lax.all_to_all(total, "vir", 0, 0).astype(f32), 0)

    residual = total.T.astype(bf16)
    place = lax.axis_index(("ph", "vec"))
    pair_index = place * share + jnp.arange(share, dtype=jnp.int32)
    occ_ids = jnp.arange(eps_occ.shape[0], dtype=jnp.int32)[None, :]
    first_occ = jnp.sum(
        jnp.where((pair_index // second_count)[:, None] == occ_ids, eps_occ[None, :], 0.0), 1
    )
    second_occ = jnp.sum(
        jnp.where((pair_index % second_count)[:, None] == occ_ids, eps_occ[None, :], 0.0), 1
    )
    slab_energy = lax.dynamic_slice_in_dim(eps_vir, vir * slab, slab, 0)
    denominator = (eps_vir[0] + slab_energy)[:, None] - first_occ[None, :] - second_occ[None, :]
    update = residual.astype(f32) / denominator
    return residual, update


def solution(mesh):
    placed = (
        P(("ph", "vec"), "vir", None),
        P(None, "vir", None),
        P(("vir", "ph"), None, "vec"),
        P(("vir", "ph"), None, "vec"),
        P(("vir", "ph")),
        P(("vir", "ph")),
        P(("ph", "vec"), None, "vir"),
        P(),
        P(),
    )
    return jax.shard_map(
        local,
        mesh=mesh,
        in_specs=placed,
        out_specs=(P("vir", ("ph", "vec")), P("vir", ("ph", "vec"))),
        check_vma=False,
    )
```

```python
import functools

import jax
import jax.numpy as jnp
from jax import lax
from jax.experimental import pallas as pl
from jax.experimental.pallas import tpu as pltpu
from jax.sharding import PartitionSpec as P

LANES = 128
bf16, f32 = jnp.bfloat16, jnp.float32


def plain(
    vv_factor, ladder_amp, cycle_amp, ov_slots, owner_of, slot_of, ov_pairs, eps_vir, eps_occ
):
    chol_local, slab_width, virtuals = vv_factor.shape
    pair_count = ladder_amp.shape[2]
    row_piece = vv_factor[:, :, 0]
    factor_row = lax.all_gather(row_piece, "vir", axis=1, tiled=True)
    half = jnp.dot(
        factor_row,
        ladder_amp.reshape(virtuals, slab_width * pair_count),
        preferred_element_type=jnp.float32,
    )
    half = half.astype(jnp.bfloat16).reshape(chol_local * slab_width, pair_count)
    flat_factor = vv_factor.reshape(chol_local * slab_width, virtuals)
    block_local, occ_rows, block_part = cycle_amp.shape
    owner_total = lax.axis_size("ph")
    targets = owner_of[None, :] == jnp.arange(owner_total, dtype=jnp.int32)[:, None]
    outgoing = jnp.where(targets[:, :, None, None], cycle_amp[None], jnp.zeros((), jnp.bfloat16))
    places = jnp.where(targets, slot_of[None, :], 0)
    arrived, arrived_slots = (
        lax.all_to_all(outgoing, "ph", split_axis=0, concat_axis=0, tiled=True),
        lax.all_to_all(places, "ph", split_axis=0, concat_axis=0, tiled=True),
    )
    capacity = ov_slots.shape[0]
    picks = (
        arrived_slots.reshape(-1)[:, None] == jnp.arange(capacity, dtype=jnp.int32)[None, :]
    ).astype(jnp.bfloat16)
    arranged = jnp.einsum(
        "ns,niw->siw",
        picks,
        arrived.reshape(-1, occ_rows, block_part),
        preferred_element_type=jnp.float32,
    )
    arranged = arranged.astype(jnp.bfloat16)
    cycle_part = jnp.einsum("siw,spw->ip", arranged, ov_slots, preferred_element_type=jnp.float32)
    near_groups = lax.axis_size("ph") * lax.axis_size("vec")
    summed = lax.psum(cycle_part, ("vir", "ph", "vec"))
    vector_share = summed.shape[1] // near_groups
    own_share = lax.dynamic_slice_in_dim(
        summed, lax.axis_index(("ph", "vec")) * vector_share, vector_share, 1
    )
    coupling = own_share.astype(jnp.bfloat16)
    second_count = ov_pairs.shape[1]
    cycle_term = jnp.einsum("ip,pjb->bij", coupling, ov_pairs, preferred_element_type=jnp.float32)
    cycle_term = cycle_term.reshape(slab_width, occ_rows * second_count)
    slab_start = lax.axis_index("vir") * slab_width
    slab = (
        lax.psum_scatter(
            lax.dot_general(
                flat_factor, half, (((0,), (0,)), ((), ())), preferred_element_type=jnp.float32
            ),
            "vir",
            scatter_dimension=0,
            tiled=True,
        )
        + cycle_term
    )
    result = lax.psum_scatter(slab, ("ph", "vec"), scatter_dimension=1, tiled=True)
    residual = result.astype(jnp.bfloat16)
    share_width = result.shape[1]
    pair_index = lax.axis_index(("ph", "vec")) * share_width + jnp.arange(
        share_width, dtype=jnp.int32
    )
    occ_count = eps_occ.shape[0]
    occ_ids = jnp.arange(occ_count, dtype=jnp.int32)[None, :]
    first_occ = jnp.sum(
        jnp.where((pair_index // second_count)[:, None] == occ_ids, eps_occ[None, :], 0.0), 1
    )
    second_occ = jnp.sum(
        jnp.where((pair_index % second_count)[:, None] == occ_ids, eps_occ[None, :], 0.0), 1
    )
    slab_energy = lax.dynamic_slice_in_dim(eps_vir, slab_start, slab_width, 0)
    denominator = (eps_vir[0] + slab_energy)[:, None] - first_occ[None, :] - second_occ[None, :]
    update = residual.astype(jnp.float32) / denominator
    return (residual, update)


def shifted(x, axes, k):
    n = lax.axis_size(axes)
    return lax.ppermute(x, axes, [(i, (i + k) % n) for i in range(n)])


def round_robin(x, axes):
    return [x] + [shifted(x, axes, k) for k in range(1, lax.axis_size(axes))]


def row_kernel(x_ref, out_ref, acc):
    step, rows = pl.program_id(1), x_ref.shape[0]
    lane = lax.broadcasted_iota(jnp.int32, acc.shape, 1)

    @pl.when(step == 0)
    def _():
        acc[...] = jnp.zeros_like(acc)

    part = jnp.zeros(acc.shape, f32)
    for p in range(rows):
        column = x_ref[p].astype(f32)
        part = jnp.where(lane == p, pltpu.roll(column, p, 1) if p else column, part)
    part = pltpu.roll(part, step * rows, 1)
    acc[...] = jnp.where(lane // rows == step, part, acc[...])

    @pl.when(step == pl.num_programs(1) - 1)
    def _():
        out_ref[...] = acc[...].T.astype(bf16)


def own_row(vv_factor):
    chol, slab, _ = vv_factor.shape
    rows = 32
    steps = LANES // rows
    return pl.pallas_call(
        row_kernel,
        grid=(chol // LANES, steps),
        in_specs=[pl.BlockSpec((rows, slab, LANES), lambda g, k: (g * steps + k, 0, 0))],
        out_specs=pl.BlockSpec((LANES, slab), lambda g, k: (g, 0)),
        out_shape=jax.ShapeDtypeStruct((chol, slab), bf16),
        scratch_shapes=[pltpu.VMEM((slab, LANES), f32)],
        compiler_params=pltpu.CompilerParams(vmem_limit_bytes=16 << 20),
        cost_estimate=pl.CostEstimate(
            flops=2 * chol * slab * LANES, bytes_accessed=2 * chol * slab * LANES, transcendentals=0
        ),
    )(vv_factor)


def cycle_kernel(shares, place_ref, code_ref, *refs):
    (*amp_refs, ov_ref, out_ref, amps, acc, block_of) = refs
    step = pl.program_id(0)
    blocks, slots = code_ref.shape[0], block_of.shape[0]
    own, width = 2 * amp_refs[0].shape[0], amps.shape[2]

    @pl.when(step == 0)
    def _():
        for k, ref in enumerate(amp_refs):
            for h in range(2):
                amps[pl.ds(k * own + h * (own // 2), own // 2)] = ref[
                    :, :, h * width : (h + 1) * width
                ]
        amps[blocks] = jnp.zeros(amps.shape[1:], bf16)
        acc[...] = jnp.zeros_like(acc)
        first = place_ref[0] * slots

        @pl.loop(0, slots)
        def _(s):
            block_of[s] = blocks

        @pl.loop(0, blocks)
        def _(n):
            slot = code_ref[n] - first

            @pl.when((slot >= 0) & (slot < slots))
            def _():
                block_of[slot] = n

    here, _, chol = ov_ref.shape
    group = max(1, 256 // width)
    total = acc[...]
    for s in range(0, here, group):
        left = jnp.concatenate([amps[block_of[step * here + s + q]] for q in range(group)], axis=1)
        right = ov_ref[pl.ds(s, group)].reshape(group * width, chol)
        total += jnp.dot(left, right, preferred_element_type=f32)
    acc[...] = total

    @pl.when(step == pl.num_programs(0) - 1)
    def _():
        share = chol // shares
        for k in range(shares):
            out_ref[k] = acc[:, k * share : (k + 1) * share]


def cycle_partial(cycle_amp, ov_slots, owner_of, slot_of):
    slots, chol, width = ov_slots.shape
    occ = cycle_amp.shape[1]
    shares = lax.axis_size(("ph", "vec"))
    codes = jnp.concatenate(round_robin(owner_of * slots + slot_of, "ph"))
    near, far = jnp.split(cycle_amp, 2, 0)
    amps = round_robin(jnp.concatenate([near, far], 2), "ph")
    place = lax.axis_index("ph").astype(jnp.int32)[None]
    here = 16
    whole = pl.BlockSpec(memory_space=pltpu.VMEM)
    scalars = pl.BlockSpec(memory_space=pltpu.SMEM)
    return pl.pallas_call(
        functools.partial(cycle_kernel, shares),
        grid=(slots // here,),
        in_specs=[scalars, scalars]
        + [whole] * len(amps)
        + [pl.BlockSpec((here, width, chol), lambda i: (i, 0, 0))],
        out_specs=pl.BlockSpec((shares, occ, chol // shares), lambda i: (0, 0, 0)),
        out_shape=jax.ShapeDtypeStruct((shares, occ, chol // shares), f32),
        scratch_shapes=[
            pltpu.VMEM((codes.shape[0] + 1, occ, width), bf16),
            pltpu.VMEM((occ, chol), f32),
            pltpu.SMEM((slots,), jnp.int32),
        ],
        compiler_params=pltpu.CompilerParams(vmem_limit_bytes=60 << 20),
        cost_estimate=pl.CostEstimate(
            flops=2 * occ * slots * width * chol,
            bytes_accessed=2 * slots * width * chol,
            transcendentals=0,
        ),
    )(place, codes, *amps, jnp.swapaxes(ov_slots, 1, 2))


def ladder_kernel(row_ref, amp_ref, factor_ref, out_ref, wide, *scratch):
    turned, half, flat = scratch[:2], scratch[2:4], scratch[4:]
    virtuals, octet, pairs = amp_ref.shape
    count, chol, _ = row_ref.shape
    step, octets = pl.program_id(0), pl.num_programs(0) - 3
    lanes = [slice(h * LANES, (h + 1) * LANES) for h in range(pairs // LANES)]
    rounds = octet
    tall, deep = virtuals // rounds, chol * octet // rounds
    columns, span = 256, chol * octet * virtuals // (256 * rounds)

    def reorder(j, area, turned):
        here = pl.ds(pl.multiple_of(j * tall, tall), tall)
        for h, lane in enumerate(lanes):
            area[h] = amp_ref[here, :, lane].astype(f32).reshape(tall * octet, LANES)
        for d in range(octet):
            for h, lane in enumerate(lanes):
                turned[d, here, lane] = area[h, pl.ds(d, tall, stride=octet), :].astype(bf16)

    def halves(j, turned, half):
        row = jnp.concatenate([row_ref[k] for k in range(count)], axis=1)
        product = jnp.dot(row, turned[j], preferred_element_type=f32)
        for h, lane in enumerate(lanes):
            half[h, pl.ds(j, chol, stride=octet), :] = product[:, lane]

    def flatten(j, half, flat):
        here = pl.ds(pl.multiple_of(j * deep, deep), deep)
        for h, lane in enumerate(lanes):
            flat[lane, here] = half[h, here, :].astype(bf16).T

    def ladder(j, flat):
        parts = chol * octet // span
        n, k = lax.div(j, parts), lax.rem(j, parts)
        column = pl.ds(pl.multiple_of(n * columns, columns), columns)
        here = pl.ds(pl.multiple_of(k * span, span), span)
        these = pl.ds(pl.multiple_of(k * (span // octet), span // octet), span // octet)
        out_ref[:, column] += jnp.dot(
            flat[:, here],
            factor_ref[these, :, column].reshape(span, columns),
            preferred_element_type=f32,
        )

    def body(parity, first, last):
        together = 2

        @pl.loop(0, rounds // together)
        def _(i):
            for q in range(together):
                j = i * together + q
                if first <= 3 <= last:
                    ladder(j, flat[1 - parity])
                if first <= 1 <= last:
                    halves(j, turned[1 - parity], half[1 - parity])
                if first <= 2 <= last:
                    flatten(j, half[parity], flat[parity])
                if first <= 0 <= last:
                    reorder(j, wide.at[q], turned[parity])

    @pl.when(step == 0)
    def _():
        out_ref[...] = jnp.zeros_like(out_ref)

    for t in range(3):

        @pl.when(step == t)
        def _():
            body(t % 2, 0, t)

        @pl.when(step == octets + t)
        def _():
            body(t % 2, t + 1, 3)

    for parity in range(2):

        @pl.when((step > 2) & (step < octets) & (lax.rem(step, 2) == parity))
        def _():
            body(parity, 0, 3)


def ladder_partial(row, ladder_amp, vv_factor):
    virtuals, slab, pairs = ladder_amp.shape
    chol = vv_factor.shape[0]
    octet = 8
    octets = slab // octet
    return pl.pallas_call(
        ladder_kernel,
        grid=(octets + 3,),
        in_specs=[
            pl.BlockSpec(memory_space=pltpu.VMEM),
            pl.BlockSpec((virtuals, octet, pairs), lambda i: (0, jnp.minimum(i, octets - 1), 0)),
            pl.BlockSpec((chol, octet, virtuals), lambda i: (0, jnp.clip(i - 3, 0, octets - 1), 0)),
        ],
        out_specs=pl.BlockSpec((pairs, virtuals), lambda i: (0, 0)),
        out_shape=jax.ShapeDtypeStruct((pairs, virtuals), f32),
        scratch_shapes=[pltpu.VMEM((2, pairs // LANES, virtuals, LANES), f32)]
        + [pltpu.VMEM((octet, virtuals, pairs), bf16)] * 2
        + [pltpu.VMEM((pairs // LANES, chol * octet, LANES), f32)] * 2
        + [pltpu.VMEM((pairs, chol * octet), bf16)] * 2,
        compiler_params=pltpu.CompilerParams(vmem_limit_bytes=60 << 20),
        cost_estimate=pl.CostEstimate(
            flops=4 * chol * virtuals * slab * pairs,
            bytes_accessed=2 * virtuals * slab * (pairs + chol),
            transcendentals=0,
        ),
    )(row, ladder_amp, vv_factor)


def gather(x, axes):
    n = lax.axis_size(axes)
    return lax.all_to_all(jnp.broadcast_to(x[None], (n,) + x.shape), axes, 0, 0)


def scatter_sum(x, axes):
    n = lax.axis_size(axes)
    me = lax.axis_index(axes)
    total = lax.dynamic_index_in_dim(x, me, 0, keepdims=False)
    sent = x.astype(bf16)
    for k in range(1, n):
        piece = lax.dynamic_index_in_dim(sent, (me + k) % n, 0, keepdims=False)
        total = total + shifted(piece, axes, k).astype(f32)
    return total


def local(
    vv_factor, ladder_amp, cycle_amp, ov_slots, owner_of, slot_of, ov_pairs, eps_vir, eps_occ
):
    chol, slab, virtuals = vv_factor.shape
    pairs = ladder_amp.shape[2]
    slots, _, width = ov_slots.shape
    n_vir, n_ph, n_vec = (lax.axis_size(a) for a in ("vir", "ph", "vec"))
    fits = slab == LANES and pairs == 2 * LANES and chol % LANES == 0 and slots % 16 == 0
    if not fits or 256 % width or cycle_amp.shape[0] % 2:
        return plain(
            vv_factor, ladder_amp, cycle_amp, ov_slots, owner_of, slot_of, ov_pairs, eps_vir, eps_occ
        )
    row = gather(own_row(vv_factor), "vir")
    pieces = cycle_partial(cycle_amp, ov_slots, owner_of, slot_of)
    everyone = jnp.broadcast_to(pieces[None], (n_vir,) + pieces.shape)
    pieces = lax.all_to_all(everyone.reshape((-1,) + pieces.shape[1:]), ("vir", "ph", "vec"), 0, 0)
    coupling = jnp.sum(pieces, 0).astype(bf16)
    second_count = ov_pairs.shape[1]
    cycle_term = jnp.einsum("ip,pjb->ijb", coupling, ov_pairs, preferred_element_type=f32)
    cycle_term = cycle_term.reshape(pairs, slab)

    ladder = ladder_partial(row, ladder_amp, vv_factor)
    vir = lax.axis_index("vir")
    share = pairs // (n_ph * n_vec)
    own = jnp.arange(n_vir, dtype=jnp.int32)[None, :, None] == vir
    total = ladder.reshape(pairs, n_vir, slab) + jnp.where(own, cycle_term[:, None, :], 0.0)
    total = total.reshape(n_ph, n_vec, share, virtuals)
    total = scatter_sum(jnp.swapaxes(total, 0, 1), "vec")
    total = scatter_sum(total, "ph")
    total = jnp.swapaxes(total.reshape(share, n_vir, slab), 0, 1).astype(bf16)
    total = jnp.sum(lax.all_to_all(total, "vir", 0, 0).astype(f32), 0)

    residual = total.T.astype(bf16)
    place = lax.axis_index(("ph", "vec"))
    pair_index = place * share + jnp.arange(share, dtype=jnp.int32)
    occ_ids = jnp.arange(eps_occ.shape[0], dtype=jnp.int32)[None, :]
    first_occ = jnp.sum(
        jnp.where((pair_index // second_count)[:, None] == occ_ids, eps_occ[None, :], 0.0), 1
    )
    second_occ = jnp.sum(
        jnp.where((pair_index % second_count)[:, None] == occ_ids, eps_occ[None, :], 0.0), 1
    )
    slab_energy = lax.dynamic_slice_in_dim(eps_vir, vir * slab, slab, 0)
    denominator = (eps_vir[0] + slab_energy)[:, None] - first_occ[None, :] - second_occ[None, :]
    update = residual.astype(f32) / denominator
    return residual, update


def solution(mesh):
    placed = (
        P(("ph", "vec"), "vir", None),
        P(None, "vir", None),
        P(("vir", "ph"), None, "vec"),
        P(("vir", "ph"), None, "vec"),
        P(("vir", "ph")),
        P(("vir", "ph")),
        P(("ph", "vec"), None, "vir"),
        P(),
        P(),
    )
    return jax.shard_map(
        local,
        mesh=mesh,
        in_specs=placed,
        out_specs=(P("vir", ("ph", "vec")), P("vir", ("ph", "vec"))),
        check_vma=False,
    )
```

```python
import functools

import jax
import jax.numpy as jnp
from jax import lax
from jax.experimental import pallas as pl
from jax.experimental.pallas import tpu as pltpu
from jax.sharding import PartitionSpec as P

LANES = 128
bf16, f32 = jnp.bfloat16, jnp.float32


def plain(
    vv_factor, ladder_amp, cycle_amp, ov_slots, owner_of, slot_of, ov_pairs, eps_vir, eps_occ
):
    chol_local, slab_width, virtuals = vv_factor.shape
    pair_count = ladder_amp.shape[2]
    row_piece = vv_factor[:, :, 0]
    factor_row = lax.all_gather(row_piece, "vir", axis=1, tiled=True)
    half = jnp.dot(
        factor_row,
        ladder_amp.reshape(virtuals, slab_width * pair_count),
        preferred_element_type=jnp.float32,
    )
    half = half.astype(jnp.bfloat16).reshape(chol_local * slab_width, pair_count)
    flat_factor = vv_factor.reshape(chol_local * slab_width, virtuals)
    block_local, occ_rows, block_part = cycle_amp.shape
    owner_total = lax.axis_size("ph")
    targets = owner_of[None, :] == jnp.arange(owner_total, dtype=jnp.int32)[:, None]
    outgoing = jnp.where(targets[:, :, None, None], cycle_amp[None], jnp.zeros((), jnp.bfloat16))
    places = jnp.where(targets, slot_of[None, :], 0)
    arrived, arrived_slots = (
        lax.all_to_all(outgoing, "ph", split_axis=0, concat_axis=0, tiled=True),
        lax.all_to_all(places, "ph", split_axis=0, concat_axis=0, tiled=True),
    )
    capacity = ov_slots.shape[0]
    picks = (
        arrived_slots.reshape(-1)[:, None] == jnp.arange(capacity, dtype=jnp.int32)[None, :]
    ).astype(jnp.bfloat16)
    arranged = jnp.einsum(
        "ns,niw->siw",
        picks,
        arrived.reshape(-1, occ_rows, block_part),
        preferred_element_type=jnp.float32,
    )
    arranged = arranged.astype(jnp.bfloat16)
    cycle_part = jnp.einsum("siw,spw->ip", arranged, ov_slots, preferred_element_type=jnp.float32)
    near_groups = lax.axis_size("ph") * lax.axis_size("vec")
    summed = lax.psum(cycle_part, ("vir", "ph", "vec"))
    vector_share = summed.shape[1] // near_groups
    own_share = lax.dynamic_slice_in_dim(
        summed, lax.axis_index(("ph", "vec")) * vector_share, vector_share, 1
    )
    coupling = own_share.astype(jnp.bfloat16)
    second_count = ov_pairs.shape[1]
    cycle_term = jnp.einsum("ip,pjb->bij", coupling, ov_pairs, preferred_element_type=jnp.float32)
    cycle_term = cycle_term.reshape(slab_width, occ_rows * second_count)
    slab_start = lax.axis_index("vir") * slab_width
    slab = (
        lax.psum_scatter(
            lax.dot_general(
                flat_factor, half, (((0,), (0,)), ((), ())), preferred_element_type=jnp.float32
            ),
            "vir",
            scatter_dimension=0,
            tiled=True,
        )
        + cycle_term
    )
    result = lax.psum_scatter(slab, ("ph", "vec"), scatter_dimension=1, tiled=True)
    residual = result.astype(jnp.bfloat16)
    share_width = result.shape[1]
    pair_index = lax.axis_index(("ph", "vec")) * share_width + jnp.arange(
        share_width, dtype=jnp.int32
    )
    occ_count = eps_occ.shape[0]
    occ_ids = jnp.arange(occ_count, dtype=jnp.int32)[None, :]
    first_occ = jnp.sum(
        jnp.where((pair_index // second_count)[:, None] == occ_ids, eps_occ[None, :], 0.0), 1
    )
    second_occ = jnp.sum(
        jnp.where((pair_index % second_count)[:, None] == occ_ids, eps_occ[None, :], 0.0), 1
    )
    slab_energy = lax.dynamic_slice_in_dim(eps_vir, slab_start, slab_width, 0)
    denominator = (eps_vir[0] + slab_energy)[:, None] - first_occ[None, :] - second_occ[None, :]
    update = residual.astype(jnp.float32) / denominator
    return (residual, update)


def shifted(x, axes, k):
    n = lax.axis_size(axes)
    return lax.ppermute(x, axes, [(i, (i + k) % n) for i in range(n)])


def round_robin(x, axes):
    return [x] + [shifted(x, axes, k) for k in range(1, lax.axis_size(axes))]


def row_kernel(*refs):
    (*x_refs, out_ref, acc) = refs
    step, rows = pl.program_id(1), x_refs[0].shape[0]
    lane = lax.broadcasted_iota(jnp.int32, acc.shape, 1)

    @pl.when(step == 0)
    def _():
        acc[...] = jnp.zeros_like(acc)

    part = jnp.zeros(acc.shape, f32)
    for q, ref in enumerate(x_refs):
        for p in range(rows):
            shift = q * rows + p
            column = ref[p].astype(f32)
            part = jnp.where(lane == shift, pltpu.roll(column, shift, 1) if shift else column, part)
    rows = rows * len(x_refs)
    part = pltpu.roll(part, step * rows, 1)
    acc[...] = jnp.where(lane // rows == step, part, acc[...])

    @pl.when(step == pl.num_programs(1) - 1)
    def _():
        piece = acc[...].T.astype(bf16)
        for k in range(out_ref.shape[0]):
            out_ref[k] = piece


def own_row(vv_factor, copies):
    chol, slab, _ = vv_factor.shape
    rows, sides = 16, 4
    steps = LANES // (rows * sides)

    def side(q):
        return pl.BlockSpec((rows, slab, LANES), lambda g, k: ((g * steps + k) * sides + q, 0, 0))

    return pl.pallas_call(
        row_kernel,
        grid=(chol // LANES, steps),
        in_specs=[side(q) for q in range(sides)],
        out_specs=pl.BlockSpec((copies, LANES, slab), lambda g, k: (0, g, 0)),
        out_shape=jax.ShapeDtypeStruct((copies, chol, slab), bf16),
        scratch_shapes=[pltpu.VMEM((slab, LANES), f32)],
        compiler_params=pltpu.CompilerParams(vmem_limit_bytes=32 << 20),
        cost_estimate=pl.CostEstimate(
            flops=2 * chol * slab * LANES, bytes_accessed=2 * chol * slab * LANES, transcendentals=0
        ),
    )(*[vv_factor] * sides)


def cycle_kernel(shares, place_ref, code_ref, *refs):
    (*amp_refs, ov_ref, out_ref, amps, acc, block_of) = refs
    step = pl.program_id(0)
    blocks, slots = code_ref.shape[0], block_of.shape[0]
    own, width = 2 * amp_refs[0].shape[0], amps.shape[2]

    @pl.when(step == 0)
    def _():
        for k, ref in enumerate(amp_refs):
            for h in range(2):
                amps[pl.ds(k * own + h * (own // 2), own // 2)] = ref[
                    :, :, h * width : (h + 1) * width
                ]
        amps[blocks] = jnp.zeros(amps.shape[1:], bf16)
        acc[...] = jnp.zeros_like(acc)
        first = place_ref[0] * slots

        @pl.loop(0, slots)
        def _(s):
            block_of[s] = blocks

        @pl.loop(0, blocks)
        def _(n):
            slot = code_ref[n] - first

            @pl.when((slot >= 0) & (slot < slots))
            def _():
                block_of[slot] = n

    here, _, chol = ov_ref.shape
    left = jnp.concatenate([amps[block_of[step * here + s]] for s in range(here)], axis=1)
    right = ov_ref[...].reshape(here * width, chol)
    acc[...] += jnp.dot(left, right, preferred_element_type=f32)

    @pl.when(step == pl.num_programs(0) - 1)
    def _():
        share = chol // shares
        for k in range(out_ref.shape[0]):
            start = k % shares * share
            out_ref[k] = acc[:, start : start + share]


def cycle_operands(cycle_amp, owner_of, slot_of, slots):
    codes = jnp.concatenate(round_robin(owner_of * slots + slot_of, "ph"))
    near, far = jnp.split(cycle_amp, 2, 0)
    return round_robin(jnp.concatenate([near, far], 2), "ph"), codes


def cycle_partial(amps, codes, ov_slots):
    slots, chol, width = ov_slots.shape
    occ = amps[0].shape[1]
    shares = lax.axis_size(("ph", "vec"))
    copies = shares * lax.axis_size("vir")
    place = lax.axis_index("ph").astype(jnp.int32)[None]
    here = 32
    whole = pl.BlockSpec(memory_space=pltpu.VMEM)
    scalars = pl.BlockSpec(memory_space=pltpu.SMEM)
    return pl.pallas_call(
        functools.partial(cycle_kernel, shares),
        grid=(slots // here,),
        in_specs=[scalars, scalars]
        + [whole] * len(amps)
        + [pl.BlockSpec((here, width, chol), lambda i: (i, 0, 0))],
        out_specs=pl.BlockSpec((copies, occ, chol // shares), lambda i: (0, 0, 0)),
        out_shape=jax.ShapeDtypeStruct((copies, occ, chol // shares), f32),
        scratch_shapes=[
            pltpu.VMEM((codes.shape[0] + 1, occ, width), bf16),
            pltpu.VMEM((occ, chol), f32),
            pltpu.SMEM((slots,), jnp.int32),
        ],
        compiler_params=pltpu.CompilerParams(vmem_limit_bytes=60 << 20),
        cost_estimate=pl.CostEstimate(
            flops=2 * occ * slots * width * chol,
            bytes_accessed=2 * slots * width * chol,
            transcendentals=0,
        ),
    )(place, codes, *amps, jnp.swapaxes(ov_slots, 1, 2))


def swap_matrix(deep):
    n = deep * deep
    r = lax.broadcasted_iota(jnp.int32, (n, n), 0)
    s = lax.broadcasted_iota(jnp.int32, (n, n), 1)
    return (lax.rem(r, deep) * deep + lax.div(r, deep) == s).astype(bf16)


def ladder_kernel(row_ref, amp_ref, factor_ref, out_ref, swap, turned, half):
    virtuals, deep, pairs = amp_ref.shape
    count, chol, _ = row_ref.shape
    square = deep * deep

    @pl.when(pl.program_id(0) == 0)
    def _():
        out_ref[...] = jnp.zeros_like(out_ref)
        swap[...] = swap_matrix(deep)

    group = 8

    @pl.loop(0, virtuals // (deep * group))
    def _(k):
        for q in range(0, group, 2):
            here = [pl.ds(pl.multiple_of((k * group + q + r) * deep, deep), deep) for r in range(2)]
            block = jnp.concatenate([amp_ref[h].reshape(square, pairs) for h in here], axis=1)
            block = jnp.dot(swap[...], block, preferred_element_type=f32).astype(bf16)
            for r, h in enumerate(here):
                part = block[:, r * pairs : (r + 1) * pairs]
                turned[:, h, :] = part.reshape(deep, deep, pairs)

    row = jnp.concatenate([row_ref[k] for k in range(count)], axis=1)
    for d in range(0, deep, 2):
        block = jnp.concatenate([turned[d], turned[d + 1]], axis=1)
        block = jnp.dot(row, block, preferred_element_type=f32).astype(bf16)
        half[d], half[d + 1] = block[:, :pairs], block[:, pairs:]

    join = 4

    @pl.loop(0, chol // (deep * join))
    def _(k):
        parts = []
        for q in range(0, join, 2):
            here = [pl.ds(pl.multiple_of((k * join + q + r) * deep, deep), deep) for r in range(2)]
            block = jnp.concatenate([half[:, h, :].reshape(square, pairs) for h in here], axis=1)
            block = jnp.dot(swap[...], block, preferred_element_type=f32).astype(bf16)
            parts += [block[:, :pairs], block[:, pairs:]]
        flat = jnp.concatenate(parts, axis=0)
        start = pl.multiple_of(k * join * deep, deep)
        block = factor_ref[pl.ds(start, join * deep)]
        out_ref[...] += lax.dot_general(
            flat,
            block.reshape(join * square, block.shape[2]),
            (((0,), (0,)), ((), ())),
            preferred_element_type=f32,
        )


def ladder_partial(row, ladder_amp, vv_factor):
    virtuals, slab, pairs = ladder_amp.shape
    chol = vv_factor.shape[0]
    deep = 16
    return pl.pallas_call(
        ladder_kernel,
        grid=(slab // deep,),
        in_specs=[
            pl.BlockSpec(memory_space=pltpu.VMEM),
            pl.BlockSpec((virtuals, deep, pairs), lambda i: (0, i, 0)),
            pl.BlockSpec((chol, deep, virtuals), lambda i: (0, i, 0)),
        ],
        out_specs=pl.BlockSpec((pairs, virtuals), lambda i: (0, 0)),
        out_shape=jax.ShapeDtypeStruct((pairs, virtuals), f32),
        scratch_shapes=[
            pltpu.VMEM((deep * deep, deep * deep), bf16),
            pltpu.VMEM((deep, virtuals, pairs), bf16),
            pltpu.VMEM((deep, chol, pairs), bf16),
        ],
        compiler_params=pltpu.CompilerParams(vmem_limit_bytes=60 << 20),
        cost_estimate=pl.CostEstimate(
            flops=4 * chol * virtuals * slab * pairs,
            bytes_accessed=2 * virtuals * slab * (pairs + chol),
            transcendentals=0,
        ),
    )(row, ladder_amp, vv_factor)


def scatter_sum(x, axes):
    n = lax.axis_size(axes)
    me = lax.axis_index(axes)
    total = lax.dynamic_index_in_dim(x, me, 0, keepdims=False)
    sent = x.astype(bf16)
    for k in range(1, n):
        piece = lax.dynamic_index_in_dim(sent, (me + k) % n, 0, keepdims=False)
        total = total + shifted(piece, axes, k).astype(f32)
    return total


def local(
    vv_factor, ladder_amp, cycle_amp, ov_slots, owner_of, slot_of, ov_pairs, eps_vir, eps_occ
):
    chol, slab, virtuals = vv_factor.shape
    pairs = ladder_amp.shape[2]
    slots, _, width = ov_slots.shape
    n_vir, n_ph, n_vec = (lax.axis_size(a) for a in ("vir", "ph", "vec"))
    fits = slab == LANES and pairs == 2 * LANES and chol % LANES == 0 and slots % 32 == 0
    if not fits or 256 % width or cycle_amp.shape[0] % 2:
        return plain(
            vv_factor, ladder_amp, cycle_amp, ov_slots, owner_of, slot_of, ov_pairs, eps_vir, eps_occ
        )
    amps, codes = cycle_operands(cycle_amp, owner_of, slot_of, slots)
    row, amps, codes = lax.optimization_barrier((own_row(vv_factor, n_vir), amps, codes))
    row = lax.all_to_all(row, "vir", 0, 0)
    pieces = lax.all_to_all(cycle_partial(amps, codes, ov_slots), ("vir", "ph", "vec"), 0, 0)
    coupling = jnp.sum(pieces, 0).astype(bf16)
    second_count = ov_pairs.shape[1]
    cycle_term = jnp.einsum("ip,pjb->ijb", coupling, ov_pairs, preferred_element_type=f32)
    cycle_term = cycle_term.reshape(pairs, slab)

    ladder = ladder_partial(row, ladder_amp, vv_factor)
    vir = lax.axis_index("vir")
    share = pairs // (n_ph * n_vec)
    own = jnp.arange(n_vir, dtype=jnp.int32)[None, :, None] == vir
    total = ladder.reshape(pairs, n_vir, slab) + jnp.where(own, cycle_term[:, None, :], 0.0)
    total = total.reshape(n_ph, n_vec, share, virtuals)
    total = scatter_sum(jnp.swapaxes(total, 0, 1), "vec").astype(bf16)
    total = total.reshape(n_ph, share, n_vir, slab).transpose(2, 0, 1, 3)
    total = lax.all_to_all(total.reshape(n_vir * n_ph, share, slab), ("vir", "ph"), 0, 0)
    total = jnp.sum(total.astype(f32), 0)

    residual = total.T.astype(bf16)
    place = lax.axis_index(("ph", "vec"))
    pair_index = place * share + jnp.arange(share, dtype=jnp.int32)
    occ_ids = jnp.arange(eps_occ.shape[0], dtype=jnp.int32)[None, :]
    first_occ = jnp.sum(
        jnp.where((pair_index // second_count)[:, None] == occ_ids, eps_occ[None, :], 0.0), 1
    )
    second_occ = jnp.sum(
        jnp.where((pair_index % second_count)[:, None] == occ_ids, eps_occ[None, :], 0.0), 1
    )
    slab_energy = lax.dynamic_slice_in_dim(eps_vir, vir * slab, slab, 0)
    denominator = (eps_vir[0] + slab_energy)[:, None] - first_occ[None, :] - second_occ[None, :]
    update = residual.astype(f32) / denominator
    return residual, update


def solution(mesh):
    placed = (
        P(("ph", "vec"), "vir", None),
        P(None, "vir", None),
        P(("vir", "ph"), None, "vec"),
        P(("vir", "ph"), None, "vec"),
        P(("vir", "ph")),
        P(("vir", "ph")),
        P(("ph", "vec"), None, "vir"),
        P(),
        P(),
    )
    return jax.shard_map(
        local,
        mesh=mesh,
        in_specs=placed,
        out_specs=(P("vir", ("ph", "vec")), P("vir", ("ph", "vec"))),
        check_vma=False,
    )
```

```python
import functools

import jax
import jax.numpy as jnp
from jax import lax
from jax.experimental import pallas as pl
from jax.experimental.pallas import tpu as pltpu
from jax.sharding import PartitionSpec as P

LANES = 128
bf16, f32 = jnp.bfloat16, jnp.float32


def plain(
    vv_factor, ladder_amp, cycle_amp, ov_slots, owner_of, slot_of, ov_pairs, eps_vir, eps_occ
):
    chol_local, slab_width, virtuals = vv_factor.shape
    pair_count = ladder_amp.shape[2]
    row_piece = vv_factor[:, :, 0]
    factor_row = lax.all_gather(row_piece, "vir", axis=1, tiled=True)
    half = jnp.dot(
        factor_row,
        ladder_amp.reshape(virtuals, slab_width * pair_count),
        preferred_element_type=jnp.float32,
    )
    half = half.astype(jnp.bfloat16).reshape(chol_local * slab_width, pair_count)
    flat_factor = vv_factor.reshape(chol_local * slab_width, virtuals)
    block_local, occ_rows, block_part = cycle_amp.shape
    owner_total = lax.axis_size("ph")
    targets = owner_of[None, :] == jnp.arange(owner_total, dtype=jnp.int32)[:, None]
    outgoing = jnp.where(targets[:, :, None, None], cycle_amp[None], jnp.zeros((), jnp.bfloat16))
    places = jnp.where(targets, slot_of[None, :], 0)
    arrived, arrived_slots = (
        lax.all_to_all(outgoing, "ph", split_axis=0, concat_axis=0, tiled=True),
        lax.all_to_all(places, "ph", split_axis=0, concat_axis=0, tiled=True),
    )
    capacity = ov_slots.shape[0]
    picks = (
        arrived_slots.reshape(-1)[:, None] == jnp.arange(capacity, dtype=jnp.int32)[None, :]
    ).astype(jnp.bfloat16)
    arranged = jnp.einsum(
        "ns,niw->siw",
        picks,
        arrived.reshape(-1, occ_rows, block_part),
        preferred_element_type=jnp.float32,
    )
    arranged = arranged.astype(jnp.bfloat16)
    cycle_part = jnp.einsum("siw,spw->ip", arranged, ov_slots, preferred_element_type=jnp.float32)
    near_groups = lax.axis_size("ph") * lax.axis_size("vec")
    summed = lax.psum(cycle_part, ("vir", "ph", "vec"))
    vector_share = summed.shape[1] // near_groups
    own_share = lax.dynamic_slice_in_dim(
        summed, lax.axis_index(("ph", "vec")) * vector_share, vector_share, 1
    )
    coupling = own_share.astype(jnp.bfloat16)
    second_count = ov_pairs.shape[1]
    cycle_term = jnp.einsum("ip,pjb->bij", coupling, ov_pairs, preferred_element_type=jnp.float32)
    cycle_term = cycle_term.reshape(slab_width, occ_rows * second_count)
    slab_start = lax.axis_index("vir") * slab_width
    slab = (
        lax.psum_scatter(
            lax.dot_general(
                flat_factor, half, (((0,), (0,)), ((), ())), preferred_element_type=jnp.float32
            ),
            "vir",
            scatter_dimension=0,
            tiled=True,
        )
        + cycle_term
    )
    result = lax.psum_scatter(slab, ("ph", "vec"), scatter_dimension=1, tiled=True)
    residual = result.astype(jnp.bfloat16)
    share_width = result.shape[1]
    pair_index = lax.axis_index(("ph", "vec")) * share_width + jnp.arange(
        share_width, dtype=jnp.int32
    )
    occ_count = eps_occ.shape[0]
    occ_ids = jnp.arange(occ_count, dtype=jnp.int32)[None, :]
    first_occ = jnp.sum(
        jnp.where((pair_index // second_count)[:, None] == occ_ids, eps_occ[None, :], 0.0), 1
    )
    second_occ = jnp.sum(
        jnp.where((pair_index % second_count)[:, None] == occ_ids, eps_occ[None, :], 0.0), 1
    )
    slab_energy = lax.dynamic_slice_in_dim(eps_vir, slab_start, slab_width, 0)
    denominator = (eps_vir[0] + slab_energy)[:, None] - first_occ[None, :] - second_occ[None, :]
    update = residual.astype(jnp.float32) / denominator
    return (residual, update)


def shifted(x, axes, k):
    n = lax.axis_size(axes)
    return lax.ppermute(x, axes, [(i, (i + k) % n) for i in range(n)])


def round_robin(x, axes):
    return [x] + [shifted(x, axes, k) for k in range(1, lax.axis_size(axes))]


def row_kernel(*refs):
    (*x_refs, out_ref, acc) = refs
    step, rows = pl.program_id(1), x_refs[0].shape[0]
    lane = lax.broadcasted_iota(jnp.int32, acc.shape, 1)

    @pl.when(step == 0)
    def _():
        acc[...] = jnp.zeros_like(acc)

    part = jnp.zeros(acc.shape, f32)
    for q, ref in enumerate(x_refs):
        for p in range(rows):
            shift = q * rows + p
            column = ref[p].astype(f32)
            part = jnp.where(lane == shift, pltpu.roll(column, shift, 1) if shift else column, part)
    rows = rows * len(x_refs)
    part = pltpu.roll(part, step * rows, 1)
    acc[...] = jnp.where(lane // rows == step, part, acc[...])

    @pl.when(step == pl.num_programs(1) - 1)
    def _():
        piece = acc[...].T.astype(bf16)
        for k in range(out_ref.shape[0]):
            out_ref[k] = piece


def own_row(vv_factor, copies):
    chol, slab, _ = vv_factor.shape
    rows, sides = 16, 4
    steps = LANES // (rows * sides)

    def side(q):
        return pl.BlockSpec((rows, slab, LANES), lambda g, k: ((g * steps + k) * sides + q, 0, 0))

    return pl.pallas_call(
        row_kernel,
        grid=(chol // LANES, steps),
        in_specs=[side(q) for q in range(sides)],
        out_specs=pl.BlockSpec((copies, LANES, slab), lambda g, k: (0, g, 0)),
        out_shape=jax.ShapeDtypeStruct((copies, chol, slab), bf16),
        scratch_shapes=[pltpu.VMEM((slab, LANES), f32)],
        compiler_params=pltpu.CompilerParams(vmem_limit_bytes=32 << 20),
        cost_estimate=pl.CostEstimate(
            flops=2 * chol * slab * LANES, bytes_accessed=2 * chol * slab * LANES, transcendentals=0
        ),
    )(*[vv_factor] * sides)


def cycle_kernel(shares, groups, place_ref, code_ref, *refs):
    (*amp_refs, out_ref, amps, acc, block_of) = refs
    amp_refs, ov_refs = amp_refs[:groups], amp_refs[groups:]
    step = pl.program_id(0)
    blocks, slots = code_ref.shape[0], block_of.shape[0]
    own, width = 2 * amp_refs[0].shape[0], amps.shape[2]

    @pl.when(step == 0)
    def _():
        for k, ref in enumerate(amp_refs):
            for h in range(2):
                amps[pl.ds(k * own + h * (own // 2), own // 2)] = ref[
                    :, :, h * width : (h + 1) * width
                ]
        amps[blocks] = jnp.zeros(amps.shape[1:], bf16)
        acc[...] = jnp.zeros_like(acc)
        first = place_ref[0] * slots

        @pl.loop(0, slots)
        def _(s):
            block_of[s] = blocks

        @pl.loop(0, blocks)
        def _(n):
            slot = code_ref[n] - first

            @pl.when((slot >= 0) & (slot < slots))
            def _():
                block_of[slot] = n

    here, _, chol = ov_refs[0].shape
    for side, ref in enumerate(ov_refs):
        start = (step * len(ov_refs) + side) * here
        left = jnp.concatenate([amps[block_of[start + s]] for s in range(here)], axis=1)
        right = ref[...].reshape(here * width, chol)
        acc[...] += jnp.dot(left, right, preferred_element_type=f32)

    @pl.when(step == pl.num_programs(0) - 1)
    def _():
        share = chol // shares
        for k in range(out_ref.shape[0]):
            start = k % shares * share
            out_ref[k] = acc[:, start : start + share]


def cycle_operands(cycle_amp, owner_of, slot_of, slots):
    codes = jnp.concatenate(round_robin(owner_of * slots + slot_of, "ph"))
    near, far = jnp.split(cycle_amp, 2, 0)
    return round_robin(jnp.concatenate([near, far], 2), "ph"), codes


def cycle_partial(amps, codes, ov_slots):
    slots, chol, width = ov_slots.shape
    occ = amps[0].shape[1]
    shares = lax.axis_size(("ph", "vec"))
    copies = shares * lax.axis_size("vir")
    place = lax.axis_index("ph").astype(jnp.int32)[None]
    here, sides = 8, 4

    def side(q):
        return pl.BlockSpec((here, width, chol), lambda i: (i * sides + q, 0, 0))

    whole = pl.BlockSpec(memory_space=pltpu.VMEM)
    scalars = pl.BlockSpec(memory_space=pltpu.SMEM)
    return pl.pallas_call(
        functools.partial(cycle_kernel, shares, len(amps)),
        grid=(slots // (here * sides),),
        in_specs=[scalars, scalars]
        + [whole] * len(amps)
        + [side(q) for q in range(sides)],
        out_specs=pl.BlockSpec((copies, occ, chol // shares), lambda i: (0, 0, 0)),
        out_shape=jax.ShapeDtypeStruct((copies, occ, chol // shares), f32),
        scratch_shapes=[
            pltpu.VMEM((codes.shape[0] + 1, occ, width), bf16),
            pltpu.VMEM((occ, chol), f32),
            pltpu.SMEM((slots,), jnp.int32),
        ],
        compiler_params=pltpu.CompilerParams(vmem_limit_bytes=60 << 20),
        cost_estimate=pl.CostEstimate(
            flops=2 * occ * slots * width * chol,
            bytes_accessed=2 * slots * width * chol,
            transcendentals=0,
        ),
    )(place, codes, *amps, *[jnp.swapaxes(ov_slots, 1, 2)] * sides)


def swap_matrix(deep):
    n = deep * deep
    r = lax.broadcasted_iota(jnp.int32, (n, n), 0)
    s = lax.broadcasted_iota(jnp.int32, (n, n), 1)
    return (lax.rem(r, deep) * deep + lax.div(r, deep) == s).astype(bf16)


def ladder_kernel(row_ref, *refs):
    (*in_refs, out_ref, swap, turned, half) = refs
    sides = len(in_refs) // 2
    amp_refs, factor_refs = in_refs[:sides], in_refs[sides:]
    virtuals, deep, pairs = amp_refs[0].shape
    count, chol, _ = row_ref.shape
    square = deep * deep

    @pl.when(pl.program_id(0) == 0)
    def _():
        out_ref[...] = jnp.zeros_like(out_ref)
        swap[...] = swap_matrix(deep)

    group = 8
    for side, amp_ref in enumerate(amp_refs):

        @pl.loop(0, virtuals // (deep * group))
        def _(k):
            for q in range(0, group, 2):
                start = [pl.multiple_of((k * group + q + r) * deep, deep) for r in range(2)]
                block = [amp_ref[pl.ds(s, deep)].reshape(square, pairs) for s in start]
                block = jnp.concatenate(block, axis=1)
                block = jnp.dot(swap[...], block, preferred_element_type=f32).astype(bf16)
                for r, s in enumerate(start):
                    part = block[:, r * pairs : (r + 1) * pairs].reshape(deep, deep, pairs)
                    turned[:, pl.ds(side * virtuals + s, deep), :] = part

    row = jnp.concatenate([row_ref[k] for k in range(count)], axis=1)
    for d in range(0, deep, 2):
        block = jnp.concatenate([turned[d], turned[d + 1]], axis=1)
        block = jnp.dot(row, block, preferred_element_type=f32).astype(bf16)
        half[d], half[d + 1] = block[:, :pairs], block[:, pairs:]

    for side, factor_ref in enumerate(factor_refs):
        parts = []
        join = factor_ref.shape[0] // deep
        for q in range(0, join, 2):
            start = [(side * join + q + r) * deep for r in range(2)]
            block = [half[:, s : s + deep, :].reshape(square, pairs) for s in start]
            block = jnp.concatenate(block, axis=1)
            block = jnp.dot(swap[...], block, preferred_element_type=f32).astype(bf16)
            parts += [block[:, :pairs], block[:, pairs:]]
        out_ref[...] += lax.dot_general(
            jnp.concatenate(parts, axis=0),
            factor_ref[...].reshape(join * square, factor_ref.shape[2]),
            (((0,), (0,)), ((), ())),
            preferred_element_type=f32,
        )


def ladder_partial(row, ladder_amp, vv_factor):
    virtuals, slab, pairs = ladder_amp.shape
    chol = vv_factor.shape[0]
    deep, sides = 16, 4

    def side(shape, q):
        return pl.BlockSpec((shape[0] // sides, deep, shape[2]), lambda i: (q, i, 0))

    return pl.pallas_call(
        ladder_kernel,
        grid=(slab // deep,),
        in_specs=[pl.BlockSpec(memory_space=pltpu.VMEM)]
        + [side(ladder_amp.shape, q) for q in range(sides)]
        + [side(vv_factor.shape, q) for q in range(sides)],
        out_specs=pl.BlockSpec((pairs, virtuals), lambda i: (0, 0)),
        out_shape=jax.ShapeDtypeStruct((pairs, virtuals), f32),
        scratch_shapes=[
            pltpu.VMEM((deep * deep, deep * deep), bf16),
            pltpu.VMEM((deep, virtuals, pairs), bf16),
            pltpu.VMEM((deep, chol, pairs), bf16),
        ],
        compiler_params=pltpu.CompilerParams(vmem_limit_bytes=60 << 20),
        cost_estimate=pl.CostEstimate(
            flops=4 * chol * virtuals * slab * pairs,
            bytes_accessed=2 * virtuals * slab * (pairs + chol),
            transcendentals=0,
        ),
    )(row, *[ladder_amp] * sides, *[vv_factor] * sides)


def scatter_sum(x, axes):
    n = lax.axis_size(axes)
    me = lax.axis_index(axes)
    total = lax.dynamic_index_in_dim(x, me, 0, keepdims=False)
    sent = x.astype(bf16)
    for k in range(1, n):
        piece = lax.dynamic_index_in_dim(sent, (me + k) % n, 0, keepdims=False)
        total = total + shifted(piece, axes, k).astype(f32)
    return total


def local(
    vv_factor, ladder_amp, cycle_amp, ov_slots, owner_of, slot_of, ov_pairs, eps_vir, eps_occ
):
    chol, slab, virtuals = vv_factor.shape
    pairs = ladder_amp.shape[2]
    slots, _, width = ov_slots.shape
    n_vir, n_ph, n_vec = (lax.axis_size(a) for a in ("vir", "ph", "vec"))
    fits = slab == LANES and pairs == 2 * LANES and chol % LANES == 0 and slots % 32 == 0
    if not fits or 256 % width or cycle_amp.shape[0] % 2:
        return plain(
            vv_factor, ladder_amp, cycle_amp, ov_slots, owner_of, slot_of, ov_pairs, eps_vir, eps_occ
        )
    amps, codes = cycle_operands(cycle_amp, owner_of, slot_of, slots)
    row, amps, codes = lax.optimization_barrier((own_row(vv_factor, n_vir), amps, codes))
    row = lax.all_to_all(row, "vir", 0, 0)
    pieces = lax.all_to_all(cycle_partial(amps, codes, ov_slots), ("vir", "ph", "vec"), 0, 0)
    coupling = jnp.sum(pieces, 0).astype(bf16)
    second_count = ov_pairs.shape[1]
    cycle_term = jnp.einsum("ip,pjb->ijb", coupling, ov_pairs, preferred_element_type=f32)
    cycle_term = cycle_term.reshape(pairs, slab)

    ladder = ladder_partial(row, ladder_amp, vv_factor)
    vir = lax.axis_index("vir")
    share = pairs // (n_ph * n_vec)
    own = jnp.arange(n_vir, dtype=jnp.int32)[None, :, None] == vir
    total = ladder.reshape(pairs, n_vir, slab) + jnp.where(own, cycle_term[:, None, :], 0.0)
    total = total.reshape(n_ph, n_vec, share, virtuals)
    total = scatter_sum(jnp.swapaxes(total, 0, 1), "vec").astype(bf16)
    total = total.reshape(n_ph, share, n_vir, slab).transpose(2, 0, 1, 3)
    total = lax.all_to_all(total.reshape(n_vir * n_ph, share, slab), ("vir", "ph"), 0, 0)
    total = jnp.sum(total.astype(f32), 0)

    residual = total.T.astype(bf16)
    place = lax.axis_index(("ph", "vec"))
    pair_index = place * share + jnp.arange(share, dtype=jnp.int32)
    occ_ids = jnp.arange(eps_occ.shape[0], dtype=jnp.int32)[None, :]
    first_occ = jnp.sum(
        jnp.where((pair_index // second_count)[:, None] == occ_ids, eps_occ[None, :], 0.0), 1
    )
    second_occ = jnp.sum(
        jnp.where((pair_index % second_count)[:, None] == occ_ids, eps_occ[None, :], 0.0), 1
    )
    slab_energy = lax.dynamic_slice_in_dim(eps_vir, vir * slab, slab, 0)
    denominator = (eps_vir[0] + slab_energy)[:, None] - first_occ[None, :] - second_occ[None, :]
    update = residual.astype(f32) / denominator
    return residual, update


def solution(mesh):
    placed = (
        P(("ph", "vec"), "vir", None),
        P(None, "vir", None),
        P(("vir", "ph"), None, "vec"),
        P(("vir", "ph"), None, "vec"),
        P(("vir", "ph")),
        P(("vir", "ph")),
        P(("ph", "vec"), None, "vir"),
        P(),
        P(),
    )
    return jax.shard_map(
        local,
        mesh=mesh,
        in_specs=placed,
        out_specs=(P("vir", ("ph", "vec")), P("vir", ("ph", "vec"))),
        check_vma=False,
    )
```

```python
import functools

import jax
import jax.numpy as jnp
from jax import lax
from jax.experimental import pallas as pl
from jax.experimental.pallas import tpu as pltpu
from jax.sharding import PartitionSpec as P

LANES = 128
bf16, f32 = jnp.bfloat16, jnp.float32


def plain(
    vv_factor, ladder_amp, cycle_amp, ov_slots, owner_of, slot_of, ov_pairs, eps_vir, eps_occ
):
    chol_local, slab_width, virtuals = vv_factor.shape
    pair_count = ladder_amp.shape[2]
    row_piece = vv_factor[:, :, 0]
    factor_row = lax.all_gather(row_piece, "vir", axis=1, tiled=True)
    half = jnp.dot(
        factor_row,
        ladder_amp.reshape(virtuals, slab_width * pair_count),
        preferred_element_type=jnp.float32,
    )
    half = half.astype(jnp.bfloat16).reshape(chol_local * slab_width, pair_count)
    flat_factor = vv_factor.reshape(chol_local * slab_width, virtuals)
    block_local, occ_rows, block_part = cycle_amp.shape
    owner_total = lax.axis_size("ph")
    targets = owner_of[None, :] == jnp.arange(owner_total, dtype=jnp.int32)[:, None]
    outgoing = jnp.where(targets[:, :, None, None], cycle_amp[None], jnp.zeros((), jnp.bfloat16))
    places = jnp.where(targets, slot_of[None, :], 0)
    arrived, arrived_slots = (
        lax.all_to_all(outgoing, "ph", split_axis=0, concat_axis=0, tiled=True),
        lax.all_to_all(places, "ph", split_axis=0, concat_axis=0, tiled=True),
    )
    capacity = ov_slots.shape[0]
    picks = (
        arrived_slots.reshape(-1)[:, None] == jnp.arange(capacity, dtype=jnp.int32)[None, :]
    ).astype(jnp.bfloat16)
    arranged = jnp.einsum(
        "ns,niw->siw",
        picks,
        arrived.reshape(-1, occ_rows, block_part),
        preferred_element_type=jnp.float32,
    )
    arranged = arranged.astype(jnp.bfloat16)
    cycle_part = jnp.einsum("siw,spw->ip", arranged, ov_slots, preferred_element_type=jnp.float32)
    near_groups = lax.axis_size("ph") * lax.axis_size("vec")
    summed = lax.psum(cycle_part, ("vir", "ph", "vec"))
    vector_share = summed.shape[1] // near_groups
    own_share = lax.dynamic_slice_in_dim(
        summed, lax.axis_index(("ph", "vec")) * vector_share, vector_share, 1
    )
    coupling = own_share.astype(jnp.bfloat16)
    second_count = ov_pairs.shape[1]
    cycle_term = jnp.einsum("ip,pjb->bij", coupling, ov_pairs, preferred_element_type=jnp.float32)
    cycle_term = cycle_term.reshape(slab_width, occ_rows * second_count)
    slab_start = lax.axis_index("vir") * slab_width
    slab = (
        lax.psum_scatter(
            lax.dot_general(
                flat_factor, half, (((0,), (0,)), ((), ())), preferred_element_type=jnp.float32
            ),
            "vir",
            scatter_dimension=0,
            tiled=True,
        )
        + cycle_term
    )
    result = lax.psum_scatter(slab, ("ph", "vec"), scatter_dimension=1, tiled=True)
    residual = result.astype(jnp.bfloat16)
    share_width = result.shape[1]
    pair_index = lax.axis_index(("ph", "vec")) * share_width + jnp.arange(
        share_width, dtype=jnp.int32
    )
    occ_count = eps_occ.shape[0]
    occ_ids = jnp.arange(occ_count, dtype=jnp.int32)[None, :]
    first_occ = jnp.sum(
        jnp.where((pair_index // second_count)[:, None] == occ_ids, eps_occ[None, :], 0.0), 1
    )
    second_occ = jnp.sum(
        jnp.where((pair_index % second_count)[:, None] == occ_ids, eps_occ[None, :], 0.0), 1
    )
    slab_energy = lax.dynamic_slice_in_dim(eps_vir, slab_start, slab_width, 0)
    denominator = (eps_vir[0] + slab_energy)[:, None] - first_occ[None, :] - second_occ[None, :]
    update = residual.astype(jnp.float32) / denominator
    return (residual, update)


def shifted(x, axes, k):
    n = lax.axis_size(axes)
    return lax.ppermute(x, axes, [(i, (i + k) % n) for i in range(n)])


def round_robin(x, axes):
    return [x] + [shifted(x, axes, k) for k in range(1, lax.axis_size(axes))]


def row_kernel(*refs):
    (*x_refs, out_ref, acc) = refs
    step, rows = pl.program_id(1), x_refs[0].shape[0]
    lane = lax.broadcasted_iota(jnp.int32, acc.shape, 1)

    @pl.when(step == 0)
    def _():
        acc[...] = jnp.zeros_like(acc)

    part = jnp.zeros(acc.shape, f32)
    for q, ref in enumerate(x_refs):
        for p in range(rows):
            shift = q * rows + p
            column = ref[p].astype(f32)
            part = jnp.where(lane == shift, pltpu.roll(column, shift, 1) if shift else column, part)
    rows = rows * len(x_refs)
    part = pltpu.roll(part, step * rows, 1)
    acc[...] = jnp.where(lane // rows == step, part, acc[...])

    @pl.when(step == pl.num_programs(1) - 1)
    def _():
        piece = acc[...].T.astype(bf16)
        for k in range(out_ref.shape[0]):
            out_ref[k] = piece


def own_row(vv_factor, copies):
    chol, slab, _ = vv_factor.shape
    rows, sides = 16, 4
    steps = LANES // (rows * sides)

    def side(q):
        return pl.BlockSpec((rows, slab, LANES), lambda g, k: ((g * steps + k) * sides + q, 0, 0))

    return pl.pallas_call(
        row_kernel,
        grid=(chol // LANES, steps),
        in_specs=[side(q) for q in range(sides)],
        out_specs=pl.BlockSpec((copies, LANES, slab), lambda g, k: (0, g, 0)),
        out_shape=jax.ShapeDtypeStruct((copies, chol, slab), bf16),
        scratch_shapes=[pltpu.VMEM((slab, LANES), f32)],
        compiler_params=pltpu.CompilerParams(vmem_limit_bytes=32 << 20),
        cost_estimate=pl.CostEstimate(
            flops=2 * chol * slab * LANES, bytes_accessed=2 * chol * slab * LANES, transcendentals=0
        ),
    )(*[vv_factor] * sides)


def cycle_kernel(shares, groups, place_ref, code_ref, *refs):
    (*amp_refs, out_ref, amps, acc, block_of) = refs
    amp_refs, ov_refs = amp_refs[:groups], amp_refs[groups:]
    step = pl.program_id(0)
    blocks, slots = code_ref.shape[0], block_of.shape[0]
    own, width = 2 * amp_refs[0].shape[0], amps.shape[2]

    @pl.when(step == 0)
    def _():
        for k, ref in enumerate(amp_refs):
            for h in range(2):
                amps[pl.ds(k * own + h * (own // 2), own // 2)] = ref[
                    :, :, h * width : (h + 1) * width
                ]
        amps[blocks] = jnp.zeros(amps.shape[1:], bf16)
        acc[...] = jnp.zeros_like(acc)
        first = place_ref[0] * slots

        @pl.loop(0, slots)
        def _(s):
            block_of[s] = blocks

        @pl.loop(0, blocks)
        def _(n):
            slot = code_ref[n] - first

            @pl.when((slot >= 0) & (slot < slots))
            def _():
                block_of[slot] = n

    here, _, chol = ov_refs[0].shape
    for side, ref in enumerate(ov_refs):
        start = (step * len(ov_refs) + side) * here
        left = jnp.concatenate([amps[block_of[start + s]] for s in range(here)], axis=1)
        right = ref[...].reshape(here * width, chol)
        acc[...] += jnp.dot(left, right, preferred_element_type=f32)

    @pl.when(step == pl.num_programs(0) - 1)
    def _():
        share = chol // shares
        for k in range(out_ref.shape[0]):
            start = k % shares * share
            out_ref[k] = acc[:, start : start + share]


def cycle_operands(cycle_amp, owner_of, slot_of, slots):
    codes = jnp.concatenate(round_robin(owner_of * slots + slot_of, "ph"))
    near, far = jnp.split(cycle_amp, 2, 0)
    return round_robin(jnp.concatenate([near, far], 2), "ph"), codes


def cycle_partial(amps, codes, ov_slots):
    slots, chol, width = ov_slots.shape
    occ = amps[0].shape[1]
    shares = lax.axis_size(("ph", "vec"))
    copies = shares * lax.axis_size("vir")
    place = lax.axis_index("ph").astype(jnp.int32)[None]
    here, sides = 8, 4

    def side(q):
        return pl.BlockSpec((here, width, chol), lambda i: (i * sides + q, 0, 0))

    whole = pl.BlockSpec(memory_space=pltpu.VMEM)
    scalars = pl.BlockSpec(memory_space=pltpu.SMEM)
    return pl.pallas_call(
        functools.partial(cycle_kernel, shares, len(amps)),
        grid=(slots // (here * sides),),
        in_specs=[scalars, scalars]
        + [whole] * len(amps)
        + [side(q) for q in range(sides)],
        out_specs=pl.BlockSpec((copies, occ, chol // shares), lambda i: (0, 0, 0)),
        out_shape=jax.ShapeDtypeStruct((copies, occ, chol // shares), f32),
        scratch_shapes=[
            pltpu.VMEM((codes.shape[0] + 1, occ, width), bf16),
            pltpu.VMEM((occ, chol), f32),
            pltpu.SMEM((slots,), jnp.int32),
        ],
        compiler_params=pltpu.CompilerParams(vmem_limit_bytes=60 << 20),
        cost_estimate=pl.CostEstimate(
            flops=2 * occ * slots * width * chol,
            bytes_accessed=2 * slots * width * chol,
            transcendentals=0,
        ),
    )(place, codes, *amps, *[jnp.swapaxes(ov_slots, 1, 2)] * sides)


def swap_matrix(deep):
    n = deep * deep
    r = lax.broadcasted_iota(jnp.int32, (n, n), 0)
    s = lax.broadcasted_iota(jnp.int32, (n, n), 1)
    return (lax.rem(r, deep) * deep + lax.div(r, deep) == s).astype(bf16)


def ladder_kernel(sides, row_ref, amp_hbm, factor_hbm, out_ref, *scratch):
    (amp_buf, factor_buf, amp_sem, factor_sem, swap, turned, half, *areas) = scratch
    _, virtuals, deep, pairs = amp_buf.shape
    count, chol, _ = row_ref.shape
    square = deep * deep
    step, steps = pl.program_id(0), pl.num_programs(0)
    slot = lax.rem(step, 2)

    def arriving(hbm, buf, sem, step, side):
        size = buf.shape[1] // sides
        rows, slot = pl.ds(side * size, size), lax.rem(step, 2)
        block = pl.ds(pl.multiple_of(step * deep, deep), deep)
        return pltpu.make_async_copy(
            hbm.at[rows, block], buf.at[slot, rows], sem.at[slot, side]
        )

    def start(step):
        for q in range(sides):
            arriving(amp_hbm, amp_buf, amp_sem, step, q).start()
        for q in range(sides):
            arriving(factor_hbm, factor_buf, factor_sem, step, q).start()

    @pl.when(step == 0)
    def _():
        start(step)
        out_ref[...] = jnp.zeros_like(out_ref)
        swap[...] = swap_matrix(deep)

    @pl.when(step + 1 < steps)
    def _():
        start(step + 1)

    def by_matmul(first):
        rows = [slice(first + r * deep, first + (r + 1) * deep) for r in range(2)]
        block = [amp_buf[slot, r].reshape(square, pairs) for r in rows]
        block = jnp.dot(
            swap[...], jnp.concatenate(block, axis=1), preferred_element_type=f32
        ).astype(bf16)
        for i, r in enumerate(rows):
            turned[:, r, :] = block[:, i * pairs : (i + 1) * pairs].reshape(deep, deep, pairs)

    def by_stride(first, tall, areas):
        for h, area in enumerate(areas):
            lane = slice(h * LANES, (h + 1) * LANES)
            block = amp_buf[slot, first : first + tall, :, lane].astype(f32)
            for o in range(deep // 8):
                area[o] = block[:, o * 8 : (o + 1) * 8].reshape(tall * 8, LANES)
            for d in range(deep):
                turned[d, first : first + tall, lane] = area[
                    d // 8, pl.ds(d % 8, tall, stride=8), :
                ].astype(bf16)

    tall = 2 * deep
    for q in range(sides):
        arriving(amp_hbm, amp_buf, amp_sem, step, q).wait()
        size = virtuals // sides
        for k in range(0, size, 2 * tall):
            first = q * size + k
            by_matmul(first)
            pick = k // (2 * tall) % 2 * 2
            by_stride(first + tall, tall, areas[pick : pick + 2])

    row = jnp.concatenate([row_ref[k] for k in range(count)], axis=1)
    for d in range(0, deep, 2):
        block = jnp.concatenate([turned[d], turned[d + 1]], axis=1)
        block = jnp.dot(row, block, preferred_element_type=f32).astype(bf16)
        half[d], half[d + 1] = block[:, :pairs], block[:, pairs:]

    for q in range(sides):
        arriving(factor_hbm, factor_buf, factor_sem, step, q).wait()
        size = chol // sides
        block = [
            half[:, k : k + deep, :].reshape(square, pairs).T
            for k in range(q * size, (q + 1) * size, deep)
        ]
        block = jnp.dot(
            jnp.concatenate(block, axis=0), swap[...], preferred_element_type=f32
        ).astype(bf16)
        block = [block[k * pairs : (k + 1) * pairs] for k in range(size // deep)]
        factor = factor_buf[slot, q * size : (q + 1) * size]
        out_ref[...] += jnp.dot(
            jnp.concatenate(block, axis=1),
            factor.reshape(size * deep, factor.shape[2]),
            preferred_element_type=f32,
        )


def ladder_partial(row, ladder_amp, vv_factor):
    virtuals, slab, pairs = ladder_amp.shape
    chol = vv_factor.shape[0]
    deep, sides = 16, 4
    whole = pl.BlockSpec(memory_space=pl.ANY)
    return pl.pallas_call(
        functools.partial(ladder_kernel, sides),
        grid=(slab // deep,),
        in_specs=[pl.BlockSpec(memory_space=pltpu.VMEM), whole, whole],
        out_specs=pl.BlockSpec((pairs, virtuals), lambda i: (0, 0)),
        out_shape=jax.ShapeDtypeStruct((pairs, virtuals), f32),
        scratch_shapes=[
            pltpu.VMEM((2, virtuals, deep, pairs), bf16),
            pltpu.VMEM((2, chol, deep, virtuals), bf16),
            pltpu.SemaphoreType.DMA((2, sides)),
            pltpu.SemaphoreType.DMA((2, sides)),
            pltpu.VMEM((deep * deep, deep * deep), bf16),
            pltpu.VMEM((deep, virtuals, pairs), bf16),
            pltpu.VMEM((deep, chol, pairs), bf16),
        ]
        + [pltpu.VMEM((deep // 8, 2 * deep * 8, LANES), f32)] * 4,
        compiler_params=pltpu.CompilerParams(vmem_limit_bytes=60 << 20),
        cost_estimate=pl.CostEstimate(
            flops=4 * chol * virtuals * slab * pairs,
            bytes_accessed=2 * virtuals * slab * (pairs + chol),
            transcendentals=0,
        ),
    )(row, ladder_amp, vv_factor)


def scatter_sum(x, axes):
    n = lax.axis_size(axes)
    me = lax.axis_index(axes)
    total = lax.dynamic_index_in_dim(x, me, 0, keepdims=False)
    sent = x.astype(bf16)
    for k in range(1, n):
        piece = lax.dynamic_index_in_dim(sent, (me + k) % n, 0, keepdims=False)
        total = total + shifted(piece, axes, k).astype(f32)
    return total


def local(
    vv_factor, ladder_amp, cycle_amp, ov_slots, owner_of, slot_of, ov_pairs, eps_vir, eps_occ
):
    chol, slab, virtuals = vv_factor.shape
    pairs = ladder_amp.shape[2]
    slots, _, width = ov_slots.shape
    n_vir, n_ph, n_vec = (lax.axis_size(a) for a in ("vir", "ph", "vec"))
    fits = slab == LANES and pairs == 2 * LANES and chol % LANES == 0 and slots % 32 == 0
    if not fits or 256 % width or cycle_amp.shape[0] % 2:
        return plain(
            vv_factor, ladder_amp, cycle_amp, ov_slots, owner_of, slot_of, ov_pairs, eps_vir, eps_occ
        )
    amps, codes = cycle_operands(cycle_amp, owner_of, slot_of, slots)
    row, amps, codes = lax.optimization_barrier((own_row(vv_factor, n_vir), amps, codes))
    row = lax.all_to_all(row, "vir", 0, 0)
    pieces = lax.all_to_all(cycle_partial(amps, codes, ov_slots), ("vir", "ph", "vec"), 0, 0)
    coupling = jnp.sum(pieces, 0).astype(bf16)
    second_count = ov_pairs.shape[1]
    cycle_term = jnp.einsum("ip,pjb->ijb", coupling, ov_pairs, preferred_element_type=f32)
    cycle_term = cycle_term.reshape(pairs, slab)

    ladder = ladder_partial(row, ladder_amp, vv_factor)
    vir = lax.axis_index("vir")
    share = pairs // (n_ph * n_vec)
    own = jnp.arange(n_vir, dtype=jnp.int32)[None, :, None] == vir
    total = ladder.reshape(pairs, n_vir, slab) + jnp.where(own, cycle_term[:, None, :], 0.0)
    total = total.reshape(n_ph, n_vec, share, virtuals)
    total = scatter_sum(jnp.swapaxes(total, 0, 1), "vec").astype(bf16)
    total = total.reshape(n_ph, share, n_vir, slab).transpose(2, 0, 1, 3)
    total = lax.all_to_all(total.reshape(n_vir * n_ph, share, slab), ("vir", "ph"), 0, 0)
    total = jnp.sum(total.astype(f32), 0)

    residual = total.T.astype(bf16)
    place = lax.axis_index(("ph", "vec"))
    pair_index = place * share + jnp.arange(share, dtype=jnp.int32)
    occ_ids = jnp.arange(eps_occ.shape[0], dtype=jnp.int32)[None, :]
    first_occ = jnp.sum(
        jnp.where((pair_index // second_count)[:, None] == occ_ids, eps_occ[None, :], 0.0), 1
    )
    second_occ = jnp.sum(
        jnp.where((pair_index % second_count)[:, None] == occ_ids, eps_occ[None, :], 0.0), 1
    )
    slab_energy = lax.dynamic_slice_in_dim(eps_vir, vir * slab, slab, 0)
    denominator = (eps_vir[0] + slab_energy)[:, None] - first_occ[None, :] - second_occ[None, :]
    update = residual.astype(f32) / denominator
    return residual, update


def solution(mesh):
    placed = (
        P(("ph", "vec"), "vir", None),
        P(None, "vir", None),
        P(("vir", "ph"), None, "vec"),
        P(("vir", "ph"), None, "vec"),
        P(("vir", "ph")),
        P(("vir", "ph")),
        P(("ph", "vec"), None, "vir"),
        P(),
        P(),
    )
    return jax.shard_map(
        local,
        mesh=mesh,
        in_specs=placed,
        out_specs=(P("vir", ("ph", "vec")), P("vir", ("ph", "vec"))),
        check_vma=False,
    )
```

```python
import functools

import jax
import jax.numpy as jnp
from jax import lax
from jax.experimental import pallas as pl
from jax.experimental.pallas import tpu as pltpu
from jax.sharding import PartitionSpec as P

LANES = 128
bf16, f32 = jnp.bfloat16, jnp.float32


def plain(
    vv_factor, ladder_amp, cycle_amp, ov_slots, owner_of, slot_of, ov_pairs, eps_vir, eps_occ
):
    chol_local, slab_width, virtuals = vv_factor.shape
    pair_count = ladder_amp.shape[2]
    row_piece = vv_factor[:, :, 0]
    factor_row = lax.all_gather(row_piece, "vir", axis=1, tiled=True)
    half = jnp.dot(
        factor_row,
        ladder_amp.reshape(virtuals, slab_width * pair_count),
        preferred_element_type=jnp.float32,
    )
    half = half.astype(jnp.bfloat16).reshape(chol_local * slab_width, pair_count)
    flat_factor = vv_factor.reshape(chol_local * slab_width, virtuals)
    block_local, occ_rows, block_part = cycle_amp.shape
    owner_total = lax.axis_size("ph")
    targets = owner_of[None, :] == jnp.arange(owner_total, dtype=jnp.int32)[:, None]
    outgoing = jnp.where(targets[:, :, None, None], cycle_amp[None], jnp.zeros((), jnp.bfloat16))
    places = jnp.where(targets, slot_of[None, :], 0)
    arrived, arrived_slots = (
        lax.all_to_all(outgoing, "ph", split_axis=0, concat_axis=0, tiled=True),
        lax.all_to_all(places, "ph", split_axis=0, concat_axis=0, tiled=True),
    )
    capacity = ov_slots.shape[0]
    picks = (
        arrived_slots.reshape(-1)[:, None] == jnp.arange(capacity, dtype=jnp.int32)[None, :]
    ).astype(jnp.bfloat16)
    arranged = jnp.einsum(
        "ns,niw->siw",
        picks,
        arrived.reshape(-1, occ_rows, block_part),
        preferred_element_type=jnp.float32,
    )
    arranged = arranged.astype(jnp.bfloat16)
    cycle_part = jnp.einsum("siw,spw->ip", arranged, ov_slots, preferred_element_type=jnp.float32)
    near_groups = lax.axis_size("ph") * lax.axis_size("vec")
    summed = lax.psum(cycle_part, ("vir", "ph", "vec"))
    vector_share = summed.shape[1] // near_groups
    own_share = lax.dynamic_slice_in_dim(
        summed, lax.axis_index(("ph", "vec")) * vector_share, vector_share, 1
    )
    coupling = own_share.astype(jnp.bfloat16)
    second_count = ov_pairs.shape[1]
    cycle_term = jnp.einsum("ip,pjb->bij", coupling, ov_pairs, preferred_element_type=jnp.float32)
    cycle_term = cycle_term.reshape(slab_width, occ_rows * second_count)
    slab_start = lax.axis_index("vir") * slab_width
    slab = (
        lax.psum_scatter(
            lax.dot_general(
                flat_factor, half, (((0,), (0,)), ((), ())), preferred_element_type=jnp.float32
            ),
            "vir",
            scatter_dimension=0,
            tiled=True,
        )
        + cycle_term
    )
    result = lax.psum_scatter(slab, ("ph", "vec"), scatter_dimension=1, tiled=True)
    residual = result.astype(jnp.bfloat16)
    share_width = result.shape[1]
    pair_index = lax.axis_index(("ph", "vec")) * share_width + jnp.arange(
        share_width, dtype=jnp.int32
    )
    occ_count = eps_occ.shape[0]
    occ_ids = jnp.arange(occ_count, dtype=jnp.int32)[None, :]
    first_occ = jnp.sum(
        jnp.where((pair_index // second_count)[:, None] == occ_ids, eps_occ[None, :], 0.0), 1
    )
    second_occ = jnp.sum(
        jnp.where((pair_index % second_count)[:, None] == occ_ids, eps_occ[None, :], 0.0), 1
    )
    slab_energy = lax.dynamic_slice_in_dim(eps_vir, slab_start, slab_width, 0)
    denominator = (eps_vir[0] + slab_energy)[:, None] - first_occ[None, :] - second_occ[None, :]
    update = residual.astype(jnp.float32) / denominator
    return (residual, update)


def shifted(x, axes, k):
    n = lax.axis_size(axes)
    return lax.ppermute(x, axes, [(i, (i + k) % n) for i in range(n)])


def round_robin(x, axes):
    return [x] + [shifted(x, axes, k) for k in range(1, lax.axis_size(axes))]


def row_kernel(*refs):
    (*x_refs, out_ref, acc) = refs
    step, rows = pl.program_id(1), x_refs[0].shape[0]
    lane = lax.broadcasted_iota(jnp.int32, acc.shape, 1)

    @pl.when(step == 0)
    def _():
        acc[...] = jnp.zeros_like(acc)

    part = jnp.zeros(acc.shape, f32)
    for q, ref in enumerate(x_refs):
        for p in range(rows):
            shift = q * rows + p
            column = ref[p].astype(f32)
            part = jnp.where(lane == shift, pltpu.roll(column, shift, 1) if shift else column, part)
    rows = rows * len(x_refs)
    part = pltpu.roll(part, step * rows, 1)
    acc[...] = jnp.where(lane // rows == step, part, acc[...])

    @pl.when(step == pl.num_programs(1) - 1)
    def _():
        piece = acc[...].T.astype(bf16)
        for k in range(out_ref.shape[0]):
            out_ref[k] = piece


def own_row(vv_factor, copies):
    chol, slab, _ = vv_factor.shape
    rows, sides = 16, 4
    steps = LANES // (rows * sides)

    def side(q):
        return pl.BlockSpec((rows, slab, LANES), lambda g, k: ((g * steps + k) * sides + q, 0, 0))

    return pl.pallas_call(
        row_kernel,
        grid=(chol // LANES, steps),
        in_specs=[side(q) for q in range(sides)],
        out_specs=pl.BlockSpec((copies, LANES, slab), lambda g, k: (0, g, 0)),
        out_shape=jax.ShapeDtypeStruct((copies, chol, slab), bf16),
        scratch_shapes=[pltpu.VMEM((slab, LANES), f32)],
        compiler_params=pltpu.CompilerParams(vmem_limit_bytes=32 << 20),
        cost_estimate=pl.CostEstimate(
            flops=2 * chol * slab * LANES, bytes_accessed=2 * chol * slab * LANES, transcendentals=0
        ),
    )(*[vv_factor] * sides)


def cycle_kernel(shares, groups, place_ref, code_ref, *refs):
    (*amp_refs, out_ref, amps, acc, block_of) = refs
    amp_refs, ov_refs = amp_refs[:groups], amp_refs[groups:]
    step = pl.program_id(0)
    blocks, slots = code_ref.shape[0], block_of.shape[0]
    own = amp_refs[0].shape[0]

    @pl.when(step == 0)
    def _():
        for k, ref in enumerate(amp_refs):
            amps[pl.ds(k * own, own)] = ref[...]
        amps[blocks] = jnp.zeros(amps.shape[1:], bf16)
        acc[...] = jnp.zeros_like(acc)
        first = place_ref[0] * slots

        @pl.loop(0, slots)
        def _(s):
            block_of[s] = blocks

        @pl.loop(0, blocks)
        def _(n):
            slot = code_ref[n] - first

            @pl.when((slot >= 0) & (slot < slots))
            def _():
                block_of[slot] = n

    here, width, chol = ov_refs[0].shape
    for side, ref in enumerate(ov_refs):
        start = (step * len(ov_refs) + side) * here
        left = jnp.concatenate([amps[block_of[start + s]] for s in range(here)], axis=1)
        right = ref[...].reshape(here * width, chol)
        acc[...] += jnp.dot(left, right, preferred_element_type=f32)

    @pl.when(step == pl.num_programs(0) - 1)
    def _():
        share = chol // shares
        for k in range(out_ref.shape[0]):
            start = k % shares * share
            out_ref[k] = acc[:, start : start + share]


def cycle_operands(cycle_amp, owner_of, slot_of, slots):
    codes = jnp.concatenate(round_robin(owner_of * slots + slot_of, "ph"))
    return round_robin(cycle_amp, "ph"), codes


def cycle_partial(amps, codes, ov_slots):
    slots, chol, width = ov_slots.shape
    occ = amps[0].shape[1]
    shares = lax.axis_size(("ph", "vec"))
    copies = shares * lax.axis_size("vir")
    place = lax.axis_index("ph").astype(jnp.int32)[None]
    here, sides = 8, 4

    def side(q):
        return pl.BlockSpec((here, width, chol), lambda i: (i * sides + q, 0, 0))

    whole = pl.BlockSpec(memory_space=pltpu.VMEM)
    scalars = pl.BlockSpec(memory_space=pltpu.SMEM)
    return pl.pallas_call(
        functools.partial(cycle_kernel, shares, len(amps)),
        grid=(slots // (here * sides),),
        in_specs=[scalars, scalars]
        + [whole] * len(amps)
        + [side(q) for q in range(sides)],
        out_specs=pl.BlockSpec((copies, occ, chol // shares), lambda i: (0, 0, 0)),
        out_shape=jax.ShapeDtypeStruct((copies, occ, chol // shares), f32),
        scratch_shapes=[
            pltpu.VMEM((codes.shape[0] + 1, occ, width), bf16),
            pltpu.VMEM((occ, chol), f32),
            pltpu.SMEM((slots,), jnp.int32),
        ],
        compiler_params=pltpu.CompilerParams(vmem_limit_bytes=60 << 20),
        cost_estimate=pl.CostEstimate(
            flops=2 * occ * slots * width * chol,
            bytes_accessed=2 * slots * width * chol,
            transcendentals=0,
        ),
    )(place, codes, *amps, *[jnp.swapaxes(ov_slots, 1, 2)] * sides)


def swap_matrix(deep):
    n = deep * deep
    r = lax.broadcasted_iota(jnp.int32, (n, n), 0)
    s = lax.broadcasted_iota(jnp.int32, (n, n), 1)
    return (lax.rem(r, deep) * deep + lax.div(r, deep) == s).astype(bf16)


def ladder_kernel(sides, row_ref, amp_hbm, factor_hbm, out_ref, *scratch):
    (amp_buf, factor_buf, amp_sem, factor_sem, swap, turned, half) = scratch
    _, virtuals, deep, pairs = amp_buf.shape
    count, chol, _ = row_ref.shape
    square = deep * deep
    step, steps = pl.program_id(0), pl.num_programs(0)
    slot = lax.rem(step, 2)

    def arriving(hbm, buf, sem, step, side):
        size = buf.shape[1] // sides
        rows, slot = pl.ds(side * size, size), lax.rem(step, 2)
        block = pl.ds(pl.multiple_of(step * deep, deep), deep)
        return pltpu.make_async_copy(
            hbm.at[rows, block], buf.at[slot, rows], sem.at[slot, side]
        )

    def start(step):
        for q in range(sides):
            arriving(amp_hbm, amp_buf, amp_sem, step, q).start()
        for q in range(sides):
            arriving(factor_hbm, factor_buf, factor_sem, step, q).start()

    @pl.when(step == 0)
    def _():
        start(step)
        out_ref[...] = jnp.zeros_like(out_ref)
        swap[...] = swap_matrix(deep)

    @pl.when(step + 1 < steps)
    def _():
        start(step + 1)

    def by_matmul(first):
        rows = [slice(first + r * deep, first + (r + 1) * deep) for r in range(2)]
        block = [amp_buf[slot, r].reshape(square, pairs) for r in rows]
        block = jnp.dot(
            swap[...], jnp.concatenate(block, axis=1), preferred_element_type=f32
        ).astype(bf16)
        for i, r in enumerate(rows):
            turned[:, r, :] = block[:, i * pairs : (i + 1) * pairs].reshape(deep, deep, pairs)

    for q in range(sides):
        arriving(amp_hbm, amp_buf, amp_sem, step, q).wait()
        size = virtuals // sides
        for k in range(q * size, (q + 1) * size, 2 * deep):
            by_matmul(k)

    row = jnp.concatenate([row_ref[k] for k in range(count)], axis=1)
    for d in range(0, deep, 2):
        block = jnp.concatenate([turned[d], turned[d + 1]], axis=1)
        block = jnp.dot(row, block, preferred_element_type=f32).astype(bf16)
        half[d], half[d + 1] = block[:, :pairs], block[:, pairs:]

    for q in range(sides):
        arriving(factor_hbm, factor_buf, factor_sem, step, q).wait()
        size = chol // sides
        block = [
            half[:, k : k + deep, :].reshape(square, pairs).T
            for k in range(q * size, (q + 1) * size, deep)
        ]
        block = jnp.dot(
            jnp.concatenate(block, axis=0), swap[...], preferred_element_type=f32
        ).astype(bf16)
        block = [block[k * pairs : (k + 1) * pairs] for k in range(size // deep)]
        factor = factor_buf[slot, q * size : (q + 1) * size]
        out_ref[...] += jnp.dot(
            jnp.concatenate(block, axis=1),
            factor.reshape(size * deep, factor.shape[2]),
            preferred_element_type=f32,
        )


def ladder_partial(row, ladder_amp, vv_factor):
    virtuals, slab, pairs = ladder_amp.shape
    chol = vv_factor.shape[0]
    deep, sides = 16, 4
    whole = pl.BlockSpec(memory_space=pl.ANY)
    return pl.pallas_call(
        functools.partial(ladder_kernel, sides),
        grid=(slab // deep,),
        in_specs=[pl.BlockSpec(memory_space=pltpu.VMEM), whole, whole],
        out_specs=pl.BlockSpec((pairs, virtuals), lambda i: (0, 0)),
        out_shape=jax.ShapeDtypeStruct((pairs, virtuals), f32),
        scratch_shapes=[
            pltpu.VMEM((2, virtuals, deep, pairs), bf16),
            pltpu.VMEM((2, chol, deep, virtuals), bf16),
            pltpu.SemaphoreType.DMA((2, sides)),
            pltpu.SemaphoreType.DMA((2, sides)),
            pltpu.VMEM((deep * deep, deep * deep), bf16),
            pltpu.VMEM((deep, virtuals, pairs), bf16),
            pltpu.VMEM((deep, chol, pairs), bf16),
        ],
        compiler_params=pltpu.CompilerParams(vmem_limit_bytes=60 << 20),
        cost_estimate=pl.CostEstimate(
            flops=4 * chol * virtuals * slab * pairs,
            bytes_accessed=2 * virtuals * slab * (pairs + chol),
            transcendentals=0,
        ),
    )(row, ladder_amp, vv_factor)


def scatter_sum(x, axes, near=None):
    total_places = lax.axis_size(axes)
    me = lax.axis_index(axes)
    n = x.shape[0]

    def moved(place, k):
        if near is None:
            return (place + k) % n
        if near > 0:
            return place // near * near + (place % near + k) % near
        return (place + k * -near) % total_places

    def rank(place):
        return place if near is None else place % near if near > 0 else place // -near

    total = lax.dynamic_index_in_dim(x, rank(me), 0, keepdims=False)
    sent = x.astype(bf16)
    for k in range(1, n):
        piece = lax.dynamic_index_in_dim(sent, rank(moved(me, k)), 0, keepdims=False)
        pairs = [(i, moved(i, k)) for i in range(total_places)]
        total = total + lax.ppermute(piece, axes, pairs).astype(f32)
    return total


def local(
    vv_factor, ladder_amp, cycle_amp, ov_slots, owner_of, slot_of, ov_pairs, eps_vir, eps_occ
):
    chol, slab, virtuals = vv_factor.shape
    pairs = ladder_amp.shape[2]
    slots, _, width = ov_slots.shape
    n_vir, n_ph, n_vec = (lax.axis_size(a) for a in ("vir", "ph", "vec"))
    fits = slab == LANES and pairs == 2 * LANES and chol % LANES == 0 and slots % 32 == 0
    if not fits or 256 % width or n_vir * n_ph % 4:
        return plain(
            vv_factor, ladder_amp, cycle_amp, ov_slots, owner_of, slot_of, ov_pairs, eps_vir, eps_occ
        )
    amps, codes = cycle_operands(cycle_amp, owner_of, slot_of, slots)
    row, amps, codes = lax.optimization_barrier((own_row(vv_factor, n_vir), amps, codes))
    row = lax.all_to_all(row, "vir", 0, 0)
    pieces = lax.all_to_all(cycle_partial(amps, codes, ov_slots), ("vir", "ph", "vec"), 0, 0)
    coupling = jnp.sum(pieces, 0).astype(bf16)
    second_count = ov_pairs.shape[1]
    cycle_term = jnp.einsum("ip,pjb->ijb", coupling, ov_pairs, preferred_element_type=f32)
    cycle_term = cycle_term.reshape(pairs, slab)

    ladder = ladder_partial(row, ladder_amp, vv_factor)
    vir = lax.axis_index("vir")
    share = pairs // (n_ph * n_vec)
    own = jnp.arange(n_vir, dtype=jnp.int32)[None, :, None] == vir
    total = ladder.reshape(pairs, n_vir, slab) + jnp.where(own, cycle_term[:, None, :], 0.0)
    total = total.reshape(n_ph, n_vec, share, virtuals)
    total = scatter_sum(jnp.swapaxes(total, 0, 1), "vec")
    total = total.reshape(n_ph, share, n_vir, slab).transpose(2, 0, 1, 3)
    total = total.reshape(n_vir * n_ph // 4, 4, share, slab).transpose(1, 0, 2, 3)
    total = scatter_sum(scatter_sum(total, ("vir", "ph"), 4), ("vir", "ph"), -4)

    residual = total.T.astype(bf16)
    place = lax.axis_index(("ph", "vec"))
    pair_index = place * share + jnp.arange(share, dtype=jnp.int32)
    occ_ids = jnp.arange(eps_occ.shape[0], dtype=jnp.int32)[None, :]
    first_occ = jnp.sum(
        jnp.where((pair_index // second_count)[:, None] == occ_ids, eps_occ[None, :], 0.0), 1
    )
    second_occ = jnp.sum(
        jnp.where((pair_index % second_count)[:, None] == occ_ids, eps_occ[None, :], 0.0), 1
    )
    slab_energy = lax.dynamic_slice_in_dim(eps_vir, vir * slab, slab, 0)
    denominator = (eps_vir[0] + slab_energy)[:, None] - first_occ[None, :] - second_occ[None, :]
    update = residual.astype(f32) / denominator
    return residual, update


def solution(mesh):
    placed = (
        P(("ph", "vec"), "vir", None),
        P(None, "vir", None),
        P(("vir", "ph"), None, "vec"),
        P(("vir", "ph"), None, "vec"),
        P(("vir", "ph")),
        P(("vir", "ph")),
        P(("ph", "vec"), None, "vir"),
        P(),
        P(),
    )
    return jax.shard_map(
        local,
        mesh=mesh,
        in_specs=placed,
        out_specs=(P("vir", ("ph", "vec")), P("vir", ("ph", "vec"))),
        check_vma=False,
    )
```

```python
import functools

import jax
import jax.numpy as jnp
from jax import lax
from jax.experimental import pallas as pl
from jax.experimental.pallas import tpu as pltpu
from jax.sharding import PartitionSpec as P

LANES = 128
bf16, f32 = jnp.bfloat16, jnp.float32


def plain(
    vv_factor, ladder_amp, cycle_amp, ov_slots, owner_of, slot_of, ov_pairs, eps_vir, eps_occ
):
    chol_local, slab_width, virtuals = vv_factor.shape
    pair_count = ladder_amp.shape[2]
    row_piece = vv_factor[:, :, 0]
    factor_row = lax.all_gather(row_piece, "vir", axis=1, tiled=True)
    half = jnp.dot(
        factor_row,
        ladder_amp.reshape(virtuals, slab_width * pair_count),
        preferred_element_type=jnp.float32,
    )
    half = half.astype(jnp.bfloat16).reshape(chol_local * slab_width, pair_count)
    flat_factor = vv_factor.reshape(chol_local * slab_width, virtuals)
    block_local, occ_rows, block_part = cycle_amp.shape
    owner_total = lax.axis_size("ph")
    targets = owner_of[None, :] == jnp.arange(owner_total, dtype=jnp.int32)[:, None]
    outgoing = jnp.where(targets[:, :, None, None], cycle_amp[None], jnp.zeros((), jnp.bfloat16))
    places = jnp.where(targets, slot_of[None, :], 0)
    arrived, arrived_slots = (
        lax.all_to_all(outgoing, "ph", split_axis=0, concat_axis=0, tiled=True),
        lax.all_to_all(places, "ph", split_axis=0, concat_axis=0, tiled=True),
    )
    capacity = ov_slots.shape[0]
    picks = (
        arrived_slots.reshape(-1)[:, None] == jnp.arange(capacity, dtype=jnp.int32)[None, :]
    ).astype(jnp.bfloat16)
    arranged = jnp.einsum(
        "ns,niw->siw",
        picks,
        arrived.reshape(-1, occ_rows, block_part),
        preferred_element_type=jnp.float32,
    )
    arranged = arranged.astype(jnp.bfloat16)
    cycle_part = jnp.einsum("siw,spw->ip", arranged, ov_slots, preferred_element_type=jnp.float32)
    near_groups = lax.axis_size("ph") * lax.axis_size("vec")
    summed = lax.psum(cycle_part, ("vir", "ph", "vec"))
    vector_share = summed.shape[1] // near_groups
    own_share = lax.dynamic_slice_in_dim(
        summed, lax.axis_index(("ph", "vec")) * vector_share, vector_share, 1
    )
    coupling = own_share.astype(jnp.bfloat16)
    second_count = ov_pairs.shape[1]
    cycle_term = jnp.einsum("ip,pjb->bij", coupling, ov_pairs, preferred_element_type=jnp.float32)
    cycle_term = cycle_term.reshape(slab_width, occ_rows * second_count)
    slab_start = lax.axis_index("vir") * slab_width
    slab = (
        lax.psum_scatter(
            lax.dot_general(
                flat_factor, half, (((0,), (0,)), ((), ())), preferred_element_type=jnp.float32
            ),
            "vir",
            scatter_dimension=0,
            tiled=True,
        )
        + cycle_term
    )
    result = lax.psum_scatter(slab, ("ph", "vec"), scatter_dimension=1, tiled=True)
    residual = result.astype(jnp.bfloat16)
    share_width = result.shape[1]
    pair_index = lax.axis_index(("ph", "vec")) * share_width + jnp.arange(
        share_width, dtype=jnp.int32
    )
    occ_count = eps_occ.shape[0]
    occ_ids = jnp.arange(occ_count, dtype=jnp.int32)[None, :]
    first_occ = jnp.sum(
        jnp.where((pair_index // second_count)[:, None] == occ_ids, eps_occ[None, :], 0.0), 1
    )
    second_occ = jnp.sum(
        jnp.where((pair_index % second_count)[:, None] == occ_ids, eps_occ[None, :], 0.0), 1
    )
    slab_energy = lax.dynamic_slice_in_dim(eps_vir, slab_start, slab_width, 0)
    denominator = (eps_vir[0] + slab_energy)[:, None] - first_occ[None, :] - second_occ[None, :]
    update = residual.astype(jnp.float32) / denominator
    return (residual, update)


def shifted(x, axes, k):
    n = lax.axis_size(axes)
    return lax.ppermute(x, axes, [(i, (i + k) % n) for i in range(n)])


def round_robin(x, axes):
    return [x] + [shifted(x, axes, k) for k in range(1, lax.axis_size(axes))]


def row_kernel(*refs):
    (*x_refs, out_ref, acc) = refs
    step, rows = pl.program_id(1), x_refs[0].shape[0]
    lane = lax.broadcasted_iota(jnp.int32, acc.shape, 1)

    @pl.when(step == 0)
    def _():
        acc[...] = jnp.zeros_like(acc)

    part = jnp.zeros(acc.shape, f32)
    for q, ref in enumerate(x_refs):
        for p in range(rows):
            shift = q * rows + p
            column = ref[p].astype(f32)
            part = jnp.where(lane == shift, pltpu.roll(column, shift, 1) if shift else column, part)
    rows = rows * len(x_refs)
    part = pltpu.roll(part, step * rows, 1)
    acc[...] = jnp.where(lane // rows == step, part, acc[...])

    @pl.when(step == pl.num_programs(1) - 1)
    def _():
        piece = acc[...].T.astype(bf16)
        for k in range(out_ref.shape[0]):
            out_ref[k] = piece


def own_row(vv_factor, copies):
    chol, slab, _ = vv_factor.shape
    rows, sides = 16, 4
    steps = LANES // (rows * sides)

    def side(q):
        return pl.BlockSpec((rows, slab, LANES), lambda g, k: ((g * steps + k) * sides + q, 0, 0))

    return pl.pallas_call(
        row_kernel,
        grid=(chol // LANES, steps),
        in_specs=[side(q) for q in range(sides)],
        out_specs=pl.BlockSpec((copies, LANES, slab), lambda g, k: (0, g, 0)),
        out_shape=jax.ShapeDtypeStruct((copies, chol, slab), bf16),
        scratch_shapes=[pltpu.VMEM((slab, LANES), f32)],
        compiler_params=pltpu.CompilerParams(vmem_limit_bytes=32 << 20),
        cost_estimate=pl.CostEstimate(
            flops=2 * chol * slab * LANES, bytes_accessed=2 * chol * slab * LANES, transcendentals=0
        ),
    )(*[vv_factor] * sides)


def cycle_kernel(shares, groups, place_ref, code_ref, *refs):
    (*amp_refs, out_ref, amps, acc, block_of) = refs
    amp_refs, ov_refs = amp_refs[:groups], amp_refs[groups:]
    step = pl.program_id(0)
    blocks, slots = code_ref.shape[0], block_of.shape[0]
    own, width = 2 * amp_refs[0].shape[0], amps.shape[2]

    @pl.when(step == 0)
    def _():
        for k, ref in enumerate(amp_refs):
            for h in range(2):
                amps[pl.ds(k * own + h * (own // 2), own // 2)] = ref[
                    :, :, h * width : (h + 1) * width
                ]
        amps[blocks] = jnp.zeros(amps.shape[1:], bf16)
        acc[...] = jnp.zeros_like(acc)
        first = place_ref[0] * slots

        @pl.loop(0, slots, unroll=16)
        def _(s):
            block_of[s] = blocks

        @pl.loop(0, blocks, unroll=8)
        def _(n):
            slot = code_ref[n] - first

            @pl.when((slot >= 0) & (slot < slots))
            def _():
                block_of[slot] = n

    here, _, chol = ov_refs[0].shape
    start, count = step * len(ov_refs) * here, len(ov_refs) * here
    left = jnp.concatenate([amps[block_of[start + s]] for s in range(count)], axis=1)
    right = jnp.concatenate([ref[...].reshape(here * width, chol) for ref in ov_refs], axis=0)
    acc[...] += jnp.dot(left, right, preferred_element_type=f32)

    @pl.when(step == pl.num_programs(0) - 1)
    def _():
        share = chol // shares
        for k in range(out_ref.shape[0]):
            start = k % shares * share
            out_ref[k] = acc[:, start : start + share]


def cycle_operands(cycle_amp, owner_of, slot_of, slots):
    codes = jnp.concatenate(round_robin(owner_of * slots + slot_of, "ph"))
    near, far = jnp.split(cycle_amp, 2, 0)
    return round_robin(jnp.concatenate([near, far], 2), "ph"), codes


def cycle_partial(amps, codes, ov_slots):
    slots, chol, width = ov_slots.shape
    occ = amps[0].shape[1]
    shares = lax.axis_size(("ph", "vec"))
    copies = shares * lax.axis_size("vir")
    place = lax.axis_index("ph").astype(jnp.int32)[None]
    here, sides = 8, 4

    def side(q):
        return pl.BlockSpec((here, width, chol), lambda i: (i * sides + q, 0, 0))

    whole = pl.BlockSpec(memory_space=pltpu.VMEM)
    scalars = pl.BlockSpec(memory_space=pltpu.SMEM)
    return pl.pallas_call(
        functools.partial(cycle_kernel, shares, len(amps)),
        grid=(slots // (here * sides),),
        in_specs=[scalars, scalars]
        + [whole] * len(amps)
        + [side(q) for q in range(sides)],
        out_specs=pl.BlockSpec((copies, occ, chol // shares), lambda i: (0, 0, 0)),
        out_shape=jax.ShapeDtypeStruct((copies, occ, chol // shares), f32),
        scratch_shapes=[
            pltpu.VMEM((codes.shape[0] + 1, occ, width), bf16),
            pltpu.VMEM((occ, chol), f32),
            pltpu.SMEM((slots,), jnp.int32),
        ],
        compiler_params=pltpu.CompilerParams(vmem_limit_bytes=60 << 20),
        cost_estimate=pl.CostEstimate(
            flops=2 * occ * slots * width * chol,
            bytes_accessed=2 * slots * width * chol,
            transcendentals=0,
        ),
    )(place, codes, *amps, *[jnp.swapaxes(ov_slots, 1, 2)] * sides)


def swap_matrix(deep):
    n = deep * deep
    r = lax.broadcasted_iota(jnp.int32, (n, n), 0)
    s = lax.broadcasted_iota(jnp.int32, (n, n), 1)
    return (lax.rem(r, deep) * deep + lax.div(r, deep) == s).astype(bf16)


def ladder_kernel(sides, row_ref, amp_hbm, factor_hbm, out_ref, *scratch):
    (amp_buf, factor_buf, amp_sem, factor_sem, swap, turned, half) = scratch
    _, virtuals, deep, pairs = amp_buf.shape
    count, chol, _ = row_ref.shape
    square = deep * deep
    step, steps = pl.program_id(0), pl.num_programs(0)
    slot = lax.rem(step, 2)

    def arriving(hbm, buf, sem, step, side):
        size = buf.shape[1] // sides
        rows, slot = pl.ds(side * size, size), lax.rem(step, 2)
        block = pl.ds(pl.multiple_of(step * deep, deep), deep)
        return pltpu.make_async_copy(
            hbm.at[rows, block], buf.at[slot, rows], sem.at[slot, side]
        )

    def start(step):
        for q in range(sides):
            arriving(amp_hbm, amp_buf, amp_sem, step, q).start()
        for q in range(sides):
            arriving(factor_hbm, factor_buf, factor_sem, step, q).start()

    @pl.when(step == 0)
    def _():
        start(step)
        out_ref[...] = jnp.zeros_like(out_ref)
        swap[...] = swap_matrix(deep)

    @pl.when(step + 1 < steps)
    def _():
        start(step + 1)

    def by_matmul(first):
        rows = [slice(first + r * deep, first + (r + 1) * deep) for r in range(2)]
        block = [amp_buf[slot, r].reshape(square, pairs) for r in rows]
        block = jnp.dot(
            swap[...], jnp.concatenate(block, axis=1), preferred_element_type=f32
        ).astype(bf16)
        for i, r in enumerate(rows):
            turned[:, r, :] = block[:, i * pairs : (i + 1) * pairs].reshape(deep, deep, pairs)

    sublane = lax.broadcasted_iota(jnp.int32, (deep // 8, 8, LANES), 1)

    def by_shuffle(first):
        for h in range(pairs // LANES):
            lane = slice(h * LANES, (h + 1) * LANES)
            block = amp_buf[slot, first : first + deep, :, lane].astype(f32)
            block = block.reshape(deep // 8, 8, deep, LANES)
            for o in range(0, deep, 8):
                v = [block[:, a, o : o + 8] for a in range(8)]
                for k in (4, 2, 1):
                    keep = (sublane & k) == 0
                    for a in range(8):
                        if not a & k:
                            x, y = v[a], v[a + k]
                            v[a] = jnp.where(keep, x, pltpu.roll(y, k, 1))
                            v[a + k] = jnp.where(keep, pltpu.roll(x, 8 - k, 1), y)
                for d in range(8):
                    turned[o + d, first : first + deep, lane] = (
                        v[d].reshape(deep, LANES).astype(bf16)
                    )

    for q in range(sides):
        arriving(amp_hbm, amp_buf, amp_sem, step, q).wait()
        size = virtuals // sides
        for k in range(q * size, (q + 1) * size, 4 * deep):
            by_matmul(k)
            by_shuffle(k + 2 * deep)
            by_shuffle(k + 3 * deep)

    row = jnp.concatenate([row_ref[k] for k in range(count)], axis=1)
    for d in range(0, deep, 2):
        block = jnp.concatenate([turned[d], turned[d + 1]], axis=1)
        block = jnp.dot(row, block, preferred_element_type=f32).astype(bf16)
        half[d], half[d + 1] = block[:, :pairs], block[:, pairs:]

    for q in range(sides):
        arriving(factor_hbm, factor_buf, factor_sem, step, q).wait()
        size = chol // sides
        block = [
            half[:, k : k + deep, :].reshape(square, pairs).T
            for k in range(q * size, (q + 1) * size, deep)
        ]
        block = jnp.dot(
            jnp.concatenate(block, axis=0), swap[...], preferred_element_type=f32
        ).astype(bf16)
        block = [block[k * pairs : (k + 1) * pairs] for k in range(size // deep)]
        factor = factor_buf[slot, q * size : (q + 1) * size]
        out_ref[...] += jnp.dot(
            jnp.concatenate(block, axis=1),
            factor.reshape(size * deep, factor.shape[2]),
            preferred_element_type=f32,
        )


def ladder_partial(row, ladder_amp, vv_factor):
    virtuals, slab, pairs = ladder_amp.shape
    chol = vv_factor.shape[0]
    deep, sides = 16, 4
    whole = pl.BlockSpec(memory_space=pl.ANY)
    return pl.pallas_call(
        functools.partial(ladder_kernel, sides),
        grid=(slab // deep,),
        in_specs=[pl.BlockSpec(memory_space=pltpu.VMEM), whole, whole],
        out_specs=pl.BlockSpec((pairs, virtuals), lambda i: (0, 0)),
        out_shape=jax.ShapeDtypeStruct((pairs, virtuals), f32),
        scratch_shapes=[
            pltpu.VMEM((2, virtuals, deep, pairs), bf16),
            pltpu.VMEM((2, chol, deep, virtuals), bf16),
            pltpu.SemaphoreType.DMA((2, sides)),
            pltpu.SemaphoreType.DMA((2, sides)),
            pltpu.VMEM((deep * deep, deep * deep), bf16),
            pltpu.VMEM((deep, virtuals, pairs), bf16),
            pltpu.VMEM((deep, chol, pairs), bf16),
        ],
        compiler_params=pltpu.CompilerParams(vmem_limit_bytes=60 << 20),
        cost_estimate=pl.CostEstimate(
            flops=4 * chol * virtuals * slab * pairs,
            bytes_accessed=2 * virtuals * slab * (pairs + chol),
            transcendentals=0,
        ),
    )(row, ladder_amp, vv_factor)


def scatter_sum(x, axes, near=None):
    total_places = lax.axis_size(axes)
    me = lax.axis_index(axes)
    n = x.shape[0]

    def moved(place, k):
        if near is None:
            return (place + k) % n
        if near > 0:
            return place // near * near + (place % near + k) % near
        return (place + k * -near) % total_places

    def rank(place):
        return place if near is None else place % near if near > 0 else place // -near

    total = lax.dynamic_index_in_dim(x, rank(me), 0, keepdims=False)
    sent = x.astype(bf16)
    for k in range(1, n):
        piece = lax.dynamic_index_in_dim(sent, rank(moved(me, k)), 0, keepdims=False)
        pairs = [(i, moved(i, k)) for i in range(total_places)]
        total = total + lax.ppermute(piece, axes, pairs).astype(f32)
    return total


def local(
    vv_factor, ladder_amp, cycle_amp, ov_slots, owner_of, slot_of, ov_pairs, eps_vir, eps_occ
):
    chol, slab, virtuals = vv_factor.shape
    pairs = ladder_amp.shape[2]
    slots, _, width = ov_slots.shape
    n_vir, n_ph, n_vec = (lax.axis_size(a) for a in ("vir", "ph", "vec"))
    fits = slab == LANES and pairs == 2 * LANES and chol % LANES == 0 and slots % 32 == 0
    if not fits or 256 % width or cycle_amp.shape[0] % 2 or n_vir * n_ph % 4:
        return plain(
            vv_factor, ladder_amp, cycle_amp, ov_slots, owner_of, slot_of, ov_pairs, eps_vir, eps_occ
        )
    amps, codes = cycle_operands(cycle_amp, owner_of, slot_of, slots)
    row, amps, codes = lax.optimization_barrier((own_row(vv_factor, n_vir), amps, codes))
    row = lax.all_to_all(row, "vir", 0, 0)
    pieces = lax.all_to_all(cycle_partial(amps, codes, ov_slots), ("vir", "ph", "vec"), 0, 0)
    coupling = jnp.sum(pieces, 0).astype(bf16)
    second_count = ov_pairs.shape[1]
    cycle_term = jnp.einsum("ip,pjb->ijb", coupling, ov_pairs, preferred_element_type=f32)
    cycle_term = cycle_term.reshape(pairs, slab)

    ladder = ladder_partial(row, ladder_amp, vv_factor)
    vir = lax.axis_index("vir")
    share = pairs // (n_ph * n_vec)
    own = jnp.arange(n_vir, dtype=jnp.int32)[None, :, None] == vir
    total = ladder.reshape(pairs, n_vir, slab) + jnp.where(own, cycle_term[:, None, :], 0.0)
    total = total.reshape(n_ph, n_vec, share, virtuals)
    total = scatter_sum(jnp.swapaxes(total, 0, 1), "vec")
    total = total.reshape(n_ph, share, n_vir, slab).transpose(2, 0, 1, 3)
    total = total.reshape(n_vir * n_ph // 4, 4, share, slab).transpose(1, 0, 2, 3)
    total = scatter_sum(scatter_sum(total, ("vir", "ph"), 4), ("vir", "ph"), -4)

    residual = total.T.astype(bf16)
    place = lax.axis_index(("ph", "vec"))
    pair_index = place * share + jnp.arange(share, dtype=jnp.int32)
    occ_ids = jnp.arange(eps_occ.shape[0], dtype=jnp.int32)[None, :]
    first_occ = jnp.sum(
        jnp.where((pair_index // second_count)[:, None] == occ_ids, eps_occ[None, :], 0.0), 1
    )
    second_occ = jnp.sum(
        jnp.where((pair_index % second_count)[:, None] == occ_ids, eps_occ[None, :], 0.0), 1
    )
    slab_energy = lax.dynamic_slice_in_dim(eps_vir, vir * slab, slab, 0)
    denominator = (eps_vir[0] + slab_energy)[:, None] - first_occ[None, :] - second_occ[None, :]
    update = residual.astype(f32) / denominator
    return residual, update


def solution(mesh):
    placed = (
        P(("ph", "vec"), "vir", None),
        P(None, "vir", None),
        P(("vir", "ph"), None, "vec"),
        P(("vir", "ph"), None, "vec"),
        P(("vir", "ph")),
        P(("vir", "ph")),
        P(("ph", "vec"), None, "vir"),
        P(),
        P(),
    )
    return jax.shard_map(
        local,
        mesh=mesh,
        in_specs=placed,
        out_specs=(P("vir", ("ph", "vec")), P("vir", ("ph", "vec"))),
        check_vma=False,
    )
```

```python
import functools

import jax
import jax.numpy as jnp
from jax import lax
from jax.experimental import pallas as pl
from jax.experimental.pallas import tpu as pltpu
from jax.sharding import PartitionSpec as P

LANES = 128
bf16, f32 = jnp.bfloat16, jnp.float32


def plain(
    vv_factor, ladder_amp, cycle_amp, ov_slots, owner_of, slot_of, ov_pairs, eps_vir, eps_occ
):
    chol_local, slab_width, virtuals = vv_factor.shape
    pair_count = ladder_amp.shape[2]
    row_piece = vv_factor[:, :, 0]
    factor_row = lax.all_gather(row_piece, "vir", axis=1, tiled=True)
    half = jnp.dot(
        factor_row,
        ladder_amp.reshape(virtuals, slab_width * pair_count),
        preferred_element_type=jnp.float32,
    )
    half = half.astype(jnp.bfloat16).reshape(chol_local * slab_width, pair_count)
    flat_factor = vv_factor.reshape(chol_local * slab_width, virtuals)
    block_local, occ_rows, block_part = cycle_amp.shape
    owner_total = lax.axis_size("ph")
    targets = owner_of[None, :] == jnp.arange(owner_total, dtype=jnp.int32)[:, None]
    outgoing = jnp.where(targets[:, :, None, None], cycle_amp[None], jnp.zeros((), jnp.bfloat16))
    places = jnp.where(targets, slot_of[None, :], 0)
    arrived, arrived_slots = (
        lax.all_to_all(outgoing, "ph", split_axis=0, concat_axis=0, tiled=True),
        lax.all_to_all(places, "ph", split_axis=0, concat_axis=0, tiled=True),
    )
    capacity = ov_slots.shape[0]
    picks = (
        arrived_slots.reshape(-1)[:, None] == jnp.arange(capacity, dtype=jnp.int32)[None, :]
    ).astype(jnp.bfloat16)
    arranged = jnp.einsum(
        "ns,niw->siw",
        picks,
        arrived.reshape(-1, occ_rows, block_part),
        preferred_element_type=jnp.float32,
    )
    arranged = arranged.astype(jnp.bfloat16)
    cycle_part = jnp.einsum("siw,spw->ip", arranged, ov_slots, preferred_element_type=jnp.float32)
    near_groups = lax.axis_size("ph") * lax.axis_size("vec")
    summed = lax.psum(cycle_part, ("vir", "ph", "vec"))
    vector_share = summed.shape[1] // near_groups
    own_share = lax.dynamic_slice_in_dim(
        summed, lax.axis_index(("ph", "vec")) * vector_share, vector_share, 1
    )
    coupling = own_share.astype(jnp.bfloat16)
    second_count = ov_pairs.shape[1]
    cycle_term = jnp.einsum("ip,pjb->bij", coupling, ov_pairs, preferred_element_type=jnp.float32)
    cycle_term = cycle_term.reshape(slab_width, occ_rows * second_count)
    slab_start = lax.axis_index("vir") * slab_width
    slab = (
        lax.psum_scatter(
            lax.dot_general(
                flat_factor, half, (((0,), (0,)), ((), ())), preferred_element_type=jnp.float32
            ),
            "vir",
            scatter_dimension=0,
            tiled=True,
        )
        + cycle_term
    )
    result = lax.psum_scatter(slab, ("ph", "vec"), scatter_dimension=1, tiled=True)
    residual = result.astype(jnp.bfloat16)
    share_width = result.shape[1]
    pair_index = lax.axis_index(("ph", "vec")) * share_width + jnp.arange(
        share_width, dtype=jnp.int32
    )
    occ_count = eps_occ.shape[0]
    occ_ids = jnp.arange(occ_count, dtype=jnp.int32)[None, :]
    first_occ = jnp.sum(
        jnp.where((pair_index // second_count)[:, None] == occ_ids, eps_occ[None, :], 0.0), 1
    )
    second_occ = jnp.sum(
        jnp.where((pair_index % second_count)[:, None] == occ_ids, eps_occ[None, :], 0.0), 1
    )
    slab_energy = lax.dynamic_slice_in_dim(eps_vir, slab_start, slab_width, 0)
    denominator = (eps_vir[0] + slab_energy)[:, None] - first_occ[None, :] - second_occ[None, :]
    update = residual.astype(jnp.float32) / denominator
    return (residual, update)


def shifted(x, axes, k):
    n = lax.axis_size(axes)
    return lax.ppermute(x, axes, [(i, (i + k) % n) for i in range(n)])


def round_robin(x, axes):
    return [x] + [shifted(x, axes, k) for k in range(1, lax.axis_size(axes))]


def row_kernel(*refs):
    (*x_refs, out_ref, acc) = refs
    step, rows = pl.program_id(1), x_refs[0].shape[0]
    lane = lax.broadcasted_iota(jnp.int32, acc.shape, 1)

    @pl.when(step == 0)
    def _():
        acc[...] = jnp.zeros_like(acc)

    part = jnp.zeros(acc.shape, f32)
    for q, ref in enumerate(x_refs):
        for p in range(rows):
            shift = q * rows + p
            column = ref[p].astype(f32)
            part = jnp.where(lane == shift, pltpu.roll(column, shift, 1) if shift else column, part)
    rows = rows * len(x_refs)
    part = pltpu.roll(part, step * rows, 1)
    acc[...] = jnp.where(lane // rows == step, part, acc[...])

    @pl.when(step == pl.num_programs(1) - 1)
    def _():
        piece = acc[...].T.astype(bf16)
        for k in range(out_ref.shape[0]):
            out_ref[k] = piece


def own_row(vv_factor, copies):
    chol, slab, _ = vv_factor.shape
    rows, sides = 16, 4
    steps = LANES // (rows * sides)

    def side(q):
        return pl.BlockSpec((rows, slab, LANES), lambda g, k: ((g * steps + k) * sides + q, 0, 0))

    return pl.pallas_call(
        row_kernel,
        grid=(chol // LANES, steps),
        in_specs=[side(q) for q in range(sides)],
        out_specs=pl.BlockSpec((copies, LANES, slab), lambda g, k: (0, g, 0)),
        out_shape=jax.ShapeDtypeStruct((copies, chol, slab), bf16),
        scratch_shapes=[pltpu.VMEM((slab, LANES), f32)],
        compiler_params=pltpu.CompilerParams(vmem_limit_bytes=32 << 20),
        cost_estimate=pl.CostEstimate(
            flops=2 * chol * slab * LANES, bytes_accessed=2 * chol * slab * LANES, transcendentals=0
        ),
    )(*[vv_factor] * sides)


def cycle_kernel(shares, groups, place_ref, code_ref, *refs):
    (*amp_refs, out_ref, amps, acc, block_of) = refs
    amp_refs, ov_refs = amp_refs[:groups], amp_refs[groups:]
    step = pl.program_id(0)
    blocks, slots = code_ref.shape[0], block_of.shape[0]
    own, width = 2 * amp_refs[0].shape[0], amps.shape[2]

    @pl.when(step == 0)
    def _():
        for k, ref in enumerate(amp_refs):
            for h in range(2):
                amps[pl.ds(k * own + h * (own // 2), own // 2)] = ref[
                    :, :, h * width : (h + 1) * width
                ]
        amps[blocks] = jnp.zeros(amps.shape[1:], bf16)
        acc[...] = jnp.zeros_like(acc)
        first = place_ref[0] * slots

        @pl.loop(0, slots, unroll=16)
        def _(s):
            block_of[s] = blocks

        @pl.loop(0, blocks, unroll=8)
        def _(n):
            slot = code_ref[n] - first

            @pl.when((slot >= 0) & (slot < slots))
            def _():
                block_of[slot] = n

    here, _, chol = ov_refs[0].shape
    start, count = step * len(ov_refs) * here, len(ov_refs) * here
    left = jnp.concatenate([amps[block_of[start + s]] for s in range(count)], axis=1)
    right = jnp.concatenate([ref[...].reshape(here * width, chol) for ref in ov_refs], axis=0)
    acc[...] += jnp.dot(left, right, preferred_element_type=f32)

    @pl.when(step == pl.num_programs(0) - 1)
    def _():
        share = chol // shares
        for k in range(out_ref.shape[0]):
            start = k % shares * share
            out_ref[k] = acc[:, start : start + share]


def cycle_operands(cycle_amp, owner_of, slot_of, slots):
    codes = jnp.concatenate(round_robin(owner_of * slots + slot_of, "ph"))
    near, far = jnp.split(cycle_amp, 2, 0)
    return round_robin(jnp.concatenate([near, far], 2), "ph"), codes


def cycle_partial(amps, codes, ov_slots):
    slots, chol, width = ov_slots.shape
    occ = amps[0].shape[1]
    shares = lax.axis_size(("ph", "vec"))
    copies = shares * lax.axis_size("vir")
    place = lax.axis_index("ph").astype(jnp.int32)[None]
    here, sides = 8, 4

    def side(q):
        return pl.BlockSpec((here, width, chol), lambda i: (i * sides + q, 0, 0))

    whole = pl.BlockSpec(memory_space=pltpu.VMEM)
    scalars = pl.BlockSpec(memory_space=pltpu.SMEM)
    return pl.pallas_call(
        functools.partial(cycle_kernel, shares, len(amps)),
        grid=(slots // (here * sides),),
        in_specs=[scalars, scalars]
        + [whole] * len(amps)
        + [side(q) for q in range(sides)],
        out_specs=pl.BlockSpec((copies, occ, chol // shares), lambda i: (0, 0, 0)),
        out_shape=jax.ShapeDtypeStruct((copies, occ, chol // shares), f32),
        scratch_shapes=[
            pltpu.VMEM((codes.shape[0] + 1, occ, width), bf16),
            pltpu.VMEM((occ, chol), f32),
            pltpu.SMEM((slots,), jnp.int32),
        ],
        compiler_params=pltpu.CompilerParams(vmem_limit_bytes=60 << 20),
        cost_estimate=pl.CostEstimate(
            flops=2 * occ * slots * width * chol,
            bytes_accessed=2 * slots * width * chol,
            transcendentals=0,
        ),
    )(place, codes, *amps, *[jnp.swapaxes(ov_slots, 1, 2)] * sides)


def swap_matrix(deep):
    n = deep * deep
    r = lax.broadcasted_iota(jnp.int32, (n, n), 0)
    s = lax.broadcasted_iota(jnp.int32, (n, n), 1)
    return (lax.rem(r, deep) * deep + lax.div(r, deep) == s).astype(bf16)


def ladder_kernel(sides, row_ref, amp_hbm, factor_hbm, out_ref, *scratch):
    (amp_buf, factor_buf, amp_sem, factor_sem, swap, turned, half, flat) = scratch
    _, virtuals, deep, pairs = amp_buf.shape
    count, chol, _ = row_ref.shape
    square = deep * deep
    step, steps = pl.program_id(0), pl.num_programs(0)
    slot = lax.rem(step, 2)

    def arriving(hbm, buf, sem, step, side):
        size = buf.shape[1] // sides
        rows, slot = pl.ds(side * size, size), lax.rem(step, 2)
        block = pl.ds(pl.multiple_of(step * deep, deep), deep)
        return pltpu.make_async_copy(
            hbm.at[rows, block], buf.at[slot, rows], sem.at[slot, side]
        )

    def start(step):
        for q in range(sides):
            arriving(amp_hbm, amp_buf, amp_sem, step, q).start()
        for q in range(sides):
            arriving(factor_hbm, factor_buf, factor_sem, step, q).start()

    @pl.when(step == 0)
    def _():
        start(step)
        out_ref[...] = jnp.zeros_like(out_ref)
        swap[...] = swap_matrix(deep)

    @pl.when(step + 1 < steps)
    def _():
        start(step + 1)

    def later(jobs):
        store = None
        for job in jobs:
            after = job()
            if store is not None:
                store()
            store = after
        store()

    def reorder(first):
        rows = [slice(first + r * deep, first + (r + 1) * deep) for r in range(2)]
        block = [amp_buf[slot, r].reshape(square, pairs) for r in rows]
        block = jnp.dot(
            swap[...], jnp.concatenate(block, axis=1), preferred_element_type=f32
        ).astype(bf16)

        def store():
            for i, r in enumerate(rows):
                turned[:, r, :] = block[:, i * pairs : (i + 1) * pairs].reshape(deep, deep, pairs)

        return store

    for q in range(sides):
        arriving(amp_hbm, amp_buf, amp_sem, step, q).wait()
        size = virtuals // sides
        later(
            functools.partial(reorder, k) for k in range(q * size, (q + 1) * size, 2 * deep)
        )

    row = jnp.concatenate([row_ref[k] for k in range(count)], axis=1)

    def halves(d):
        block = jnp.concatenate([turned[d], turned[d + 1]], axis=1)
        block = jnp.dot(row, block, preferred_element_type=f32).astype(bf16)

        def store():
            half[d], half[d + 1] = block[:, :pairs], block[:, pairs:]

        return store

    later(functools.partial(halves, d) for d in range(0, deep, 2))

    def flatten(first):
        parts = range(first, first + 4 * deep, deep)
        block = [half[:, k : k + deep, :].reshape(square, pairs).T for k in parts]
        block = jnp.dot(
            jnp.concatenate(block, axis=0), swap[...], preferred_element_type=f32
        ).astype(bf16)

        def store():
            for i, k in enumerate(parts):
                flat[:, k * deep : (k + deep) * deep] = block[i * pairs : (i + 1) * pairs]

        return store

    later(functools.partial(flatten, k) for k in range(0, chol, 4 * deep))
    for q in range(sides):
        arriving(factor_hbm, factor_buf, factor_sem, step, q).wait()
    columns = 512

    def ladder(first):
        block = factor_buf[slot, :, :, first : first + columns].reshape(chol * deep, columns)
        block = jnp.dot(flat[...], block, preferred_element_type=f32)

        def store():
            out_ref[:, first : first + columns] += block

        return store

    later(functools.partial(ladder, n) for n in range(0, out_ref.shape[1], columns))


def ladder_partial(row, ladder_amp, vv_factor):
    virtuals, slab, pairs = ladder_amp.shape
    chol = vv_factor.shape[0]
    deep, sides = 16, 4
    whole = pl.BlockSpec(memory_space=pl.ANY)
    return pl.pallas_call(
        functools.partial(ladder_kernel, sides),
        grid=(slab // deep,),
        in_specs=[pl.BlockSpec(memory_space=pltpu.VMEM), whole, whole],
        out_specs=pl.BlockSpec((pairs, virtuals), lambda i: (0, 0)),
        out_shape=jax.ShapeDtypeStruct((pairs, virtuals), f32),
        scratch_shapes=[
            pltpu.VMEM((2, virtuals, deep, pairs), bf16),
            pltpu.VMEM((2, chol, deep, virtuals), bf16),
            pltpu.SemaphoreType.DMA((2, sides)),
            pltpu.SemaphoreType.DMA((2, sides)),
            pltpu.VMEM((deep * deep, deep * deep), bf16),
            pltpu.VMEM((deep, virtuals, pairs), bf16),
            pltpu.VMEM((deep, chol, pairs), bf16),
            pltpu.VMEM((pairs, chol * deep), bf16),
        ],
        compiler_params=pltpu.CompilerParams(vmem_limit_bytes=60 << 20),
        cost_estimate=pl.CostEstimate(
            flops=4 * chol * virtuals * slab * pairs,
            bytes_accessed=2 * virtuals * slab * (pairs + chol),
            transcendentals=0,
        ),
    )(row, ladder_amp, vv_factor)


def scatter_sum(x, axes, near=None):
    total_places = lax.axis_size(axes)
    me = lax.axis_index(axes)
    n = x.shape[0]

    def moved(place, k):
        if near is None:
            return (place + k) % n
        if near > 0:
            return place // near * near + (place % near + k) % near
        return (place + k * -near) % total_places

    def rank(place):
        return place if near is None else place % near if near > 0 else place // -near

    total = lax.dynamic_index_in_dim(x, rank(me), 0, keepdims=False)
    sent = x.astype(bf16)
    for k in range(1, n):
        piece = lax.dynamic_index_in_dim(sent, rank(moved(me, k)), 0, keepdims=False)
        pairs = [(i, moved(i, k)) for i in range(total_places)]
        total = total + lax.ppermute(piece, axes, pairs).astype(f32)
    return total


def local(
    vv_factor, ladder_amp, cycle_amp, ov_slots, owner_of, slot_of, ov_pairs, eps_vir, eps_occ
):
    chol, slab, virtuals = vv_factor.shape
    pairs = ladder_amp.shape[2]
    slots, _, width = ov_slots.shape
    n_vir, n_ph, n_vec = (lax.axis_size(a) for a in ("vir", "ph", "vec"))
    fits = slab == LANES and virtuals % 512 == 0 and pairs == 2 * LANES and chol % LANES == 0 and slots % 32 == 0
    if not fits or 256 % width or cycle_amp.shape[0] % 2 or n_vir * n_ph % 4:
        return plain(
            vv_factor, ladder_amp, cycle_amp, ov_slots, owner_of, slot_of, ov_pairs, eps_vir, eps_occ
        )
    amps, codes = cycle_operands(cycle_amp, owner_of, slot_of, slots)
    row, amps, codes = lax.optimization_barrier((own_row(vv_factor, n_vir), amps, codes))
    row = lax.all_to_all(row, "vir", 0, 0)
    pieces = lax.all_to_all(cycle_partial(amps, codes, ov_slots), ("vir", "ph", "vec"), 0, 0)
    coupling = jnp.sum(pieces, 0).astype(bf16)
    second_count = ov_pairs.shape[1]
    cycle_term = jnp.einsum("ip,pjb->ijb", coupling, ov_pairs, preferred_element_type=f32)
    cycle_term = cycle_term.reshape(pairs, slab)

    ladder = ladder_partial(row, ladder_amp, vv_factor)
    vir = lax.axis_index("vir")
    share = pairs // (n_ph * n_vec)
    own = jnp.arange(n_vir, dtype=jnp.int32)[None, :, None] == vir
    total = ladder.reshape(pairs, n_vir, slab) + jnp.where(own, cycle_term[:, None, :], 0.0)
    total = total.reshape(n_ph, n_vec, share, virtuals)
    total = scatter_sum(jnp.swapaxes(total, 0, 1), "vec")
    total = total.reshape(n_ph, share, n_vir, slab).transpose(2, 0, 1, 3)
    total = total.reshape(n_vir * n_ph // 4, 4, share, slab).transpose(1, 0, 2, 3)
    total = scatter_sum(scatter_sum(total, ("vir", "ph"), 4), ("vir", "ph"), -4)

    residual = total.T.astype(bf16)
    place = lax.axis_index(("ph", "vec"))
    pair_index = place * share + jnp.arange(share, dtype=jnp.int32)
    occ_ids = jnp.arange(eps_occ.shape[0], dtype=jnp.int32)[None, :]
    first_occ = jnp.sum(
        jnp.where((pair_index // second_count)[:, None] == occ_ids, eps_occ[None, :], 0.0), 1
    )
    second_occ = jnp.sum(
        jnp.where((pair_index % second_count)[:, None] == occ_ids, eps_occ[None, :], 0.0), 1
    )
    slab_energy = lax.dynamic_slice_in_dim(eps_vir, vir * slab, slab, 0)
    denominator = (eps_vir[0] + slab_energy)[:, None] - first_occ[None, :] - second_occ[None, :]
    update = residual.astype(f32) / denominator
    return residual, update


def solution(mesh):
    placed = (
        P(("ph", "vec"), "vir", None),
        P(None, "vir", None),
        P(("vir", "ph"), None, "vec"),
        P(("vir", "ph"), None, "vec"),
        P(("vir", "ph")),
        P(("vir", "ph")),
        P(("ph", "vec"), None, "vir"),
        P(),
        P(),
    )
    return jax.shard_map(
        local,
        mesh=mesh,
        in_specs=placed,
        out_specs=(P("vir", ("ph", "vec")), P("vir", ("ph", "vec"))),
        check_vma=False,
    )
```

```python
import functools

import jax
import jax.numpy as jnp
from jax import lax
from jax.experimental import pallas as pl
from jax.experimental.pallas import tpu as pltpu
from jax.sharding import PartitionSpec as P

LANES = 128
bf16, f32 = jnp.bfloat16, jnp.float32


def plain(
    vv_factor, ladder_amp, cycle_amp, ov_slots, owner_of, slot_of, ov_pairs, eps_vir, eps_occ
):
    chol_local, slab_width, virtuals = vv_factor.shape
    pair_count = ladder_amp.shape[2]
    row_piece = vv_factor[:, :, 0]
    factor_row = lax.all_gather(row_piece, "vir", axis=1, tiled=True)
    half = jnp.dot(
        factor_row,
        ladder_amp.reshape(virtuals, slab_width * pair_count),
        preferred_element_type=jnp.float32,
    )
    half = half.astype(jnp.bfloat16).reshape(chol_local * slab_width, pair_count)
    flat_factor = vv_factor.reshape(chol_local * slab_width, virtuals)
    block_local, occ_rows, block_part = cycle_amp.shape
    owner_total = lax.axis_size("ph")
    targets = owner_of[None, :] == jnp.arange(owner_total, dtype=jnp.int32)[:, None]
    outgoing = jnp.where(targets[:, :, None, None], cycle_amp[None], jnp.zeros((), jnp.bfloat16))
    places = jnp.where(targets, slot_of[None, :], 0)
    arrived, arrived_slots = (
        lax.all_to_all(outgoing, "ph", split_axis=0, concat_axis=0, tiled=True),
        lax.all_to_all(places, "ph", split_axis=0, concat_axis=0, tiled=True),
    )
    capacity = ov_slots.shape[0]
    picks = (
        arrived_slots.reshape(-1)[:, None] == jnp.arange(capacity, dtype=jnp.int32)[None, :]
    ).astype(jnp.bfloat16)
    arranged = jnp.einsum(
        "ns,niw->siw",
        picks,
        arrived.reshape(-1, occ_rows, block_part),
        preferred_element_type=jnp.float32,
    )
    arranged = arranged.astype(jnp.bfloat16)
    cycle_part = jnp.einsum("siw,spw->ip", arranged, ov_slots, preferred_element_type=jnp.float32)
    near_groups = lax.axis_size("ph") * lax.axis_size("vec")
    summed = lax.psum(cycle_part, ("vir", "ph", "vec"))
    vector_share = summed.shape[1] // near_groups
    own_share = lax.dynamic_slice_in_dim(
        summed, lax.axis_index(("ph", "vec")) * vector_share, vector_share, 1
    )
    coupling = own_share.astype(jnp.bfloat16)
    second_count = ov_pairs.shape[1]
    cycle_term = jnp.einsum("ip,pjb->bij", coupling, ov_pairs, preferred_element_type=jnp.float32)
    cycle_term = cycle_term.reshape(slab_width, occ_rows * second_count)
    slab_start = lax.axis_index("vir") * slab_width
    slab = (
        lax.psum_scatter(
            lax.dot_general(
                flat_factor, half, (((0,), (0,)), ((), ())), preferred_element_type=jnp.float32
            ),
            "vir",
            scatter_dimension=0,
            tiled=True,
        )
        + cycle_term
    )
    result = lax.psum_scatter(slab, ("ph", "vec"), scatter_dimension=1, tiled=True)
    residual = result.astype(jnp.bfloat16)
    share_width = result.shape[1]
    pair_index = lax.axis_index(("ph", "vec")) * share_width + jnp.arange(
        share_width, dtype=jnp.int32
    )
    occ_count = eps_occ.shape[0]
    occ_ids = jnp.arange(occ_count, dtype=jnp.int32)[None, :]
    first_occ = jnp.sum(
        jnp.where((pair_index // second_count)[:, None] == occ_ids, eps_occ[None, :], 0.0), 1
    )
    second_occ = jnp.sum(
        jnp.where((pair_index % second_count)[:, None] == occ_ids, eps_occ[None, :], 0.0), 1
    )
    slab_energy = lax.dynamic_slice_in_dim(eps_vir, slab_start, slab_width, 0)
    denominator = (eps_vir[0] + slab_energy)[:, None] - first_occ[None, :] - second_occ[None, :]
    update = residual.astype(jnp.float32) / denominator
    return (residual, update)


def shifted(x, axes, k):
    n = lax.axis_size(axes)
    return lax.ppermute(x, axes, [(i, (i + k) % n) for i in range(n)])


def round_robin(x, axes):
    return [x] + [shifted(x, axes, k) for k in range(1, lax.axis_size(axes))]


def row_kernel(*refs):
    (*x_refs, out_ref, acc) = refs
    step, rows = pl.program_id(1), x_refs[0].shape[0]
    lane = lax.broadcasted_iota(jnp.int32, acc.shape, 1)

    @pl.when(step == 0)
    def _():
        acc[...] = jnp.zeros_like(acc)

    part = jnp.zeros(acc.shape, f32)
    for q, ref in enumerate(x_refs):
        for p in range(rows):
            shift = q * rows + p
            column = ref[p].astype(f32)
            part = jnp.where(lane == shift, pltpu.roll(column, shift, 1) if shift else column, part)
    rows = rows * len(x_refs)
    part = pltpu.roll(part, step * rows, 1)
    acc[...] = jnp.where(lane // rows == step, part, acc[...])

    @pl.when(step == pl.num_programs(1) - 1)
    def _():
        piece = acc[...].T.astype(bf16)
        for k in range(out_ref.shape[0]):
            out_ref[k] = piece


def own_row(vv_factor, copies):
    chol, slab, _ = vv_factor.shape
    rows, sides = 16, 4
    steps = LANES // (rows * sides)

    def side(q):
        return pl.BlockSpec((rows, slab, LANES), lambda g, k: ((g * steps + k) * sides + q, 0, 0))

    return pl.pallas_call(
        row_kernel,
        grid=(chol // LANES, steps),
        in_specs=[side(q) for q in range(sides)],
        out_specs=pl.BlockSpec((copies, LANES, slab), lambda g, k: (0, g, 0)),
        out_shape=jax.ShapeDtypeStruct((copies, chol, slab), bf16),
        scratch_shapes=[pltpu.VMEM((slab, LANES), f32)],
        compiler_params=pltpu.CompilerParams(vmem_limit_bytes=32 << 20),
        cost_estimate=pl.CostEstimate(
            flops=2 * chol * slab * LANES, bytes_accessed=2 * chol * slab * LANES, transcendentals=0
        ),
    )(*[vv_factor] * sides)


def cycle_kernel(shares, groups, place_ref, code_ref, *refs):
    (*amp_refs, out_ref, amps, acc, block_of) = refs
    amp_refs, ov_refs = amp_refs[:groups], amp_refs[groups:]
    step = pl.program_id(0)
    blocks, slots = code_ref.shape[0], block_of.shape[0]
    own, width = 2 * amp_refs[0].shape[0], amps.shape[2]

    @pl.when(step == 0)
    def _():
        for k, ref in enumerate(amp_refs):
            for h in range(2):
                amps[pl.ds(k * own + h * (own // 2), own // 2)] = ref[
                    :, :, h * width : (h + 1) * width
                ]
        amps[blocks] = jnp.zeros(amps.shape[1:], bf16)
        acc[...] = jnp.zeros_like(acc)
        first = place_ref[0] * slots

        @pl.loop(0, slots, unroll=16)
        def _(s):
            block_of[s] = blocks

        @pl.loop(0, blocks, unroll=8)
        def _(n):
            slot = code_ref[n] - first

            @pl.when((slot >= 0) & (slot < slots))
            def _():
                block_of[slot] = n

    here, _, chol = ov_refs[0].shape
    start, count = step * len(ov_refs) * here, len(ov_refs) * here
    left = jnp.concatenate([amps[block_of[start + s]] for s in range(count)], axis=1)
    right = jnp.concatenate([ref[...].reshape(here * width, chol) for ref in ov_refs], axis=0)
    acc[...] += jnp.dot(left, right, preferred_element_type=f32)

    @pl.when(step == pl.num_programs(0) - 1)
    def _():
        share = chol // shares
        for k in range(out_ref.shape[0]):
            start = k % shares * share
            out_ref[k] = acc[:, start : start + share]


def cycle_operands(cycle_amp, owner_of, slot_of, slots):
    codes = jnp.concatenate(round_robin(owner_of * slots + slot_of, "ph"))
    near, far = jnp.split(cycle_amp, 2, 0)
    return round_robin(jnp.concatenate([near, far], 2), "ph"), codes


def cycle_partial(amps, codes, ov_slots):
    slots, chol, width = ov_slots.shape
    occ = amps[0].shape[1]
    shares = lax.axis_size(("ph", "vec"))
    copies = shares * lax.axis_size("vir")
    place = lax.axis_index("ph").astype(jnp.int32)[None]
    here, sides = 8, 4

    def side(q):
        return pl.BlockSpec((here, width, chol), lambda i: (i * sides + q, 0, 0))

    whole = pl.BlockSpec(memory_space=pltpu.VMEM)
    scalars = pl.BlockSpec(memory_space=pltpu.SMEM)
    return pl.pallas_call(
        functools.partial(cycle_kernel, shares, len(amps)),
        grid=(slots // (here * sides),),
        in_specs=[scalars, scalars]
        + [whole] * len(amps)
        + [side(q) for q in range(sides)],
        out_specs=pl.BlockSpec((copies, occ, chol // shares), lambda i: (0, 0, 0)),
        out_shape=jax.ShapeDtypeStruct((copies, occ, chol // shares), f32),
        scratch_shapes=[
            pltpu.VMEM((codes.shape[0] + 1, occ, width), bf16),
            pltpu.VMEM((occ, chol), f32),
            pltpu.SMEM((slots,), jnp.int32),
        ],
        compiler_params=pltpu.CompilerParams(vmem_limit_bytes=60 << 20),
        cost_estimate=pl.CostEstimate(
            flops=2 * occ * slots * width * chol,
            bytes_accessed=2 * slots * width * chol,
            transcendentals=0,
        ),
    )(place, codes, *amps, *[jnp.swapaxes(ov_slots, 1, 2)] * sides)


def swap_matrix(deep):
    n = deep * deep
    r = lax.broadcasted_iota(jnp.int32, (n, n), 0)
    s = lax.broadcasted_iota(jnp.int32, (n, n), 1)
    return (lax.rem(r, deep) * deep + lax.div(r, deep) == s).astype(bf16)


def ladder_kernel(sides, row_ref, amp_hbm, factor_hbm, out_ref, *scratch):
    (amp_buf, factor_buf, amp_sem, factor_sem, swap, turned, half, flat) = scratch
    _, virtuals, deep, pairs = amp_buf.shape
    count, chol, _ = row_ref.shape
    square = deep * deep
    step, blocks = pl.program_id(0), pl.num_programs(0) - 1
    slot, before = lax.rem(step, 2), lax.rem(step + 1, 2)

    def arriving(hbm, buf, sem, step, side):
        size = buf.shape[1] // sides
        rows, slot = pl.ds(side * size, size), lax.rem(step, 2)
        block = pl.ds(pl.multiple_of(step * deep, deep), deep)
        return pltpu.make_async_copy(
            hbm.at[rows, block], buf.at[slot, rows], sem.at[slot, side]
        )

    @pl.when(step == 0)
    def _():
        for q in range(sides):
            arriving(amp_hbm, amp_buf, amp_sem, step, q).start()
        out_ref[...] = jnp.zeros_like(out_ref)
        swap[...] = swap_matrix(deep)

    @pl.when(step + 1 < blocks)
    def _():
        for q in range(sides):
            arriving(amp_hbm, amp_buf, amp_sem, step + 1, q).start()

    @pl.when(step < blocks)
    def _():
        for q in range(sides):
            arriving(factor_hbm, factor_buf, factor_sem, step, q).start()

    def later(jobs):
        store = None
        for job in jobs:
            after = job()
            if store is not None:
                store()
            store = after
        store()

    def by_matmul(first):
        rows = [slice(first + r * deep, first + (r + 1) * deep) for r in range(2)]
        block = [amp_buf[slot, r].reshape(square, pairs) for r in rows]
        block = jnp.dot(
            swap[...], jnp.concatenate(block, axis=1), preferred_element_type=f32
        ).astype(bf16)

        def store():
            for i, r in enumerate(rows):
                turned[:, r, :] = block[:, i * pairs : (i + 1) * pairs].reshape(deep, deep, pairs)

        return store

    sublane = lax.broadcasted_iota(jnp.int32, (deep // 8, 8, LANES), 1)

    def by_shuffle(first, h):
        rows, lane = slice(first, first + deep), slice(h * LANES, (h + 1) * LANES)
        block = amp_buf[slot, rows, :, lane].astype(f32).reshape(deep // 8, 8, deep, LANES)
        result = []
        for o in range(0, deep, 8):
            v = [block[:, a, o : o + 8] for a in range(8)]
            for k in (4, 2, 1):
                keep = (sublane & k) == 0
                for a in range(8):
                    if not a & k:
                        x, y = v[a], v[a + k]
                        v[a] = jnp.where(keep, x, pltpu.roll(y, k, 1))
                        v[a + k] = jnp.where(keep, pltpu.roll(x, 8 - k, 1), y)
            result += [x.reshape(deep, LANES).astype(bf16) for x in v]

        def store():
            for d in range(deep):
                turned[d, rows, lane] = result[d]

        return store

    def ladder(side, first):
        size, column = chol // sides, slice(first, first + 256)
        block = factor_buf[before, side * size : (side + 1) * size, :, column]
        block = jnp.dot(
            flat[:, side * size * deep : (side + 1) * size * deep],
            block.reshape(size * deep, 256),
            preferred_element_type=f32,
        )

        def store():
            out_ref[:, column] += block

        return store

    def reorder_jobs(side):
        size, unit = virtuals // sides, 2 * deep
        firsts = range(side * size, (side + 1) * size, unit)
        shuffles = [
            functools.partial(by_shuffle, k + r, h)
            for i, k in enumerate(firsts)
            if i % 4
            for r in range(0, unit, deep)
            for h in range(pairs // LANES)
        ]
        matmuls = [functools.partial(by_matmul, k) for k in firsts[::4]]
        share = len(shuffles) // 4
        for i in range(4):
            yield matmuls[i // 2 : i // 2 + 1] * (1 - i % 2) + shuffles[i * share : (i + 1) * share]

    def ladder_jobs(side):
        width = out_ref.shape[1] // 4
        for i in range(4):
            yield [
                functools.partial(ladder, side, n) for n in range(i * width, (i + 1) * width, 256)
            ]

    row = jnp.concatenate([row_ref[k] for k in range(count)], axis=1)

    def halves(d):
        block = jnp.concatenate([turned[d], turned[d + 1]], axis=1)
        block = jnp.dot(row, block, preferred_element_type=f32).astype(bf16)

        def store():
            half[d], half[d + 1] = block[:, :pairs], block[:, pairs:]

        return store

    def flatten(first):
        parts = range(first, first + 4 * deep, deep)
        block = [half[:, k : k + deep, :].reshape(square, pairs).T for k in parts]
        block = jnp.dot(
            jnp.concatenate(block, axis=0), swap[...], preferred_element_type=f32
        ).astype(bf16)

        def store():
            for i, k in enumerate(parts):
                flat[:, k * deep : (k + deep) * deep] = block[i * pairs : (i + 1) * pairs]

        return store

    def stages(early, late):
        if late:
            for q in range(sides):
                arriving(factor_hbm, factor_buf, factor_sem, step - 1, q).wait()
        for q in range(sides):
            if early:
                arriving(amp_hbm, amp_buf, amp_sem, step, q).wait()
            jobs = []
            for one, other in zip(ladder_jobs(q), reorder_jobs(q)):
                jobs += one * late + other * early
            later(job for job in jobs)
        if early:
            later(functools.partial(halves, d) for d in range(0, deep, 2))
            later(functools.partial(flatten, k) for k in range(0, chol, 4 * deep))

    @pl.when(step == 0)
    def _():
        stages(True, False)

    @pl.when((step > 0) & (step < blocks))
    def _():
        stages(True, True)

    @pl.when(step == blocks)
    def _():
        stages(False, True)


def ladder_partial(row, ladder_amp, vv_factor):
    virtuals, slab, pairs = ladder_amp.shape
    chol = vv_factor.shape[0]
    deep, sides = 16, 4
    whole = pl.BlockSpec(memory_space=pl.ANY)
    return pl.pallas_call(
        functools.partial(ladder_kernel, sides),
        grid=(slab // deep + 1,),
        in_specs=[pl.BlockSpec(memory_space=pltpu.VMEM), whole, whole],
        out_specs=pl.BlockSpec((pairs, virtuals), lambda i: (0, 0)),
        out_shape=jax.ShapeDtypeStruct((pairs, virtuals), f32),
        scratch_shapes=[
            pltpu.VMEM((2, virtuals, deep, pairs), bf16),
            pltpu.VMEM((2, chol, deep, virtuals), bf16),
            pltpu.SemaphoreType.DMA((2, sides)),
            pltpu.SemaphoreType.DMA((2, sides)),
            pltpu.VMEM((deep * deep, deep * deep), bf16),
            pltpu.VMEM((deep, virtuals, pairs), bf16),
            pltpu.VMEM((deep, chol, pairs), bf16),
            pltpu.VMEM((pairs, chol * deep), bf16),
        ],
        compiler_params=pltpu.CompilerParams(vmem_limit_bytes=60 << 20),
        cost_estimate=pl.CostEstimate(
            flops=4 * chol * virtuals * slab * pairs,
            bytes_accessed=2 * virtuals * slab * (pairs + chol),
            transcendentals=0,
        ),
    )(row, ladder_amp, vv_factor)


def scatter_sum(x, axes, near=None):
    total_places = lax.axis_size(axes)
    me = lax.axis_index(axes)
    n = x.shape[0]

    def moved(place, k):
        if near is None:
            return (place + k) % n
        if near > 0:
            return place // near * near + (place % near + k) % near
        return (place + k * -near) % total_places

    def rank(place):
        return place if near is None else place % near if near > 0 else place // -near

    total = lax.dynamic_index_in_dim(x, rank(me), 0, keepdims=False)
    sent = x.astype(bf16)
    for k in range(1, n):
        piece = lax.dynamic_index_in_dim(sent, rank(moved(me, k)), 0, keepdims=False)
        pairs = [(i, moved(i, k)) for i in range(total_places)]
        total = total + lax.ppermute(piece, axes, pairs).astype(f32)
    return total


def local(
    vv_factor, ladder_amp, cycle_amp, ov_slots, owner_of, slot_of, ov_pairs, eps_vir, eps_occ
):
    chol, slab, virtuals = vv_factor.shape
    pairs = ladder_amp.shape[2]
    slots, _, width = ov_slots.shape
    n_vir, n_ph, n_vec = (lax.axis_size(a) for a in ("vir", "ph", "vec"))
    fits = slab == LANES and virtuals % 1024 == 0 and pairs == 2 * LANES and chol % LANES == 0 and slots % 32 == 0
    if not fits or 256 % width or cycle_amp.shape[0] % 2 or n_vir * n_ph % 4:
        return plain(
            vv_factor, ladder_amp, cycle_amp, ov_slots, owner_of, slot_of, ov_pairs, eps_vir, eps_occ
        )
    amps, codes = cycle_operands(cycle_amp, owner_of, slot_of, slots)
    row, amps, codes = lax.optimization_barrier((own_row(vv_factor, n_vir), amps, codes))
    row = lax.all_to_all(row, "vir", 0, 0)
    pieces = lax.all_to_all(cycle_partial(amps, codes, ov_slots), ("vir", "ph", "vec"), 0, 0)
    coupling = jnp.sum(pieces, 0).astype(bf16)
    second_count = ov_pairs.shape[1]
    cycle_term = jnp.einsum("ip,pjb->ijb", coupling, ov_pairs, preferred_element_type=f32)
    cycle_term = cycle_term.reshape(pairs, slab)

    ladder = ladder_partial(row, ladder_amp, vv_factor)
    vir = lax.axis_index("vir")
    share = pairs // (n_ph * n_vec)
    own = jnp.arange(n_vir, dtype=jnp.int32)[None, :, None] == vir
    total = ladder.reshape(pairs, n_vir, slab) + jnp.where(own, cycle_term[:, None, :], 0.0)
    total = total.reshape(n_ph, n_vec, share, virtuals)
    total = scatter_sum(jnp.swapaxes(total, 0, 1), "vec")
    total = total.reshape(n_ph, share, n_vir, slab).transpose(2, 0, 1, 3)
    total = total.reshape(n_vir * n_ph // 4, 4, share, slab).transpose(1, 0, 2, 3)
    total = scatter_sum(scatter_sum(total, ("vir", "ph"), 4), ("vir", "ph"), -4)

    residual = total.T.astype(bf16)
    place = lax.axis_index(("ph", "vec"))
    pair_index = place * share + jnp.arange(share, dtype=jnp.int32)
    occ_ids = jnp.arange(eps_occ.shape[0], dtype=jnp.int32)[None, :]
    first_occ = jnp.sum(
        jnp.where((pair_index // second_count)[:, None] == occ_ids, eps_occ[None, :], 0.0), 1
    )
    second_occ = jnp.sum(
        jnp.where((pair_index % second_count)[:, None] == occ_ids, eps_occ[None, :], 0.0), 1
    )
    slab_energy = lax.dynamic_slice_in_dim(eps_vir, vir * slab, slab, 0)
    denominator = (eps_vir[0] + slab_energy)[:, None] - first_occ[None, :] - second_occ[None, :]
    update = residual.astype(f32) / denominator
    return residual, update


def solution(mesh):
    placed = (
        P(("ph", "vec"), "vir", None),
        P(None, "vir", None),
        P(("vir", "ph"), None, "vec"),
        P(("vir", "ph"), None, "vec"),
        P(("vir", "ph")),
        P(("vir", "ph")),
        P(("ph", "vec"), None, "vir"),
        P(),
        P(),
    )
    return jax.shard_map(
        local,
        mesh=mesh,
        in_specs=placed,
        out_specs=(P("vir", ("ph", "vec")), P("vir", ("ph", "vec"))),
        check_vma=False,
    )
```

```python
import functools

import jax
import jax.numpy as jnp
from jax import lax
from jax.experimental import pallas as pl
from jax.experimental.pallas import tpu as pltpu
from jax.sharding import PartitionSpec as P

LANES = 128
bf16, f32 = jnp.bfloat16, jnp.float32


def plain(
    vv_factor, ladder_amp, cycle_amp, ov_slots, owner_of, slot_of, ov_pairs, eps_vir, eps_occ
):
    chol_local, slab_width, virtuals = vv_factor.shape
    pair_count = ladder_amp.shape[2]
    row_piece = vv_factor[:, :, 0]
    factor_row = lax.all_gather(row_piece, "vir", axis=1, tiled=True)
    half = jnp.dot(
        factor_row,
        ladder_amp.reshape(virtuals, slab_width * pair_count),
        preferred_element_type=jnp.float32,
    )
    half = half.astype(jnp.bfloat16).reshape(chol_local * slab_width, pair_count)
    flat_factor = vv_factor.reshape(chol_local * slab_width, virtuals)
    block_local, occ_rows, block_part = cycle_amp.shape
    owner_total = lax.axis_size("ph")
    targets = owner_of[None, :] == jnp.arange(owner_total, dtype=jnp.int32)[:, None]
    outgoing = jnp.where(targets[:, :, None, None], cycle_amp[None], jnp.zeros((), jnp.bfloat16))
    places = jnp.where(targets, slot_of[None, :], 0)
    arrived, arrived_slots = (
        lax.all_to_all(outgoing, "ph", split_axis=0, concat_axis=0, tiled=True),
        lax.all_to_all(places, "ph", split_axis=0, concat_axis=0, tiled=True),
    )
    capacity = ov_slots.shape[0]
    picks = (
        arrived_slots.reshape(-1)[:, None] == jnp.arange(capacity, dtype=jnp.int32)[None, :]
    ).astype(jnp.bfloat16)
    arranged = jnp.einsum(
        "ns,niw->siw",
        picks,
        arrived.reshape(-1, occ_rows, block_part),
        preferred_element_type=jnp.float32,
    )
    arranged = arranged.astype(jnp.bfloat16)
    cycle_part = jnp.einsum("siw,spw->ip", arranged, ov_slots, preferred_element_type=jnp.float32)
    near_groups = lax.axis_size("ph") * lax.axis_size("vec")
    summed = lax.psum(cycle_part, ("vir", "ph", "vec"))
    vector_share = summed.shape[1] // near_groups
    own_share = lax.dynamic_slice_in_dim(
        summed, lax.axis_index(("ph", "vec")) * vector_share, vector_share, 1
    )
    coupling = own_share.astype(jnp.bfloat16)
    second_count = ov_pairs.shape[1]
    cycle_term = jnp.einsum("ip,pjb->bij", coupling, ov_pairs, preferred_element_type=jnp.float32)
    cycle_term = cycle_term.reshape(slab_width, occ_rows * second_count)
    slab_start = lax.axis_index("vir") * slab_width
    slab = (
        lax.psum_scatter(
            lax.dot_general(
                flat_factor, half, (((0,), (0,)), ((), ())), preferred_element_type=jnp.float32
            ),
            "vir",
            scatter_dimension=0,
            tiled=True,
        )
        + cycle_term
    )
    result = lax.psum_scatter(slab, ("ph", "vec"), scatter_dimension=1, tiled=True)
    residual = result.astype(jnp.bfloat16)
    share_width = result.shape[1]
    pair_index = lax.axis_index(("ph", "vec")) * share_width + jnp.arange(
        share_width, dtype=jnp.int32
    )
    occ_count = eps_occ.shape[0]
    occ_ids = jnp.arange(occ_count, dtype=jnp.int32)[None, :]
    first_occ = jnp.sum(
        jnp.where((pair_index // second_count)[:, None] == occ_ids, eps_occ[None, :], 0.0), 1
    )
    second_occ = jnp.sum(
        jnp.where((pair_index % second_count)[:, None] == occ_ids, eps_occ[None, :], 0.0), 1
    )
    slab_energy = lax.dynamic_slice_in_dim(eps_vir, slab_start, slab_width, 0)
    denominator = (eps_vir[0] + slab_energy)[:, None] - first_occ[None, :] - second_occ[None, :]
    update = residual.astype(jnp.float32) / denominator
    return (residual, update)


def shifted(x, axes, k):
    n = lax.axis_size(axes)
    return lax.ppermute(x, axes, [(i, (i + k) % n) for i in range(n)])


def round_robin(x, axes):
    return [x] + [shifted(x, axes, k) for k in range(1, lax.axis_size(axes))]


def row_kernel(*refs):
    (*x_refs, out_ref, acc) = refs
    step, rows = pl.program_id(1), x_refs[0].shape[0]
    lane = lax.broadcasted_iota(jnp.int32, acc.shape, 1)

    @pl.when(step == 0)
    def _():
        acc[...] = jnp.zeros_like(acc)

    part = jnp.zeros(acc.shape, f32)
    for q, ref in enumerate(x_refs):
        for p in range(rows):
            shift = q * rows + p
            column = ref[p].astype(f32)
            part = jnp.where(lane == shift, pltpu.roll(column, shift, 1) if shift else column, part)
    rows = rows * len(x_refs)
    part = pltpu.roll(part, step * rows, 1)
    acc[...] = jnp.where(lane // rows == step, part, acc[...])

    @pl.when(step == pl.num_programs(1) - 1)
    def _():
        piece = acc[...].T.astype(bf16)
        for k in range(out_ref.shape[0]):
            out_ref[k] = piece


def own_row(vv_factor, copies):
    chol, slab, _ = vv_factor.shape
    rows, sides = 16, 4
    steps = LANES // (rows * sides)

    def side(q):
        return pl.BlockSpec((rows, slab, LANES), lambda g, k: ((g * steps + k) * sides + q, 0, 0))

    return pl.pallas_call(
        row_kernel,
        grid=(chol // LANES, steps),
        in_specs=[side(q) for q in range(sides)],
        out_specs=pl.BlockSpec((copies, LANES, slab), lambda g, k: (0, g, 0)),
        out_shape=jax.ShapeDtypeStruct((copies, chol, slab), bf16),
        scratch_shapes=[pltpu.VMEM((slab, LANES), f32)],
        compiler_params=pltpu.CompilerParams(vmem_limit_bytes=32 << 20),
        cost_estimate=pl.CostEstimate(
            flops=2 * chol * slab * LANES, bytes_accessed=2 * chol * slab * LANES, transcendentals=0
        ),
    )(*[vv_factor] * sides)


def cycle_kernel(shares, groups, place_ref, code_ref, *refs):
    (*amp_refs, out_ref, amps, acc, block_of) = refs
    amp_refs, ov_refs = amp_refs[:groups], amp_refs[groups:]
    step = pl.program_id(0)
    blocks, slots = code_ref.shape[0], block_of.shape[0]
    own, width = 2 * amp_refs[0].shape[0], amps.shape[2]

    @pl.when(step == 0)
    def _():
        for k, ref in enumerate(amp_refs):
            for h in range(2):
                amps[pl.ds(k * own + h * (own // 2), own // 2)] = ref[
                    :, :, h * width : (h + 1) * width
                ]
        amps[blocks] = jnp.zeros(amps.shape[1:], bf16)
        acc[...] = jnp.zeros_like(acc)
        first = place_ref[0] * slots

        @pl.loop(0, slots, unroll=16)
        def _(s):
            block_of[s] = blocks

        @pl.loop(0, blocks, unroll=8)
        def _(n):
            slot = code_ref[n] - first

            @pl.when((slot >= 0) & (slot < slots))
            def _():
                block_of[slot] = n

    here, _, chol = ov_refs[0].shape
    start, count = step * len(ov_refs) * here, len(ov_refs) * here
    left = jnp.concatenate([amps[block_of[start + s]] for s in range(count)], axis=1)
    right = jnp.concatenate([ref[...].reshape(here * width, chol) for ref in ov_refs], axis=0)
    acc[...] += jnp.dot(left, right, preferred_element_type=f32)

    @pl.when(step == pl.num_programs(0) - 1)
    def _():
        share = chol // shares
        for k in range(out_ref.shape[0]):
            start = k % shares * share
            out_ref[k] = acc[:, start : start + share]


def cycle_operands(cycle_amp, owner_of, slot_of, slots):
    codes = jnp.concatenate(round_robin(owner_of * slots + slot_of, "ph"))
    near, far = jnp.split(cycle_amp, 2, 0)
    return round_robin(jnp.concatenate([near, far], 2), "ph"), codes


def cycle_partial(amps, codes, ov_slots):
    slots, chol, width = ov_slots.shape
    occ = amps[0].shape[1]
    shares = lax.axis_size(("ph", "vec"))
    copies = shares * lax.axis_size("vir")
    place = lax.axis_index("ph").astype(jnp.int32)[None]
    here, sides = 8, 4

    def side(q):
        return pl.BlockSpec((here, width, chol), lambda i: (i * sides + q, 0, 0))

    whole = pl.BlockSpec(memory_space=pltpu.VMEM)
    scalars = pl.BlockSpec(memory_space=pltpu.SMEM)
    return pl.pallas_call(
        functools.partial(cycle_kernel, shares, len(amps)),
        grid=(slots // (here * sides),),
        in_specs=[scalars, scalars]
        + [whole] * len(amps)
        + [side(q) for q in range(sides)],
        out_specs=pl.BlockSpec((copies, occ, chol // shares), lambda i: (0, 0, 0)),
        out_shape=jax.ShapeDtypeStruct((copies, occ, chol // shares), f32),
        scratch_shapes=[
            pltpu.VMEM((codes.shape[0] + 1, occ, width), bf16),
            pltpu.VMEM((occ, chol), f32),
            pltpu.SMEM((slots,), jnp.int32),
        ],
        compiler_params=pltpu.CompilerParams(vmem_limit_bytes=60 << 20),
        cost_estimate=pl.CostEstimate(
            flops=2 * occ * slots * width * chol,
            bytes_accessed=2 * slots * width * chol,
            transcendentals=0,
        ),
    )(place, codes, *amps, *[jnp.swapaxes(ov_slots, 1, 2)] * sides)


def swap_matrix(deep):
    n = deep * deep
    r = lax.broadcasted_iota(jnp.int32, (n, n), 0)
    s = lax.broadcasted_iota(jnp.int32, (n, n), 1)
    return (lax.rem(r, deep) * deep + lax.div(r, deep) == s).astype(bf16)


def ladder_kernel(sides, row_ref, amp_hbm, factor_hbm, out_ref, *scratch):
    (amp_buf, factor_buf, amp_sem, factor_sem, swap, turned, half, flat) = scratch
    _, virtuals, deep, pairs = amp_buf.shape
    count, chol, _ = row_ref.shape
    square = deep * deep
    step, steps = pl.program_id(0), pl.num_programs(0)
    slot = lax.rem(step, 2)

    def arriving(hbm, buf, sem, step, side):
        size = buf.shape[1] // sides
        rows, slot = pl.ds(side * size, size), lax.rem(step, 2)
        block = pl.ds(pl.multiple_of(step * deep, deep), deep)
        return pltpu.make_async_copy(
            hbm.at[rows, block], buf.at[slot, rows], sem.at[slot, side]
        )

    def start(step):
        for q in range(sides):
            arriving(amp_hbm, amp_buf, amp_sem, step, q).start()
        for q in range(sides):
            arriving(factor_hbm, factor_buf, factor_sem, step, q).start()

    @pl.when(step == 0)
    def _():
        start(step)
        out_ref[...] = jnp.zeros_like(out_ref)
        swap[...] = swap_matrix(deep)

    @pl.when(step + 1 < steps)
    def _():
        start(step + 1)

    def later(jobs):
        store = None
        for job in jobs:
            after = job()
            if store is not None:
                store()
            store = after
        store()

    def reorder(first):
        rows = [slice(first + r * deep, first + (r + 1) * deep) for r in range(4)]
        block = [amp_buf[slot, r].reshape(square, pairs) for r in rows]
        block = jnp.dot(
            swap[...], jnp.concatenate(block, axis=1), preferred_element_type=f32
        ).astype(bf16)

        def store():
            for i, r in enumerate(rows):
                turned[:, r, :] = block[:, i * pairs : (i + 1) * pairs].reshape(deep, deep, pairs)

        return store

    for q in range(sides):
        arriving(amp_hbm, amp_buf, amp_sem, step, q).wait()
        size = virtuals // sides
        later(
            functools.partial(reorder, k) for k in range(q * size, (q + 1) * size, 4 * deep)
        )

    row = jnp.concatenate([row_ref[k] for k in range(count)], axis=1)

    def halves(d):
        block = jnp.concatenate([turned[d + r] for r in range(4)], axis=1)
        block = jnp.dot(row, block, preferred_element_type=f32).astype(bf16)

        def store():
            for r in range(4):
                half[d + r] = block[:, r * pairs : (r + 1) * pairs]

        return store

    later(functools.partial(halves, d) for d in range(0, deep, 4))

    def flatten(first):
        parts = range(first, first + chol, deep)
        block = [half[:, k : k + deep, :].reshape(square, pairs).T for k in parts]
        block = jnp.dot(
            jnp.concatenate(block, axis=0), swap[...], preferred_element_type=f32
        ).astype(bf16)

        def store():
            for i, k in enumerate(parts):
                flat[:, k * deep : (k + deep) * deep] = block[i * pairs : (i + 1) * pairs]

        return store

    flatten(0)()
    for q in range(sides):
        arriving(factor_hbm, factor_buf, factor_sem, step, q).wait()
    columns = out_ref.shape[1]

    def ladder(first):
        block = factor_buf[slot, :, :, first : first + columns].reshape(chol * deep, columns)
        block = jnp.dot(flat[...], block, preferred_element_type=f32)

        def store():
            out_ref[:, first : first + columns] += block

        return store

    later(functools.partial(ladder, n) for n in range(0, out_ref.shape[1], columns))


def ladder_partial(row, ladder_amp, vv_factor):
    virtuals, slab, pairs = ladder_amp.shape
    chol = vv_factor.shape[0]
    deep, sides = 16, 4
    whole = pl.BlockSpec(memory_space=pl.ANY)
    return pl.pallas_call(
        functools.partial(ladder_kernel, sides),
        grid=(slab // deep,),
        in_specs=[pl.BlockSpec(memory_space=pltpu.VMEM), whole, whole],
        out_specs=pl.BlockSpec((pairs, virtuals), lambda i: (0, 0)),
        out_shape=jax.ShapeDtypeStruct((pairs, virtuals), f32),
        scratch_shapes=[
            pltpu.VMEM((2, virtuals, deep, pairs), bf16),
            pltpu.VMEM((2, chol, deep, virtuals), bf16),
            pltpu.SemaphoreType.DMA((2, sides)),
            pltpu.SemaphoreType.DMA((2, sides)),
            pltpu.VMEM((deep * deep, deep * deep), bf16),
            pltpu.VMEM((deep, virtuals, pairs), bf16),
            pltpu.VMEM((deep, chol, pairs), bf16),
            pltpu.VMEM((pairs, chol * deep), bf16),
        ],
        compiler_params=pltpu.CompilerParams(vmem_limit_bytes=60 << 20),
        cost_estimate=pl.CostEstimate(
            flops=4 * chol * virtuals * slab * pairs,
            bytes_accessed=2 * virtuals * slab * (pairs + chol),
            transcendentals=0,
        ),
    )(row, ladder_amp, vv_factor)


def scatter_sum(x, axes, near=None):
    total_places = lax.axis_size(axes)
    me = lax.axis_index(axes)
    n = x.shape[0]

    def moved(place, k):
        if near is None:
            return (place + k) % n
        if near > 0:
            return place // near * near + (place % near + k) % near
        return (place + k * -near) % total_places

    def rank(place):
        return place if near is None else place % near if near > 0 else place // -near

    total = lax.dynamic_index_in_dim(x, rank(me), 0, keepdims=False)
    sent = x.astype(bf16)
    for k in range(1, n):
        piece = lax.dynamic_index_in_dim(sent, rank(moved(me, k)), 0, keepdims=False)
        pairs = [(i, moved(i, k)) for i in range(total_places)]
        total = total + lax.ppermute(piece, axes, pairs).astype(f32)
    return total


def local(
    vv_factor, ladder_amp, cycle_amp, ov_slots, owner_of, slot_of, ov_pairs, eps_vir, eps_occ
):
    chol, slab, virtuals = vv_factor.shape
    pairs = ladder_amp.shape[2]
    slots, _, width = ov_slots.shape
    n_vir, n_ph, n_vec = (lax.axis_size(a) for a in ("vir", "ph", "vec"))
    fits = slab == LANES and virtuals % 512 == 0 and pairs == 2 * LANES and chol % LANES == 0 and slots % 32 == 0
    if not fits or 256 % width or cycle_amp.shape[0] % 2 or n_vir * n_ph % 4:
        return plain(
            vv_factor, ladder_amp, cycle_amp, ov_slots, owner_of, slot_of, ov_pairs, eps_vir, eps_occ
        )
    amps, codes = cycle_operands(cycle_amp, owner_of, slot_of, slots)
    row, amps, codes = lax.optimization_barrier((own_row(vv_factor, n_vir), amps, codes))
    row = lax.all_to_all(row, "vir", 0, 0)
    pieces = lax.all_to_all(cycle_partial(amps, codes, ov_slots), ("vir", "ph", "vec"), 0, 0)
    coupling = jnp.sum(pieces, 0).astype(bf16)
    second_count = ov_pairs.shape[1]
    cycle_term = jnp.einsum("ip,pjb->ijb", coupling, ov_pairs, preferred_element_type=f32)
    cycle_term = cycle_term.reshape(pairs, slab)

    ladder = ladder_partial(row, ladder_amp, vv_factor)
    vir = lax.axis_index("vir")
    share = pairs // (n_ph * n_vec)
    own = jnp.arange(n_vir, dtype=jnp.int32)[:, None] == vir
    total = ladder.reshape(n_ph, n_vec, share, virtuals)
    total = scatter_sum(jnp.swapaxes(total, 0, 1), "vec")
    cycle_term = cycle_term.reshape(n_ph, n_vec, share, slab)
    cycle_term = scatter_sum(jnp.swapaxes(cycle_term, 0, 1), "vec")
    total = total.reshape(n_ph, share, n_vir, slab)
    total = total + jnp.where(own, cycle_term[:, :, None, :], 0.0)
    total = total.transpose(2, 0, 1, 3)
    total = total.reshape(n_vir * n_ph // 4, 4, share, slab).transpose(1, 0, 2, 3)
    total = scatter_sum(scatter_sum(total, ("vir", "ph"), 4), ("vir", "ph"), -4)

    residual = total.T.astype(bf16)
    place = lax.axis_index(("ph", "vec"))
    pair_index = place * share + jnp.arange(share, dtype=jnp.int32)
    occ_ids = jnp.arange(eps_occ.shape[0], dtype=jnp.int32)[None, :]
    first_occ = jnp.sum(
        jnp.where((pair_index // second_count)[:, None] == occ_ids, eps_occ[None, :], 0.0), 1
    )
    second_occ = jnp.sum(
        jnp.where((pair_index % second_count)[:, None] == occ_ids, eps_occ[None, :], 0.0), 1
    )
    slab_energy = lax.dynamic_slice_in_dim(eps_vir, vir * slab, slab, 0)
    denominator = (eps_vir[0] + slab_energy)[:, None] - first_occ[None, :] - second_occ[None, :]
    update = residual.astype(f32) / denominator
    return residual, update


def solution(mesh):
    placed = (
        P(("ph", "vec"), "vir", None),
        P(None, "vir", None),
        P(("vir", "ph"), None, "vec"),
        P(("vir", "ph"), None, "vec"),
        P(("vir", "ph")),
        P(("vir", "ph")),
        P(("ph", "vec"), None, "vir"),
        P(),
        P(),
    )
    return jax.shard_map(
        local,
        mesh=mesh,
        in_specs=placed,
        out_specs=(P("vir", ("ph", "vec")), P("vir", ("ph", "vec"))),
        check_vma=False,
    )
```

```python
import functools

import jax
import jax.numpy as jnp
from jax import lax
from jax.experimental import pallas as pl
from jax.experimental.pallas import tpu as pltpu
from jax.sharding import PartitionSpec as P

LANES = 128
bf16, f32 = jnp.bfloat16, jnp.float32


def plain(
    vv_factor, ladder_amp, cycle_amp, ov_slots, owner_of, slot_of, ov_pairs, eps_vir, eps_occ
):
    chol_local, slab_width, virtuals = vv_factor.shape
    pair_count = ladder_amp.shape[2]
    row_piece = vv_factor[:, :, 0]
    factor_row = lax.all_gather(row_piece, "vir", axis=1, tiled=True)
    half = jnp.dot(
        factor_row,
        ladder_amp.reshape(virtuals, slab_width * pair_count),
        preferred_element_type=jnp.float32,
    )
    half = half.astype(jnp.bfloat16).reshape(chol_local * slab_width, pair_count)
    flat_factor = vv_factor.reshape(chol_local * slab_width, virtuals)
    block_local, occ_rows, block_part = cycle_amp.shape
    owner_total = lax.axis_size("ph")
    targets = owner_of[None, :] == jnp.arange(owner_total, dtype=jnp.int32)[:, None]
    outgoing = jnp.where(targets[:, :, None, None], cycle_amp[None], jnp.zeros((), jnp.bfloat16))
    places = jnp.where(targets, slot_of[None, :], 0)
    arrived, arrived_slots = (
        lax.all_to_all(outgoing, "ph", split_axis=0, concat_axis=0, tiled=True),
        lax.all_to_all(places, "ph", split_axis=0, concat_axis=0, tiled=True),
    )
    capacity = ov_slots.shape[0]
    picks = (
        arrived_slots.reshape(-1)[:, None] == jnp.arange(capacity, dtype=jnp.int32)[None, :]
    ).astype(jnp.bfloat16)
    arranged = jnp.einsum(
        "ns,niw->siw",
        picks,
        arrived.reshape(-1, occ_rows, block_part),
        preferred_element_type=jnp.float32,
    )
    arranged = arranged.astype(jnp.bfloat16)
    cycle_part = jnp.einsum("siw,spw->ip", arranged, ov_slots, preferred_element_type=jnp.float32)
    near_groups = lax.axis_size("ph") * lax.axis_size("vec")
    summed = lax.psum(cycle_part, ("vir", "ph", "vec"))
    vector_share = summed.shape[1] // near_groups
    own_share = lax.dynamic_slice_in_dim(
        summed, lax.axis_index(("ph", "vec")) * vector_share, vector_share, 1
    )
    coupling = own_share.astype(jnp.bfloat16)
    second_count = ov_pairs.shape[1]
    cycle_term = jnp.einsum("ip,pjb->bij", coupling, ov_pairs, preferred_element_type=jnp.float32)
    cycle_term = cycle_term.reshape(slab_width, occ_rows * second_count)
    slab_start = lax.axis_index("vir") * slab_width
    slab = (
        lax.psum_scatter(
            lax.dot_general(
                flat_factor, half, (((0,), (0,)), ((), ())), preferred_element_type=jnp.float32
            ),
            "vir",
            scatter_dimension=0,
            tiled=True,
        )
        + cycle_term
    )
    result = lax.psum_scatter(slab, ("ph", "vec"), scatter_dimension=1, tiled=True)
    residual = result.astype(jnp.bfloat16)
    share_width = result.shape[1]
    pair_index = lax.axis_index(("ph", "vec")) * share_width + jnp.arange(
        share_width, dtype=jnp.int32
    )
    occ_count = eps_occ.shape[0]
    occ_ids = jnp.arange(occ_count, dtype=jnp.int32)[None, :]
    first_occ = jnp.sum(
        jnp.where((pair_index // second_count)[:, None] == occ_ids, eps_occ[None, :], 0.0), 1
    )
    second_occ = jnp.sum(
        jnp.where((pair_index % second_count)[:, None] == occ_ids, eps_occ[None, :], 0.0), 1
    )
    slab_energy = lax.dynamic_slice_in_dim(eps_vir, slab_start, slab_width, 0)
    denominator = (eps_vir[0] + slab_energy)[:, None] - first_occ[None, :] - second_occ[None, :]
    update = residual.astype(jnp.float32) / denominator
    return (residual, update)


def shifted(x, axes, k):
    n = lax.axis_size(axes)
    return lax.ppermute(x, axes, [(i, (i + k) % n) for i in range(n)])


def round_robin(x, axes):
    return [x] + [shifted(x, axes, k) for k in range(1, lax.axis_size(axes))]


def row_kernel(*refs):
    (*x_refs, out_ref, acc) = refs
    step, rows = pl.program_id(1), x_refs[0].shape[0]
    lane = lax.broadcasted_iota(jnp.int32, acc.shape, 1)

    @pl.when(step == 0)
    def _():
        acc[...] = jnp.zeros_like(acc)

    part = jnp.zeros(acc.shape, f32)
    for q, ref in enumerate(x_refs):
        for p in range(rows):
            shift = q * rows + p
            column = ref[p].astype(f32)
            part = jnp.where(lane == shift, pltpu.roll(column, shift, 1) if shift else column, part)
    rows = rows * len(x_refs)
    part = pltpu.roll(part, step * rows, 1)
    acc[...] = jnp.where(lane // rows == step, part, acc[...])

    @pl.when(step == pl.num_programs(1) - 1)
    def _():
        piece = acc[...].T.astype(bf16)
        for k in range(out_ref.shape[0]):
            out_ref[k] = piece


def own_row(vv_factor, copies):
    chol, slab, _ = vv_factor.shape
    rows, sides = 16, 4
    steps = LANES // (rows * sides)

    def side(q):
        return pl.BlockSpec((rows, slab, LANES), lambda g, k: ((g * steps + k) * sides + q, 0, 0))

    return pl.pallas_call(
        row_kernel,
        grid=(chol // LANES, steps),
        in_specs=[side(q) for q in range(sides)],
        out_specs=pl.BlockSpec((copies, LANES, slab), lambda g, k: (0, g, 0)),
        out_shape=jax.ShapeDtypeStruct((copies, chol, slab), bf16),
        scratch_shapes=[pltpu.VMEM((slab, LANES), f32)],
        compiler_params=pltpu.CompilerParams(vmem_limit_bytes=32 << 20),
        cost_estimate=pl.CostEstimate(
            flops=2 * chol * slab * LANES, bytes_accessed=2 * chol * slab * LANES, transcendentals=0
        ),
    )(*[vv_factor] * sides)


def cycle_kernel(shares, groups, place_ref, *refs):
    (*in_refs, out_ref, amps, acc, block_of) = refs
    code_refs, amp_refs = in_refs[:groups], in_refs[groups : 2 * groups]
    ov_refs = in_refs[2 * groups :]
    step = pl.program_id(0)
    blocks, slots = groups * code_refs[0].shape[0], block_of.shape[0]
    own, width = 2 * amp_refs[0].shape[0], amps.shape[2]

    @pl.when(step == 0)
    def _():
        for k, ref in enumerate(amp_refs):
            for h in range(2):
                amps[pl.ds(k * own + h * (own // 2), own // 2)] = ref[
                    :, :, h * width : (h + 1) * width
                ]
        amps[blocks] = jnp.zeros(amps.shape[1:], bf16)
        acc[...] = jnp.zeros_like(acc)
        first = place_ref[0] * slots

        @pl.loop(0, slots, unroll=16)
        def _(s):
            block_of[s] = blocks

        for k, ref in enumerate(code_refs):

            @pl.loop(0, ref.shape[0], unroll=8)
            def _(n):
                slot = ref[n] - first

                @pl.when((slot >= 0) & (slot < slots))
                def _():
                    block_of[slot] = k * ref.shape[0] + n

    here, _, chol = ov_refs[0].shape
    start, count = step * len(ov_refs) * here, len(ov_refs) * here
    left = jnp.concatenate([amps[block_of[start + s]] for s in range(count)], axis=1)
    right = jnp.concatenate([ref[...].reshape(here * width, chol) for ref in ov_refs], axis=0)
    acc[...] += jnp.dot(left, right, preferred_element_type=f32)

    @pl.when(step == pl.num_programs(0) - 1)
    def _():
        share = chol // shares
        for k in range(out_ref.shape[0]):
            start = k % shares * share
            out_ref[k] = acc[:, start : start + share]


def cycle_operands(cycle_amp, owner_of, slot_of, slots):
    codes = round_robin(owner_of * slots + slot_of, "ph")
    near, far = jnp.split(cycle_amp, 2, 0)
    return round_robin(jnp.concatenate([near, far], 2), "ph"), codes


def cycle_partial(amps, codes, ov_slots):
    slots, chol, width = ov_slots.shape
    occ = amps[0].shape[1]
    shares = lax.axis_size(("ph", "vec"))
    copies = shares * lax.axis_size("vir")
    place = lax.axis_index("ph").astype(jnp.int32)[None]
    here, sides = 8, 4

    def side(q):
        return pl.BlockSpec((here, width, chol), lambda i: (i * sides + q, 0, 0))

    whole = pl.BlockSpec(memory_space=pltpu.VMEM)
    scalars = pl.BlockSpec(memory_space=pltpu.SMEM)
    return pl.pallas_call(
        functools.partial(cycle_kernel, shares, len(amps)),
        grid=(slots // (here * sides),),
        in_specs=[scalars] * (1 + len(codes))
        + [whole] * len(amps)
        + [side(q) for q in range(sides)],
        out_specs=pl.BlockSpec((copies, occ, chol // shares), lambda i: (0, 0, 0)),
        out_shape=jax.ShapeDtypeStruct((copies, occ, chol // shares), f32),
        scratch_shapes=[
            pltpu.VMEM((len(codes) * codes[0].shape[0] + 1, occ, width), bf16),
            pltpu.VMEM((occ, chol), f32),
            pltpu.SMEM((slots,), jnp.int32),
        ],
        compiler_params=pltpu.CompilerParams(vmem_limit_bytes=60 << 20),
        cost_estimate=pl.CostEstimate(
            flops=2 * occ * slots * width * chol,
            bytes_accessed=2 * slots * width * chol,
            transcendentals=0,
        ),
    )(place, *codes, *amps, *[jnp.swapaxes(ov_slots, 1, 2)] * sides)


def swap_matrix(deep):
    n = deep * deep
    r = lax.broadcasted_iota(jnp.int32, (n, n), 0)
    s = lax.broadcasted_iota(jnp.int32, (n, n), 1)
    return (lax.rem(r, deep) * deep + lax.div(r, deep) == s).astype(bf16)


def ladder_kernel(sides, row_ref, amp_hbm, factor_hbm, out_ref, *scratch):
    (amp_buf, factor_buf, amp_sem, factor_sem, swap, turned, half, flat) = scratch
    _, virtuals, deep, pairs = amp_buf.shape
    count, chol, _ = row_ref.shape
    square = deep * deep
    step, steps = pl.program_id(0), pl.num_programs(0)
    slot = lax.rem(step, 2)

    def arriving(hbm, buf, sem, step, side):
        size = buf.shape[1] // sides
        rows, slot = pl.ds(side * size, size), lax.rem(step, 2)
        block = pl.ds(pl.multiple_of(step * deep, deep), deep)
        return pltpu.make_async_copy(
            hbm.at[rows, block], buf.at[slot, rows], sem.at[slot, side]
        )

    def start(hbm, buf, sem, step):
        for q in range(sides):
            arriving(hbm, buf, sem, step, q).start()

    @pl.when(step == 0)
    def _():
        start(amp_hbm, amp_buf, amp_sem, step)
        out_ref[...] = jnp.zeros_like(out_ref)
        swap[...] = swap_matrix(deep)

    @pl.when((step > 0) & (step + 1 < steps))
    def _():
        start(amp_hbm, amp_buf, amp_sem, step + 1)
        start(factor_hbm, factor_buf, factor_sem, step + 1)

    def later(jobs):
        store = None
        for job in jobs:
            after = job()
            if store is not None:
                store()
            store = after
        store()

    def reorder(first):
        rows = [slice(first + r * deep, first + (r + 1) * deep) for r in range(2)]
        block = [amp_buf[slot, r].reshape(square, pairs) for r in rows]
        block = jnp.dot(
            swap[...], jnp.concatenate(block, axis=1), preferred_element_type=f32
        ).astype(bf16)

        def store():
            for i, r in enumerate(rows):
                turned[:, r, :] = block[:, i * pairs : (i + 1) * pairs].reshape(deep, deep, pairs)

        return store

    for q in range(sides):
        arriving(amp_hbm, amp_buf, amp_sem, step, q).wait()
        size = virtuals // sides
        later(
            functools.partial(reorder, k) for k in range(q * size, (q + 1) * size, 2 * deep)
        )

    @pl.when(step == 0)
    def _():
        start(factor_hbm, factor_buf, factor_sem, step)

    @pl.when((step == 0) & (steps > 1))
    def _():
        start(amp_hbm, amp_buf, amp_sem, step + 1)
        start(factor_hbm, factor_buf, factor_sem, step + 1)

    row = jnp.concatenate([row_ref[k] for k in range(count)], axis=1)

    def halves(d):
        block = jnp.concatenate([turned[d], turned[d + 1]], axis=1)
        block = jnp.dot(row, block, preferred_element_type=f32).astype(bf16)

        def store():
            half[d], half[d + 1] = block[:, :pairs], block[:, pairs:]

        return store

    later(functools.partial(halves, d) for d in range(0, deep, 2))

    def flatten(first):
        parts = range(first, first + 4 * deep, deep)
        block = [half[:, k : k + deep, :].reshape(square, pairs).T for k in parts]
        block = jnp.dot(
            jnp.concatenate(block, axis=0), swap[...], preferred_element_type=f32
        ).astype(bf16)

        def store():
            for i, k in enumerate(parts):
                flat[:, k * deep : (k + deep) * deep] = block[i * pairs : (i + 1) * pairs]

        return store

    later(functools.partial(flatten, k) for k in range(0, chol, 4 * deep))
    for q in range(sides):
        arriving(factor_hbm, factor_buf, factor_sem, step, q).wait()
    columns = 512

    def ladder(first):
        block = factor_buf[slot, :, :, first : first + columns].reshape(chol * deep, columns)
        block = jnp.dot(flat[...], block, preferred_element_type=f32)

        def store():
            out_ref[:, first : first + columns] += block

        return store

    later(functools.partial(ladder, n) for n in range(0, out_ref.shape[1], columns))


def ladder_partial(row, ladder_amp, vv_factor):
    virtuals, slab, pairs = ladder_amp.shape
    chol = vv_factor.shape[0]
    deep, sides = 16, 4
    whole = pl.BlockSpec(memory_space=pl.ANY)
    return pl.pallas_call(
        functools.partial(ladder_kernel, sides),
        grid=(slab // deep,),
        in_specs=[pl.BlockSpec(memory_space=pltpu.VMEM), whole, whole],
        out_specs=pl.BlockSpec((pairs, virtuals), lambda i: (0, 0)),
        out_shape=jax.ShapeDtypeStruct((pairs, virtuals), f32),
        scratch_shapes=[
            pltpu.VMEM((2, virtuals, deep, pairs), bf16),
            pltpu.VMEM((2, chol, deep, virtuals), bf16),
            pltpu.SemaphoreType.DMA((2, sides)),
            pltpu.SemaphoreType.DMA((2, sides)),
            pltpu.VMEM((deep * deep, deep * deep), bf16),
            pltpu.VMEM((deep, virtuals, pairs), bf16),
            pltpu.VMEM((deep, chol, pairs), bf16),
            pltpu.VMEM((pairs, chol * deep), bf16),
        ],
        compiler_params=pltpu.CompilerParams(vmem_limit_bytes=60 << 20),
        cost_estimate=pl.CostEstimate(
            flops=4 * chol * virtuals * slab * pairs,
            bytes_accessed=2 * virtuals * slab * (pairs + chol),
            transcendentals=0,
        ),
    )(row, ladder_amp, vv_factor)


def scatter_sum(x, axes, near=None):
    total_places = lax.axis_size(axes)
    me = lax.axis_index(axes)
    n = x.shape[0]

    def moved(place, k):
        if near is None:
            return (place + k) % n
        if near > 0:
            return place // near * near + (place % near + k) % near
        return (place + k * -near) % total_places

    def rank(place):
        return place if near is None else place % near if near > 0 else place // -near

    total = lax.dynamic_index_in_dim(x, rank(me), 0, keepdims=False)
    sent = x.astype(bf16)
    for k in range(1, n):
        piece = lax.dynamic_index_in_dim(sent, rank(moved(me, k)), 0, keepdims=False)
        pairs = [(i, moved(i, k)) for i in range(total_places)]
        total = total + lax.ppermute(piece, axes, pairs).astype(f32)
    return total


def local(
    vv_factor, ladder_amp, cycle_amp, ov_slots, owner_of, slot_of, ov_pairs, eps_vir, eps_occ
):
    chol, slab, virtuals = vv_factor.shape
    pairs = ladder_amp.shape[2]
    slots, _, width = ov_slots.shape
    n_vir, n_ph, n_vec = (lax.axis_size(a) for a in ("vir", "ph", "vec"))
    fits = slab == LANES and virtuals % 512 == 0 and pairs == 2 * LANES and chol % LANES == 0 and slots % 32 == 0
    if not fits or 256 % width or cycle_amp.shape[0] % 2 or n_vir * n_ph % 4:
        return plain(
            vv_factor, ladder_amp, cycle_amp, ov_slots, owner_of, slot_of, ov_pairs, eps_vir, eps_occ
        )
    amps, codes = cycle_operands(cycle_amp, owner_of, slot_of, slots)
    row, amps, codes = lax.optimization_barrier((own_row(vv_factor, n_vir), amps, codes))
    row = lax.all_to_all(row, "vir", 0, 0)
    pieces = lax.all_to_all(cycle_partial(amps, codes, ov_slots), ("vir", "ph", "vec"), 0, 0)
    coupling = jnp.sum(pieces, 0).astype(bf16)
    second_count = ov_pairs.shape[1]
    cycle_term = jnp.einsum("ip,pjb->ijb", coupling, ov_pairs, preferred_element_type=f32)
    cycle_term = cycle_term.reshape(pairs, slab)

    ladder = ladder_partial(row, ladder_amp, vv_factor)
    vir = lax.axis_index("vir")
    share = pairs // (n_ph * n_vec)
    own = jnp.arange(n_vir, dtype=jnp.int32)[None, :, None] == vir
    total = ladder.reshape(pairs, n_vir, slab) + jnp.where(own, cycle_term[:, None, :], 0.0)
    total = total.reshape(n_ph, n_vec, share, virtuals)
    total = scatter_sum(jnp.swapaxes(total, 0, 1), "vec")
    total = total.reshape(n_ph, share, n_vir, slab).transpose(2, 0, 1, 3)
    total = total.reshape(n_vir * n_ph // 4, 4, share, slab).transpose(1, 0, 2, 3)
    total = scatter_sum(scatter_sum(total, ("vir", "ph"), 4), ("vir", "ph"), -4)

    residual = total.T.astype(bf16)
    place = lax.axis_index(("ph", "vec"))
    pair_index = place * share + jnp.arange(share, dtype=jnp.int32)
    occ_ids = jnp.arange(eps_occ.shape[0], dtype=jnp.int32)[None, :]
    first_occ = jnp.sum(
        jnp.where((pair_index // second_count)[:, None] == occ_ids, eps_occ[None, :], 0.0), 1
    )
    second_occ = jnp.sum(
        jnp.where((pair_index % second_count)[:, None] == occ_ids, eps_occ[None, :], 0.0), 1
    )
    slab_energy = lax.dynamic_slice_in_dim(eps_vir, vir * slab, slab, 0)
    denominator = (eps_vir[0] + slab_energy)[:, None] - first_occ[None, :] - second_occ[None, :]
    update = residual.astype(f32) / denominator
    return residual, update


def solution(mesh):
    placed = (
        P(("ph", "vec"), "vir", None),
        P(None, "vir", None),
        P(("vir", "ph"), None, "vec"),
        P(("vir", "ph"), None, "vec"),
        P(("vir", "ph")),
        P(("vir", "ph")),
        P(("ph", "vec"), None, "vir"),
        P(),
        P(),
    )
    return jax.shard_map(
        local,
        mesh=mesh,
        in_specs=placed,
        out_specs=(P("vir", ("ph", "vec")), P("vir", ("ph", "vec"))),
        check_vma=False,
    )
```

```python
import functools

import jax
import jax.numpy as jnp
from jax import lax
from jax.experimental import pallas as pl
from jax.experimental.pallas import tpu as pltpu
from jax.sharding import PartitionSpec as P

LANES = 128
bf16, f32 = jnp.bfloat16, jnp.float32


def plain(
    vv_factor, ladder_amp, cycle_amp, ov_slots, owner_of, slot_of, ov_pairs, eps_vir, eps_occ
):
    chol_local, slab_width, virtuals = vv_factor.shape
    pair_count = ladder_amp.shape[2]
    row_piece = vv_factor[:, :, 0]
    factor_row = lax.all_gather(row_piece, "vir", axis=1, tiled=True)
    half = jnp.dot(
        factor_row,
        ladder_amp.reshape(virtuals, slab_width * pair_count),
        preferred_element_type=jnp.float32,
    )
    half = half.astype(jnp.bfloat16).reshape(chol_local * slab_width, pair_count)
    flat_factor = vv_factor.reshape(chol_local * slab_width, virtuals)
    block_local, occ_rows, block_part = cycle_amp.shape
    owner_total = lax.axis_size("ph")
    targets = owner_of[None, :] == jnp.arange(owner_total, dtype=jnp.int32)[:, None]
    outgoing = jnp.where(targets[:, :, None, None], cycle_amp[None], jnp.zeros((), jnp.bfloat16))
    places = jnp.where(targets, slot_of[None, :], 0)
    arrived, arrived_slots = (
        lax.all_to_all(outgoing, "ph", split_axis=0, concat_axis=0, tiled=True),
        lax.all_to_all(places, "ph", split_axis=0, concat_axis=0, tiled=True),
    )
    capacity = ov_slots.shape[0]
    picks = (
        arrived_slots.reshape(-1)[:, None] == jnp.arange(capacity, dtype=jnp.int32)[None, :]
    ).astype(jnp.bfloat16)
    arranged = jnp.einsum(
        "ns,niw->siw",
        picks,
        arrived.reshape(-1, occ_rows, block_part),
        preferred_element_type=jnp.float32,
    )
    arranged = arranged.astype(jnp.bfloat16)
    cycle_part = jnp.einsum("siw,spw->ip", arranged, ov_slots, preferred_element_type=jnp.float32)
    near_groups = lax.axis_size("ph") * lax.axis_size("vec")
    summed = lax.psum(cycle_part, ("vir", "ph", "vec"))
    vector_share = summed.shape[1] // near_groups
    own_share = lax.dynamic_slice_in_dim(
        summed, lax.axis_index(("ph", "vec")) * vector_share, vector_share, 1
    )
    coupling = own_share.astype(jnp.bfloat16)
    second_count = ov_pairs.shape[1]
    cycle_term = jnp.einsum("ip,pjb->bij", coupling, ov_pairs, preferred_element_type=jnp.float32)
    cycle_term = cycle_term.reshape(slab_width, occ_rows * second_count)
    slab_start = lax.axis_index("vir") * slab_width
    slab = (
        lax.psum_scatter(
            lax.dot_general(
                flat_factor, half, (((0,), (0,)), ((), ())), preferred_element_type=jnp.float32
            ),
            "vir",
            scatter_dimension=0,
            tiled=True,
        )
        + cycle_term
    )
    result = lax.psum_scatter(slab, ("ph", "vec"), scatter_dimension=1, tiled=True)
    residual = result.astype(jnp.bfloat16)
    share_width = result.shape[1]
    pair_index = lax.axis_index(("ph", "vec")) * share_width + jnp.arange(
        share_width, dtype=jnp.int32
    )
    occ_count = eps_occ.shape[0]
    occ_ids = jnp.arange(occ_count, dtype=jnp.int32)[None, :]
    first_occ = jnp.sum(
        jnp.where((pair_index // second_count)[:, None] == occ_ids, eps_occ[None, :], 0.0), 1
    )
    second_occ = jnp.sum(
        jnp.where((pair_index % second_count)[:, None] == occ_ids, eps_occ[None, :], 0.0), 1
    )
    slab_energy = lax.dynamic_slice_in_dim(eps_vir, slab_start, slab_width, 0)
    denominator = (eps_vir[0] + slab_energy)[:, None] - first_occ[None, :] - second_occ[None, :]
    update = residual.astype(jnp.float32) / denominator
    return (residual, update)


def shifted(x, axes, k):
    n = lax.axis_size(axes)
    return lax.ppermute(x, axes, [(i, (i + k) % n) for i in range(n)])


def round_robin(x, axes):
    return [x] + [shifted(x, axes, k) for k in range(1, lax.axis_size(axes))]


def row_kernel(*refs):
    (*x_refs, out_ref, acc) = refs
    step, rows = pl.program_id(1), x_refs[0].shape[0]
    lane = lax.broadcasted_iota(jnp.int32, acc.shape, 1)

    @pl.when(step == 0)
    def _():
        acc[...] = jnp.zeros_like(acc)

    part = jnp.zeros(acc.shape, f32)
    for q, ref in enumerate(x_refs):
        for p in range(rows):
            shift = q * rows + p
            column = ref[p].astype(f32)
            part = jnp.where(lane == shift, pltpu.roll(column, shift, 1) if shift else column, part)
    rows = rows * len(x_refs)
    part = pltpu.roll(part, step * rows, 1)
    acc[...] = jnp.where(lane // rows == step, part, acc[...])

    @pl.when(step == pl.num_programs(1) - 1)
    def _():
        piece = acc[...].T.astype(bf16)
        for k in range(out_ref.shape[0]):
            out_ref[k] = piece


def own_row(vv_factor, copies):
    chol, slab, _ = vv_factor.shape
    rows, sides = 16, 4
    steps = LANES // (rows * sides)

    def side(q):
        return pl.BlockSpec((rows, slab, LANES), lambda g, k: ((g * steps + k) * sides + q, 0, 0))

    return pl.pallas_call(
        row_kernel,
        grid=(chol // LANES, steps),
        in_specs=[side(q) for q in range(sides)],
        out_specs=pl.BlockSpec((copies, LANES, slab), lambda g, k: (0, g, 0)),
        out_shape=jax.ShapeDtypeStruct((copies, chol, slab), bf16),
        scratch_shapes=[pltpu.VMEM((slab, LANES), f32)],
        compiler_params=pltpu.CompilerParams(vmem_limit_bytes=32 << 20),
        cost_estimate=pl.CostEstimate(
            flops=2 * chol * slab * LANES, bytes_accessed=2 * chol * slab * LANES, transcendentals=0
        ),
    )(*[vv_factor] * sides)


def cycle_kernel(shares, groups, place_ref, *refs):
    (*in_refs, out_ref, amps, acc, block_of) = refs
    code_refs, amp_refs = in_refs[:groups], in_refs[groups : 2 * groups]
    ov_refs = in_refs[2 * groups :]
    step = pl.program_id(0)
    blocks, slots = groups * code_refs[0].shape[0], block_of.shape[0]
    own, width = 2 * amp_refs[0].shape[0], amps.shape[2]

    @pl.when(step == 0)
    def _():
        for k, ref in enumerate(amp_refs):
            for h in range(2):
                amps[pl.ds(k * own + h * (own // 2), own // 2)] = ref[
                    :, :, h * width : (h + 1) * width
                ]
        amps[blocks] = jnp.zeros(amps.shape[1:], bf16)
        acc[...] = jnp.zeros_like(acc)
        first = place_ref[0] * slots

        @pl.loop(0, slots, unroll=16)
        def _(s):
            block_of[s] = blocks

        for k, ref in enumerate(code_refs):

            @pl.loop(0, ref.shape[0], unroll=8)
            def _(n):
                slot = ref[n] - first

                @pl.when((slot >= 0) & (slot < slots))
                def _():
                    block_of[slot] = k * ref.shape[0] + n

    here, _, chol = ov_refs[0].shape
    start, count = step * len(ov_refs) * here, len(ov_refs) * here
    left = jnp.concatenate([amps[block_of[start + s]] for s in range(count)], axis=1)
    right = jnp.concatenate([ref[...].reshape(here * width, chol) for ref in ov_refs], axis=0)
    acc[...] += jnp.dot(left, right, preferred_element_type=f32)

    @pl.when(step == pl.num_programs(0) - 1)
    def _():
        share = chol // shares
        for k in range(out_ref.shape[0]):
            start = k % shares * share
            out_ref[k] = acc[:, start : start + share]


def cycle_operands(cycle_amp, owner_of, slot_of, slots):
    codes = round_robin(owner_of * slots + slot_of, "ph")
    near, far = jnp.split(cycle_amp, 2, 0)
    return round_robin(jnp.concatenate([near, far], 2), "ph"), codes


def cycle_partial(amps, codes, ov_slots):
    slots, chol, width = ov_slots.shape
    occ = amps[0].shape[1]
    shares = lax.axis_size(("ph", "vec"))
    copies = shares * lax.axis_size("vir")
    place = lax.axis_index("ph").astype(jnp.int32)[None]
    here, sides = 8, 4

    def side(q):
        return pl.BlockSpec((here, width, chol), lambda i: (i * sides + q, 0, 0))

    whole = pl.BlockSpec(memory_space=pltpu.VMEM)
    scalars = pl.BlockSpec(memory_space=pltpu.SMEM)
    return pl.pallas_call(
        functools.partial(cycle_kernel, shares, len(amps)),
        grid=(slots // (here * sides),),
        in_specs=[scalars] * (1 + len(codes))
        + [whole] * len(amps)
        + [side(q) for q in range(sides)],
        out_specs=pl.BlockSpec((copies, occ, chol // shares), lambda i: (0, 0, 0)),
        out_shape=jax.ShapeDtypeStruct((copies, occ, chol // shares), f32),
        scratch_shapes=[
            pltpu.VMEM((len(codes) * codes[0].shape[0] + 1, occ, width), bf16),
            pltpu.VMEM((occ, chol), f32),
            pltpu.SMEM((slots,), jnp.int32),
        ],
        compiler_params=pltpu.CompilerParams(vmem_limit_bytes=60 << 20),
        cost_estimate=pl.CostEstimate(
            flops=2 * occ * slots * width * chol,
            bytes_accessed=2 * slots * width * chol,
            transcendentals=0,
        ),
    )(place, *codes, *amps, *[jnp.swapaxes(ov_slots, 1, 2)] * sides)


def swap_matrix(deep):
    n = deep * deep
    r = lax.broadcasted_iota(jnp.int32, (n, n), 0)
    s = lax.broadcasted_iota(jnp.int32, (n, n), 1)
    return (lax.rem(r, deep) * deep + lax.div(r, deep) == s).astype(bf16)


def ladder_kernel(sides, row_ref, amp_hbm, factor_hbm, out_ref, *scratch):
    (amp_buf, factor_buf, amp_sem, factor_sem, swap, turned, half, flat) = scratch
    _, virtuals, deep, pairs = amp_buf.shape
    count, chol, _ = row_ref.shape
    square = deep * deep
    step, steps = pl.program_id(0), pl.num_programs(0)
    slot = lax.rem(step, 2)

    def arriving(hbm, buf, sem, step, side):
        size = buf.shape[1] // sides
        rows, slot = pl.ds(side * size, size), lax.rem(step, 2)
        block = pl.ds(pl.multiple_of(step * deep, deep), deep)
        return pltpu.make_async_copy(
            hbm.at[rows, block], buf.at[slot, rows], sem.at[slot, side]
        )

    def start(hbm, buf, sem, step):
        for q in range(sides):
            arriving(hbm, buf, sem, step, q).start()

    @pl.when(step == 0)
    def _():
        start(amp_hbm, amp_buf, amp_sem, step)
        out_ref[...] = jnp.zeros_like(out_ref)
        swap[...] = swap_matrix(deep)

    @pl.when((step > 0) & (step + 1 < steps))
    def _():
        start(amp_hbm, amp_buf, amp_sem, step + 1)
        start(factor_hbm, factor_buf, factor_sem, step + 1)

    def later(jobs):
        store = None
        for job in jobs:
            after = job()
            if store is not None:
                store()
            store = after
        store()

    def reorder(first):
        rows = [slice(first + r * deep, first + (r + 1) * deep) for r in range(2)]
        block = [amp_buf[slot, r].reshape(square, pairs) for r in rows]
        block = jnp.dot(
            swap[...], jnp.concatenate(block, axis=1), preferred_element_type=f32
        ).astype(bf16)

        def store():
            for i, r in enumerate(rows):
                turned[:, r, :] = block[:, i * pairs : (i + 1) * pairs].reshape(deep, deep, pairs)

        return store

    for q in range(sides):
        arriving(amp_hbm, amp_buf, amp_sem, step, q).wait()
        size = virtuals // sides
        later(
            functools.partial(reorder, k) for k in range(q * size, (q + 1) * size, 2 * deep)
        )

    @pl.when(step == 0)
    def _():
        start(factor_hbm, factor_buf, factor_sem, step)

    @pl.when((step == 0) & (steps > 1))
    def _():
        start(amp_hbm, amp_buf, amp_sem, step + 1)

    row = jnp.concatenate([row_ref[k] for k in range(count)], axis=1)

    def halves(d):
        block = jnp.concatenate([turned[d], turned[d + 1]], axis=1)
        block = jnp.dot(row, block, preferred_element_type=f32).astype(bf16)

        def store():
            half[d], half[d + 1] = block[:, :pairs], block[:, pairs:]

        return store

    later(functools.partial(halves, d) for d in range(0, deep, 2))

    @pl.when((step == 0) & (steps > 1))
    def _():
        start(factor_hbm, factor_buf, factor_sem, step + 1)

    def flatten(first):
        parts = range(first, first + 4 * deep, deep)
        block = [half[:, k : k + deep, :].reshape(square, pairs).T for k in parts]
        block = jnp.dot(
            jnp.concatenate(block, axis=0), swap[...], preferred_element_type=f32
        ).astype(bf16)

        def store():
            for i, k in enumerate(parts):
                flat[:, k * deep : (k + deep) * deep] = block[i * pairs : (i + 1) * pairs]

        return store

    later(functools.partial(flatten, k) for k in range(0, chol, 4 * deep))
    for q in range(sides):
        arriving(factor_hbm, factor_buf, factor_sem, step, q).wait()
    columns = 512

    def ladder(first):
        block = factor_buf[slot, :, :, first : first + columns].reshape(chol * deep, columns)
        block = jnp.dot(flat[...], block, preferred_element_type=f32)

        def store():
            out_ref[:, first : first + columns] += block

        return store

    later(functools.partial(ladder, n) for n in range(0, out_ref.shape[1], columns))


def ladder_partial(row, ladder_amp, vv_factor):
    virtuals, slab, pairs = ladder_amp.shape
    chol = vv_factor.shape[0]
    deep, sides = 16, 4
    whole = pl.BlockSpec(memory_space=pl.ANY)
    return pl.pallas_call(
        functools.partial(ladder_kernel, sides),
        grid=(slab // deep,),
        in_specs=[pl.BlockSpec(memory_space=pltpu.VMEM), whole, whole],
        out_specs=pl.BlockSpec((pairs, virtuals), lambda i: (0, 0)),
        out_shape=jax.ShapeDtypeStruct((pairs, virtuals), f32),
        scratch_shapes=[
            pltpu.VMEM((2, virtuals, deep, pairs), bf16),
            pltpu.VMEM((2, chol, deep, virtuals), bf16),
            pltpu.SemaphoreType.DMA((2, sides)),
            pltpu.SemaphoreType.DMA((2, sides)),
            pltpu.VMEM((deep * deep, deep * deep), bf16),
            pltpu.VMEM((deep, virtuals, pairs), bf16),
            pltpu.VMEM((deep, chol, pairs), bf16),
            pltpu.VMEM((pairs, chol * deep), bf16),
        ],
        compiler_params=pltpu.CompilerParams(vmem_limit_bytes=60 << 20),
        cost_estimate=pl.CostEstimate(
            flops=4 * chol * virtuals * slab * pairs,
            bytes_accessed=2 * virtuals * slab * (pairs + chol),
            transcendentals=0,
        ),
    )(row, ladder_amp, vv_factor)


def scatter_sum(x, axes, near=None):
    total_places = lax.axis_size(axes)
    me = lax.axis_index(axes)
    n = x.shape[0]

    def moved(place, k):
        if near is None:
            return (place + k) % n
        if near > 0:
            return place // near * near + (place % near + k) % near
        return (place + k * -near) % total_places

    def rank(place):
        return place if near is None else place % near if near > 0 else place // -near

    total = lax.dynamic_index_in_dim(x, rank(me), 0, keepdims=False)
    sent = x.astype(bf16)
    for k in range(1, n):
        piece = lax.dynamic_index_in_dim(sent, rank(moved(me, k)), 0, keepdims=False)
        pairs = [(i, moved(i, k)) for i in range(total_places)]
        total = total + lax.ppermute(piece, axes, pairs).astype(f32)
    return total


def local(
    vv_factor, ladder_amp, cycle_amp, ov_slots, owner_of, slot_of, ov_pairs, eps_vir, eps_occ
):
    chol, slab, virtuals = vv_factor.shape
    pairs = ladder_amp.shape[2]
    slots, _, width = ov_slots.shape
    n_vir, n_ph, n_vec = (lax.axis_size(a) for a in ("vir", "ph", "vec"))
    fits = slab == LANES and virtuals % 512 == 0 and pairs == 2 * LANES and chol % LANES == 0 and slots % 32 == 0
    if not fits or 256 % width or cycle_amp.shape[0] % 2 or n_vir * n_ph % 4:
        return plain(
            vv_factor, ladder_amp, cycle_amp, ov_slots, owner_of, slot_of, ov_pairs, eps_vir, eps_occ
        )
    amps, codes = cycle_operands(cycle_amp, owner_of, slot_of, slots)
    row, amps, codes = lax.optimization_barrier((own_row(vv_factor, n_vir), amps, codes))
    row = lax.all_to_all(row, "vir", 0, 0)
    pieces = lax.all_to_all(cycle_partial(amps, codes, ov_slots), ("vir", "ph", "vec"), 0, 0)
    coupling = jnp.sum(pieces, 0).astype(bf16)
    second_count = ov_pairs.shape[1]
    cycle_term = jnp.einsum("ip,pjb->ijb", coupling, ov_pairs, preferred_element_type=f32)
    cycle_term = cycle_term.reshape(pairs, slab)

    ladder = ladder_partial(row, ladder_amp, vv_factor)
    vir = lax.axis_index("vir")
    share = pairs // (n_ph * n_vec)
    own = jnp.arange(n_vir, dtype=jnp.int32)[None, :, None] == vir
    total = ladder.reshape(pairs, n_vir, slab) + jnp.where(own, cycle_term[:, None, :], 0.0)
    total = total.reshape(n_ph, n_vec, share, virtuals)
    total = scatter_sum(jnp.swapaxes(total, 0, 1), "vec")
    total = total.reshape(n_ph, share, n_vir, slab).transpose(2, 0, 1, 3)
    total = total.reshape(n_vir * n_ph // 4, 4, share, slab).transpose(1, 0, 2, 3)
    total = scatter_sum(scatter_sum(total, ("vir", "ph"), 4), ("vir", "ph"), -4)

    residual = total.T.astype(bf16)
    place = lax.axis_index(("ph", "vec"))
    pair_index = place * share + jnp.arange(share, dtype=jnp.int32)
    occ_ids = jnp.arange(eps_occ.shape[0], dtype=jnp.int32)[None, :]
    first_occ = jnp.sum(
        jnp.where((pair_index // second_count)[:, None] == occ_ids, eps_occ[None, :], 0.0), 1
    )
    second_occ = jnp.sum(
        jnp.where((pair_index % second_count)[:, None] == occ_ids, eps_occ[None, :], 0.0), 1
    )
    slab_energy = lax.dynamic_slice_in_dim(eps_vir, vir * slab, slab, 0)
    denominator = (eps_vir[0] + slab_energy)[:, None] - first_occ[None, :] - second_occ[None, :]
    update = residual.astype(f32) / denominator
    return residual, update


def solution(mesh):
    placed = (
        P(("ph", "vec"), "vir", None),
        P(None, "vir", None),
        P(("vir", "ph"), None, "vec"),
        P(("vir", "ph"), None, "vec"),
        P(("vir", "ph")),
        P(("vir", "ph")),
        P(("ph", "vec"), None, "vir"),
        P(),
        P(),
    )
    return jax.shard_map(
        local,
        mesh=mesh,
        in_specs=placed,
        out_specs=(P("vir", ("ph", "vec")), P("vir", ("ph", "vec"))),
        check_vma=False,
    )
```

```python
import functools

import jax
import jax.numpy as jnp
from jax import lax
from jax.experimental import pallas as pl
from jax.experimental.pallas import tpu as pltpu
from jax.sharding import PartitionSpec as P

LANES = 128
bf16, f32 = jnp.bfloat16, jnp.float32


def plain(
    vv_factor, ladder_amp, cycle_amp, ov_slots, owner_of, slot_of, ov_pairs, eps_vir, eps_occ
):
    chol_local, slab_width, virtuals = vv_factor.shape
    pair_count = ladder_amp.shape[2]
    row_piece = vv_factor[:, :, 0]
    factor_row = lax.all_gather(row_piece, "vir", axis=1, tiled=True)
    half = jnp.dot(
        factor_row,
        ladder_amp.reshape(virtuals, slab_width * pair_count),
        preferred_element_type=jnp.float32,
    )
    half = half.astype(jnp.bfloat16).reshape(chol_local * slab_width, pair_count)
    flat_factor = vv_factor.reshape(chol_local * slab_width, virtuals)
    block_local, occ_rows, block_part = cycle_amp.shape
    owner_total = lax.axis_size("ph")
    targets = owner_of[None, :] == jnp.arange(owner_total, dtype=jnp.int32)[:, None]
    outgoing = jnp.where(targets[:, :, None, None], cycle_amp[None], jnp.zeros((), jnp.bfloat16))
    places = jnp.where(targets, slot_of[None, :], 0)
    arrived, arrived_slots = (
        lax.all_to_all(outgoing, "ph", split_axis=0, concat_axis=0, tiled=True),
        lax.all_to_all(places, "ph", split_axis=0, concat_axis=0, tiled=True),
    )
    capacity = ov_slots.shape[0]
    picks = (
        arrived_slots.reshape(-1)[:, None] == jnp.arange(capacity, dtype=jnp.int32)[None, :]
    ).astype(jnp.bfloat16)
    arranged = jnp.einsum(
        "ns,niw->siw",
        picks,
        arrived.reshape(-1, occ_rows, block_part),
        preferred_element_type=jnp.float32,
    )
    arranged = arranged.astype(jnp.bfloat16)
    cycle_part = jnp.einsum("siw,spw->ip", arranged, ov_slots, preferred_element_type=jnp.float32)
    near_groups = lax.axis_size("ph") * lax.axis_size("vec")
    summed = lax.psum(cycle_part, ("vir", "ph", "vec"))
    vector_share = summed.shape[1] // near_groups
    own_share = lax.dynamic_slice_in_dim(
        summed, lax.axis_index(("ph", "vec")) * vector_share, vector_share, 1
    )
    coupling = own_share.astype(jnp.bfloat16)
    second_count = ov_pairs.shape[1]
    cycle_term = jnp.einsum("ip,pjb->bij", coupling, ov_pairs, preferred_element_type=jnp.float32)
    cycle_term = cycle_term.reshape(slab_width, occ_rows * second_count)
    slab_start = lax.axis_index("vir") * slab_width
    slab = (
        lax.psum_scatter(
            lax.dot_general(
                flat_factor, half, (((0,), (0,)), ((), ())), preferred_element_type=jnp.float32
            ),
            "vir",
            scatter_dimension=0,
            tiled=True,
        )
        + cycle_term
    )
    result = lax.psum_scatter(slab, ("ph", "vec"), scatter_dimension=1, tiled=True)
    residual = result.astype(jnp.bfloat16)
    share_width = result.shape[1]
    pair_index = lax.axis_index(("ph", "vec")) * share_width + jnp.arange(
        share_width, dtype=jnp.int32
    )
    occ_count = eps_occ.shape[0]
    occ_ids = jnp.arange(occ_count, dtype=jnp.int32)[None, :]
    first_occ = jnp.sum(
        jnp.where((pair_index // second_count)[:, None] == occ_ids, eps_occ[None, :], 0.0), 1
    )
    second_occ = jnp.sum(
        jnp.where((pair_index % second_count)[:, None] == occ_ids, eps_occ[None, :], 0.0), 1
    )
    slab_energy = lax.dynamic_slice_in_dim(eps_vir, slab_start, slab_width, 0)
    denominator = (eps_vir[0] + slab_energy)[:, None] - first_occ[None, :] - second_occ[None, :]
    update = residual.astype(jnp.float32) / denominator
    return (residual, update)


def shifted(x, axes, k):
    n = lax.axis_size(axes)
    return lax.ppermute(x, axes, [(i, (i + k) % n) for i in range(n)])


def round_robin(x, axes):
    return [x] + [shifted(x, axes, k) for k in range(1, lax.axis_size(axes))]


def row_kernel(*refs):
    (*x_refs, out_ref, acc) = refs
    step, rows = pl.program_id(1), x_refs[0].shape[0]
    lane = lax.broadcasted_iota(jnp.int32, acc.shape, 1)

    @pl.when(step == 0)
    def _():
        acc[...] = jnp.zeros_like(acc)

    part = jnp.zeros(acc.shape, f32)
    for q, ref in enumerate(x_refs):
        for p in range(rows):
            shift = q * rows + p
            column = ref[p].astype(f32)
            part = jnp.where(lane == shift, pltpu.roll(column, shift, 1) if shift else column, part)
    rows = rows * len(x_refs)
    part = pltpu.roll(part, step * rows, 1)
    acc[...] = jnp.where(lane // rows == step, part, acc[...])

    @pl.when(step == pl.num_programs(1) - 1)
    def _():
        piece = acc[...].T.astype(bf16)
        for k in range(out_ref.shape[0]):
            out_ref[k] = piece


def own_row(vv_factor, copies):
    chol, slab, _ = vv_factor.shape
    rows, sides = 16, 4
    steps = LANES // (rows * sides)

    def side(q):
        return pl.BlockSpec((rows, slab, LANES), lambda g, k: ((g * steps + k) * sides + q, 0, 0))

    return pl.pallas_call(
        row_kernel,
        grid=(chol // LANES, steps),
        in_specs=[side(q) for q in range(sides)],
        out_specs=pl.BlockSpec((copies, LANES, slab), lambda g, k: (0, g, 0)),
        out_shape=jax.ShapeDtypeStruct((copies, chol, slab), bf16),
        scratch_shapes=[pltpu.VMEM((slab, LANES), f32)],
        compiler_params=pltpu.CompilerParams(vmem_limit_bytes=32 << 20),
        cost_estimate=pl.CostEstimate(
            flops=2 * chol * slab * LANES, bytes_accessed=2 * chol * slab * LANES, transcendentals=0
        ),
    )(*[vv_factor] * sides)


def cycle_kernel(shares, groups, place_ref, *refs):
    (*in_refs, out_ref, amps, acc, block_of) = refs
    code_refs, amp_refs = in_refs[:groups], in_refs[groups : 2 * groups]
    ov_refs = in_refs[2 * groups :]
    step = pl.program_id(0)
    blocks, slots = groups * code_refs[0].shape[0], block_of.shape[0]
    own, width = 2 * amp_refs[0].shape[0], amps.shape[2]

    @pl.when(step == 0)
    def _():
        for k, ref in enumerate(amp_refs):
            for h in range(2):
                amps[pl.ds(k * own + h * (own // 2), own // 2)] = ref[
                    :, :, h * width : (h + 1) * width
                ]
        amps[blocks] = jnp.zeros(amps.shape[1:], bf16)
        acc[...] = jnp.zeros_like(acc)
        first = place_ref[0] * slots

        @pl.loop(0, slots, unroll=16)
        def _(s):
            block_of[s] = blocks

        for k, ref in enumerate(code_refs):

            @pl.loop(0, ref.shape[0], unroll=8)
            def _(n):
                slot = ref[n] - first

                @pl.when((slot >= 0) & (slot < slots))
                def _():
                    block_of[slot] = k * ref.shape[0] + n

    here, _, chol = ov_refs[0].shape
    start, count = step * len(ov_refs) * here, len(ov_refs) * here
    left = jnp.concatenate([amps[block_of[start + s]] for s in range(count)], axis=1)
    right = jnp.concatenate([ref[...].reshape(here * width, chol) for ref in ov_refs], axis=0)
    acc[...] += jnp.dot(left, right, preferred_element_type=f32)

    @pl.when(step == pl.num_programs(0) - 1)
    def _():
        share = chol // shares
        for k in range(out_ref.shape[0]):
            start = k % shares * share
            out_ref[k] = acc[:, start : start + share]


def cycle_operands(cycle_amp, owner_of, slot_of, slots):
    codes = round_robin(owner_of * slots + slot_of, "ph")
    near, far = jnp.split(cycle_amp, 2, 0)
    return round_robin(jnp.concatenate([near, far], 2), "ph"), codes


def cycle_partial(amps, codes, ov_slots):
    slots, chol, width = ov_slots.shape
    occ = amps[0].shape[1]
    shares = lax.axis_size(("ph", "vec"))
    copies = shares * lax.axis_size("vir")
    place = lax.axis_index("ph").astype(jnp.int32)[None]
    here, sides = 8, 4

    def side(q):
        return pl.BlockSpec((here, width, chol), lambda i: (i * sides + q, 0, 0))

    whole = pl.BlockSpec(memory_space=pltpu.VMEM)
    scalars = pl.BlockSpec(memory_space=pltpu.SMEM)
    return pl.pallas_call(
        functools.partial(cycle_kernel, shares, len(amps)),
        grid=(slots // (here * sides),),
        in_specs=[scalars] * (1 + len(codes))
        + [whole] * len(amps)
        + [side(q) for q in range(sides)],
        out_specs=pl.BlockSpec((copies, occ, chol // shares), lambda i: (0, 0, 0)),
        out_shape=jax.ShapeDtypeStruct((copies, occ, chol // shares), f32),
        scratch_shapes=[
            pltpu.VMEM((len(codes) * codes[0].shape[0] + 1, occ, width), bf16),
            pltpu.VMEM((occ, chol), f32),
            pltpu.SMEM((slots,), jnp.int32),
        ],
        compiler_params=pltpu.CompilerParams(vmem_limit_bytes=60 << 20),
        cost_estimate=pl.CostEstimate(
            flops=2 * occ * slots * width * chol,
            bytes_accessed=2 * slots * width * chol,
            transcendentals=0,
        ),
    )(place, *codes, *amps, *[jnp.swapaxes(ov_slots, 1, 2)] * sides)


def swap_matrix(deep):
    n = deep * deep
    r = lax.broadcasted_iota(jnp.int32, (n, n), 0)
    s = lax.broadcasted_iota(jnp.int32, (n, n), 1)
    return (lax.rem(r, deep) * deep + lax.div(r, deep) == s).astype(bf16)


def ladder_kernel(sides, row_ref, amp_hbm, factor_hbm, out_ref, *scratch):
    (amp_buf, factor_buf, amp_sem, factor_sem, swap, turned, half, flat) = scratch
    _, virtuals, deep, pairs = amp_buf.shape
    count, chol, _ = row_ref.shape
    square = deep * deep
    step, steps = pl.program_id(0), pl.num_programs(0)
    slot = lax.rem(step, 2)

    def arriving(hbm, buf, sem, step, side):
        size = buf.shape[1] // sides
        rows, slot = pl.ds(side * size, size), lax.rem(step, 2)
        block = pl.ds(pl.multiple_of(step * deep, deep), deep)
        return pltpu.make_async_copy(
            hbm.at[rows, block], buf.at[slot, rows], sem.at[slot, side]
        )

    def start(step):
        for q in range(sides):
            arriving(amp_hbm, amp_buf, amp_sem, step, q).start()
        for q in range(sides):
            arriving(factor_hbm, factor_buf, factor_sem, step, q).start()

    @pl.when(step == 0)
    def _():
        start(step)
        out_ref[...] = jnp.zeros_like(out_ref)
        swap[...] = swap_matrix(deep)

    @pl.when(step + 1 < steps)
    def _():
        start(step + 1)

    def later(jobs):
        store = None
        for job in jobs:
            after = job()
            if store is not None:
                store()
            store = after
        store()

    def reorder(first):
        rows = [slice(first + r * deep, first + (r + 1) * deep) for r in range(2)]
        block = [amp_buf[slot, r].reshape(square, pairs) for r in rows]
        block = jnp.dot(
            swap[...], jnp.concatenate(block, axis=1), preferred_element_type=f32
        ).astype(bf16)

        def store():
            for i, r in enumerate(rows):
                turned[:, r, :] = block[:, i * pairs : (i + 1) * pairs].reshape(deep, deep, pairs)

        return store

    for q in range(sides):
        arriving(amp_hbm, amp_buf, amp_sem, step, q).wait()
    later(functools.partial(reorder, k) for k in range(0, virtuals, 2 * deep))

    row = jnp.concatenate([row_ref[k] for k in range(count)], axis=1)

    def halves(d):
        block = jnp.concatenate([turned[d], turned[d + 1]], axis=1)
        block = jnp.dot(row, block, preferred_element_type=f32).astype(bf16)

        def store():
            half[d], half[d + 1] = block[:, :pairs], block[:, pairs:]

        return store

    later(functools.partial(halves, d) for d in range(0, deep, 2))

    def flatten(first):
        parts = range(first, first + 4 * deep, deep)
        block = [half[:, k : k + deep, :].reshape(square, pairs).T for k in parts]
        block = jnp.dot(
            jnp.concatenate(block, axis=0), swap[...], preferred_element_type=f32
        ).astype(bf16)

        def store():
            for i, k in enumerate(parts):
                flat[:, k * deep : (k + deep) * deep] = block[i * pairs : (i + 1) * pairs]

        return store

    for q in range(sides):
        arriving(factor_hbm, factor_buf, factor_sem, step, q).wait()
    later(functools.partial(flatten, k) for k in range(0, chol, 4 * deep))
    columns = 512

    def ladder(first):
        block = factor_buf[slot, :, :, first : first + columns].reshape(chol * deep, columns)
        block = jnp.dot(flat[...], block, preferred_element_type=f32)

        def store():
            out_ref[:, first : first + columns] += block

        return store

    later(functools.partial(ladder, n) for n in range(0, out_ref.shape[1], columns))


def ladder_partial(row, ladder_amp, vv_factor):
    virtuals, slab, pairs = ladder_amp.shape
    chol = vv_factor.shape[0]
    deep, sides = 16, 4
    whole = pl.BlockSpec(memory_space=pl.ANY)
    return pl.pallas_call(
        functools.partial(ladder_kernel, sides),
        grid=(slab // deep,),
        in_specs=[pl.BlockSpec(memory_space=pltpu.VMEM), whole, whole],
        out_specs=pl.BlockSpec((pairs, virtuals), lambda i: (0, 0)),
        out_shape=jax.ShapeDtypeStruct((pairs, virtuals), f32),
        scratch_shapes=[
            pltpu.VMEM((2, virtuals, deep, pairs), bf16),
            pltpu.VMEM((2, chol, deep, virtuals), bf16),
            pltpu.SemaphoreType.DMA((2, sides)),
            pltpu.SemaphoreType.DMA((2, sides)),
            pltpu.VMEM((deep * deep, deep * deep), bf16),
            pltpu.VMEM((deep, virtuals, pairs), bf16),
            pltpu.VMEM((deep, chol, pairs), bf16),
            pltpu.VMEM((pairs, chol * deep), bf16),
        ],
        compiler_params=pltpu.CompilerParams(vmem_limit_bytes=60 << 20),
        cost_estimate=pl.CostEstimate(
            flops=4 * chol * virtuals * slab * pairs,
            bytes_accessed=2 * virtuals * slab * (pairs + chol),
            transcendentals=0,
        ),
    )(row, ladder_amp, vv_factor)


def scatter_sum(x, axes, near=None):
    total_places = lax.axis_size(axes)
    me = lax.axis_index(axes)
    n = x.shape[0]

    def moved(place, k):
        if near is None:
            return (place + k) % n
        if near > 0:
            return place // near * near + (place % near + k) % near
        return (place + k * -near) % total_places

    def rank(place):
        return place if near is None else place % near if near > 0 else place // -near

    total = lax.dynamic_index_in_dim(x, rank(me), 0, keepdims=False)
    sent = x.astype(bf16)
    for k in range(1, n):
        piece = lax.dynamic_index_in_dim(sent, rank(moved(me, k)), 0, keepdims=False)
        pairs = [(i, moved(i, k)) for i in range(total_places)]
        total = total + lax.ppermute(piece, axes, pairs).astype(f32)
    return total


def local(
    vv_factor, ladder_amp, cycle_amp, ov_slots, owner_of, slot_of, ov_pairs, eps_vir, eps_occ
):
    chol, slab, virtuals = vv_factor.shape
    pairs = ladder_amp.shape[2]
    slots, _, width = ov_slots.shape
    n_vir, n_ph, n_vec = (lax.axis_size(a) for a in ("vir", "ph", "vec"))
    fits = slab == LANES and virtuals % 512 == 0 and pairs == 2 * LANES and chol % LANES == 0 and slots % 32 == 0
    if not fits or 256 % width or cycle_amp.shape[0] % 2 or n_vir * n_ph % 4:
        return plain(
            vv_factor, ladder_amp, cycle_amp, ov_slots, owner_of, slot_of, ov_pairs, eps_vir, eps_occ
        )
    amps, codes = cycle_operands(cycle_amp, owner_of, slot_of, slots)
    row, amps, codes = lax.optimization_barrier((own_row(vv_factor, n_vir), amps, codes))
    row = lax.all_to_all(row, "vir", 0, 0)
    pieces = lax.all_to_all(cycle_partial(amps, codes, ov_slots), ("vir", "ph", "vec"), 0, 0)
    coupling = jnp.sum(pieces, 0).astype(bf16)
    second_count = ov_pairs.shape[1]
    cycle_term = jnp.einsum("ip,pjb->ijb", coupling, ov_pairs, preferred_element_type=f32)
    cycle_term = cycle_term.reshape(pairs, slab)

    ladder = ladder_partial(row, ladder_amp, vv_factor)
    vir = lax.axis_index("vir")
    share = pairs // (n_ph * n_vec)
    own = jnp.arange(n_vir, dtype=jnp.int32)[None, :, None] == vir
    total = ladder.reshape(pairs, n_vir, slab) + jnp.where(own, cycle_term[:, None, :], 0.0)
    total = total.reshape(n_ph, n_vec, share, virtuals)
    total = scatter_sum(jnp.swapaxes(total, 0, 1), "vec")
    total = total.reshape(n_ph, share, n_vir, slab).transpose(2, 0, 1, 3)
    total = total.reshape(n_vir * n_ph // 4, 4, share, slab).transpose(1, 0, 2, 3)
    total = scatter_sum(scatter_sum(total, ("vir", "ph"), 4), ("vir", "ph"), -4)

    residual = total.T.astype(bf16)
    place = lax.axis_index(("ph", "vec"))
    pair_index = place * share + jnp.arange(share, dtype=jnp.int32)
    occ_ids = jnp.arange(eps_occ.shape[0], dtype=jnp.int32)[None, :]
    first_occ = jnp.sum(
        jnp.where((pair_index // second_count)[:, None] == occ_ids, eps_occ[None, :], 0.0), 1
    )
    second_occ = jnp.sum(
        jnp.where((pair_index % second_count)[:, None] == occ_ids, eps_occ[None, :], 0.0), 1
    )
    slab_energy = lax.dynamic_slice_in_dim(eps_vir, vir * slab, slab, 0)
    denominator = (eps_vir[0] + slab_energy)[:, None] - first_occ[None, :] - second_occ[None, :]
    update = residual.astype(f32) / denominator
    return residual, update


def solution(mesh):
    placed = (
        P(("ph", "vec"), "vir", None),
        P(None, "vir", None),
        P(("vir", "ph"), None, "vec"),
        P(("vir", "ph"), None, "vec"),
        P(("vir", "ph")),
        P(("vir", "ph")),
        P(("ph", "vec"), None, "vir"),
        P(),
        P(),
    )
    return jax.shard_map(
        local,
        mesh=mesh,
        in_specs=placed,
        out_specs=(P("vir", ("ph", "vec")), P("vir", ("ph", "vec"))),
        check_vma=False,
    )
```
